32 devices in a mesh: dp: 8 (over z, y), row: 2 (over core), col: 2 (over x).
Axes of the slice: x: 2, y: 2, z: 4, core: 2. Of those that a mesh axis runs over, the one named last changes fastest.
Arguments:
- tokens_in: bfloat16 [2, 12608, 512], P(None, ('dp', 'col'), 'row'), may hold values from -6 to 6
- out_cotangent: bfloat16 [2, 12608, 512], P(None, ('dp', 'col'), 'row'), may hold values from -6 to 6
- expert_ids: int32 [2, 12608, 2], P(None, 'dp'), may hold values from 0 to 31, all different within a row; in each aligned block of 1576 rows (0 to 1575, 1576 to 3151, ..., all dimensions but the last counted through in order) at most 132 rows name the same one
- gate_values: float32 [2, 12608, 2], P(None, 'dp'), may hold values from 0.25 to 0.75
- first_gain: float32 [512], P('row'), may hold values from 0.5 to 1.5
- first_shift: float32 [512], P('row'), may hold values from -1.75 to 1.75
- second_gain: float32 [512], P('row'), may hold values from 0.5 to 1.5
- second_shift: float32 [512], P('row'), may hold values from -1.75 to 1.75
- qkv_weight: bfloat16 [512, 3, 512], P(('row', 'dp'), None, 'col'), may hold values from -0.25 to 0.25
- qkv_bias: float32 [2, 512], P(None, ('col', 'dp')), may hold values from -1.75 to 1.75
- proj_weight: bfloat16 [512, 512], P(('col', 'dp'), 'row'), may hold values from -0.5 to 0.5
- proj_bias: float32 [512], P(('row', 'dp')), may hold values from -1.75 to 1.75
- expand_weight: bfloat16 [32, 512, 2048], P('dp', 'row', 'col'), may hold values from -0.25 to 0.25
- expand_bias: float32 [32, 2048], P('row', ('col', 'dp')), may hold values from -1.75 to 1.75
- contract_weight: bfloat16 [32, 2048, 512], P('dp', 'col', 'row'), may hold values from -0.25 to 0.25
- contract_bias: float32 [32, 512], P(None, ('row', 'dp')), may hold values from -1.75 to 1.75
Outputs:
- layer_out: bfloat16 [2, 12608, 512], P(None, ('dp', 'col'), 'row')
- input_grad: float32 [2, 12608, 512], P(None, ('dp', 'col'), 'row')
- first_gain_grad: float32 [512], P('row')
- first_shift_grad: float32 [512], P('row')
- second_gain_grad: float32 [512], P('row')
- second_shift_grad: float32 [512], P('row')
- qkv_weight_grad: float32 [512, 3, 512], P(('row', 'dp'), None, 'col')
- qkv_bias_grad: float32 [2, 512], P(None, ('col', 'dp'))
- proj_weight_grad: float32 [512, 512], P(('col', 'dp'), 'row')
- proj_bias_grad: float32 [512], P(('row', 'dp'))
- expand_weight_grad: float32 [32, 512, 2048], P('dp', 'row', 'col')
- expand_bias_grad: float32 [32, 2048], P('row', ('col', 'dp'))
- contract_weight_grad: float32 [32, 2048, 512], P('dp', 'col', 'row')
- contract_bias_grad: float32 [32, 512], P(None, ('row', 'dp'))
The draws below stay inside these ranges and needn't reach their ends.
Inputs may be any that keep to these rules, and one draw needn't show every extreme that they name: `expert_ids`: in each micro-batch, among the 1576 rows of one index of dp (aligned blocks of 1576 rows), no expert is named by more than 132 rows, a bound that some block reaches; a row names 2 different experts.
All inputs are finite; a program needn't handle non-finite values.
Results may differ from the reference program's by a relative error of at most 0.028.
Values may be sent and summed in bfloat16 or wider, within the bound.
No kernel may reach another device: no remote copies, remote signals or barrier semaphores. Data moves between devices by JAX's collectives and lax.ppermute only.
A program may use at most 320 MiB of HBM per device.

```python
import math
import jax
import jax.numpy as jnp
import numpy as np
from jax import lax

D = 512
HEADS = 8
HIDDEN_SIZE = 2048
EXPERTS = 32
TOP = 2
SEQ = 197
MICRO = 2
GROUP = 1576
CAP = 132
N_DP = 8


def block_levels(own_key, extent, pieces, low, largest):
    def one(position, blocks):
        steps = jax.random.uniform(jax.random.fold_in(jax.random.fold_in(own_key, 6), position), (blocks,), jnp.float32, low / len(pieces), largest / len(pieces))
        return jnp.repeat(jnp.exp(steps), extent[position] // blocks).reshape((-1,) + (1,) * (len(extent) - position - 1))

    loudness = one(*pieces[0])
    for cut in pieces[1:]:
        loudness = loudness * one(*cut)
    return loudness


def deal_out(rng, own, number, rows, count, top, most, slope):
    order = jax.random.permutation(rng, count)
    crowded, ordinary = load_shares(count, rows * top, most, slope, True), load_shares(count, rows * top, most, slope, False)
    places = jnp.arange(count)

    def named(sizes, turn):
        used = int((sizes > 0).sum())
        fixed = max(1, used // 4)
        passed = fixed + (places - fixed + turn * (used - fixed)) % max(1, count - fixed)
        return jnp.zeros((count,), jnp.int32).at[order[jnp.where(places < fixed, places, passed)]].set(jnp.asarray(sizes, jnp.int32))

    sizes = jnp.where(number % 4 == 0, named(crowded, number // 4), named(ordinary, number - number // 4 - 1))
    mixed = jax.random.permutation(jax.random.fold_in(own, 3), count)
    donor, sink = mixed[0:count // 2 * 2:2], mixed[1:count // 2 * 2:2]
    slack = jnp.minimum(sizes[donor] - 1, most - sizes[sink]) // 2
    slack = jnp.where((donor == order[0]) | (sink == order[0]) | (sizes[sink] == 0), 0, jnp.maximum(slack, 0))
    passed = jax.random.randint(jax.random.fold_in(own, 4), (count // 2,), 0, 1 << 20) % (slack + 1)
    sizes = sizes.at[donor].add(-passed).at[sink].add(passed)
    members = jnp.searchsorted(jnp.cumsum(sizes), jnp.arange(rows * top), side="right").astype(jnp.int32)
    table = members.reshape(top, rows).T
    table = table[jax.random.permutation(jax.random.fold_in(own, 1), rows)]
    turn = jax.random.randint(jax.random.fold_in(own, 2), (rows, 1), 0, top)
    return jnp.take_along_axis(table, (jnp.arange(top)[None, :] + turn) % top, axis=1)


def load_shares(amount, total, reach, skew, full):
    loads = [(1 << 20) // math.isqrt(grade ** skew) + 1 for grade in range(1, amount + 1)]
    largest = reach if full else min(reach, max(-(-total // amount), total * loads[0] // sum(loads)))
    least = 1 if total - largest >= amount - 1 else 0
    holding, spare = [largest] + [least] * (amount - 1), total - largest - least * (amount - 1)
    while spare > 0:
        free = [i for i in range(1, amount) if holding[i] < largest] or [i for i in range(1, amount) if holding[i] < reach]
        pool, remaining = sum([loads[i] for i in free]), spare
        for i in free:
            extra = min(reach - holding[i], max(1, remaining * loads[i] // pool), spare)
            holding[i] = holding[i] + extra
            spare = spare - extra
    return np.array(holding)


def normal_values(own_key, extent, scale, limit, cuts=(), held_as=jnp.bfloat16):
    array = scale * jax.random.normal(own_key, extent, jnp.float32)
    if cuts:
        array = array * block_levels(own_key, extent, cuts, -0.22, 0.18)
    return jnp.clip(array, -limit, limit).astype(held_as)


def setup_inputs(seed: int = 0) -> dict:
    arg_keys = jax.random.split(jax.random.key(seed), 17)
    tokens_in = normal_values(arg_keys[0], (MICRO, GROUP * N_DP, D), 1.0, 6.0, ((1, 16), (2, 2)))
    out_cotangent = normal_values(arg_keys[1], (MICRO, GROUP * N_DP, D), 1.0, 6.0, ((1, 16), (2, 2)))
    expert_ids_keys = jax.random.split(jax.random.fold_in(arg_keys[2], 1), MICRO * (GROUP * N_DP) // GROUP)
    expert_ids_turns = jax.random.permutation(jax.random.fold_in(arg_keys[2], 3), MICRO * (GROUP * N_DP) // GROUP)
    expert_ids = jax.vmap(lambda own, number: deal_out(jax.random.fold_in(arg_keys[2], 2), own, number, GROUP, EXPERTS, TOP, CAP, 1))(expert_ids_keys, expert_ids_turns).reshape((MICRO, GROUP * N_DP, TOP))
    gate_values = jnp.clip(0.25 + 0.5 * jax.random.uniform(arg_keys[3], (MICRO, GROUP * N_DP, TOP), jnp.float32) ** block_levels(arg_keys[3], (MICRO, GROUP * N_DP, TOP), ((1, 8),), -0.2, 0.2), 0.25, 0.75)
    first_gain = jnp.clip(1.0 + 0.1 * jax.random.normal(arg_keys[4], (D,), jnp.float32), 0.5, 1.5)
    first_shift = normal_values(arg_keys[5], (D,), 0.3, 1.75, ((0, 2),), jnp.float32)
    second_gain = jnp.clip(1.0 + 0.1 * jax.random.normal(arg_keys[6], (D,), jnp.float32), 0.5, 1.5)
    second_shift = normal_values(arg_keys[7], (D,), 0.3, 1.75, ((0, 2),), jnp.float32)
    qkv_weight = normal_values(arg_keys[8], (D, 3, D), D ** -0.5, 0.25, ((0, 16), (2, 2)))
    qkv_bias = normal_values(arg_keys[9], (2, D), 0.3, 1.75, ((1, 16),), jnp.float32)
    proj_weight = normal_values(arg_keys[10], (D, D), (D // 4) ** -0.5, 0.5, ((0, 16), (1, 2)))
    proj_bias = normal_values(arg_keys[11], (D,), 0.3, 1.75, ((0, 16),), jnp.float32)
    expand_weight = normal_values(arg_keys[12], (EXPERTS, D, HIDDEN_SIZE), D ** -0.5, 0.25, ((0, 8), (1, 2), (2, 2)))
    expand_bias = normal_values(arg_keys[13], (EXPERTS, HIDDEN_SIZE), 0.3, 1.75, ((0, 2), (1, 16)), jnp.float32)
    contract_weight = normal_values(arg_keys[14], (EXPERTS, HIDDEN_SIZE, D), (HIDDEN_SIZE // 4) ** -0.5, 0.25, ((0, 8), (1, 2), (2, 2)))
    contract_bias = normal_values(arg_keys[15], (EXPERTS, D), 0.3, 1.75, ((1, 16),), jnp.float32)
    return dict(tokens_in=tokens_in, out_cotangent=out_cotangent, expert_ids=expert_ids, gate_values=gate_values, first_gain=first_gain, first_shift=first_shift, second_gain=second_gain, second_shift=second_shift, qkv_weight=qkv_weight, qkv_bias=qkv_bias, proj_weight=proj_weight, proj_bias=proj_bias, expand_weight=expand_weight, expand_bias=expand_bias, contract_weight=contract_weight, contract_bias=contract_bias)


@jax.custom_vjp
def low(v):
    return lax.optimization_barrier(v.astype(jnp.bfloat16)).astype(jnp.float32)

@jax.custom_vjp
def low_back(v):
    return v

def low_keep(v):
    return (low(v), None)

def low_pass(kept, grad):
    return (grad,)

def back_keep(v):
    return (v, None)

def back_low(kept, grad):
    return (low(grad),)
low.defvjp(low_keep, low_pass)
low_back.defvjp(back_keep, back_low)
EPS = 1e-06
HIGH = lax.Precision.HIGHEST

def normalize(value, gain, shift):
    center = lax.optimization_barrier(jnp.mean(value, axis=-1, keepdims=True))
    spread = lax.optimization_barrier(jnp.mean(value * value, axis=-1, keepdims=True)) - center * center
    return (value - center) * lax.rsqrt(spread + EPS) * gain + shift

def destinations(routes):
    flat = routes.reshape(-1).astype(jnp.int32)
    labels = jnp.arange(EXPERTS, dtype=jnp.int32)
    onehot = (flat[:, None] == labels[None, :]).astype(jnp.int32)
    before = jnp.cumsum(onehot, axis=0) - onehot
    place = lax.optimization_barrier(jnp.sum(before * onehot, axis=1))
    return (flat * CAP + place).reshape(routes.shape).astype(jnp.int32)

def block_forward(params, tokens, routes, weights):
    first_gain, first_shift, second_gain, second_shift, qkv_weight, qkv_bias, proj_weight, proj_bias, expand_weight, expand_bias, contract_weight, contract_bias = params
    head_dim = D // HEADS
    images = tokens.shape[0] // SEQ
    normed = low(normalize(tokens, first_gain, first_shift))
    mixed = jnp.einsum('td,dcf->tcf', normed, qkv_weight, precision=HIGH)
    offset = jnp.stack([qkv_bias[0], jnp.zeros_like(qkv_bias[0]), qkv_bias[1]])
    triple = low(low_back(mixed + offset[None]))
    triple = triple.reshape(images, SEQ, 3, HEADS, head_dim)
    query = triple[:, :, 0]
    keys = triple[:, :, 1]
    values = triple[:, :, 2]
    scores = low_back(jnp.einsum('iqhd,ikhd->ihqk', query, keys, precision=HIGH) * head_dim ** (-0.5))
    peak = lax.optimization_barrier(jnp.max(scores, axis=-1, keepdims=True))
    expo = jnp.exp(scores - peak)
    prob = low(expo / lax.optimization_barrier(jnp.sum(expo, axis=-1, keepdims=True)))
    attended = jnp.einsum('ihqk,ikhd->iqhd', prob, values, precision=HIGH).reshape(tokens.shape[0], D)
    attended = low(low_back(attended))
    branch = low_back(jnp.dot(attended, proj_weight, precision=HIGH) + proj_bias)
    middle = tokens + branch
    second = low(normalize(middle, second_gain, second_shift))
    target = destinations(routes)
    slots = jnp.zeros((EXPERTS * CAP, D), jnp.float32).at[target.reshape(-1)].add(jnp.repeat(second, TOP, axis=0))
    slots = slots.reshape(EXPERTS, CAP, D)
    inner = low_back(jnp.einsum('ecd,edh->ech', slots, expand_weight, precision=HIGH) + expand_bias[:, None, :])
    active = low(jax.nn.gelu(inner, approximate=False))
    outer = low_back(jnp.einsum('ech,ehd->ecd', active, contract_weight, precision=HIGH)).reshape(EXPERTS * CAP, D)
    picked = outer[target] + contract_bias[routes]
    expert_sum = low_back(lax.optimization_barrier(jnp.sum(weights[..., None] * picked, axis=1)))
    return middle + expert_sum

def reference(tokens_in, out_cotangent, expert_ids, gate_values, first_gain, first_shift, second_gain, second_shift, qkv_weight, qkv_bias, proj_weight, proj_bias, expand_weight, expand_bias, contract_weight, contract_bias):
    params = tuple((item.astype(jnp.float32) for item in (first_gain, first_shift, second_gain, second_shift, qkv_weight, qkv_bias, proj_weight, proj_bias, expand_weight, expand_bias, contract_weight, contract_bias)))
    blocks = MICRO * N_DP
    tokens = tokens_in.astype(jnp.float32).reshape(blocks, GROUP, D)
    routes = expert_ids.reshape(blocks, GROUP, TOP).astype(jnp.int32)
    weights = gate_values.astype(jnp.float32).reshape(blocks, GROUP, TOP)

    def forward(params, tokens):

        def single(pack):
            return block_forward(params, pack[0], pack[1], pack[2])
        return lax.map(jax.checkpoint(single), (tokens, routes, weights))
    result, pull = jax.vjp(forward, params, tokens)
    grads, token_grads = pull(out_cotangent.astype(jnp.float32).reshape(blocks, GROUP, D))
    layer_out = result.reshape(MICRO, GROUP * N_DP, D).astype(jnp.bfloat16)
    input_grad = token_grads.reshape(MICRO, GROUP * N_DP, D)
    return (layer_out, input_grad, grads[0], grads[1], grads[2], grads[3], grads[4], grads[5], grads[6], grads[7], grads[8], grads[9], grads[10], grads[11])
```

```python
import functools

import jax
import jax.numpy as jnp
from jax import lax
from jax.experimental import pallas as pl
from jax.experimental.pallas import tpu as pltpu
from jax.sharding import PartitionSpec as P

D = 512
HEADS = 8
EXPERTS = 32
TOP = 2
SEQ = 197
HEAD_DIM = D // HEADS
PAIR = 2 * HEAD_DIM
PAD = 208

EPS = 1e-06
HIGH = lax.Precision.HIGHEST
ROOT_HALF = 0.7071067811865476
DENSITY = 0.3989422804014327
SCALE = HEAD_DIM ** (-0.5)
FAR = -1e30
MIB = 1 << 20

BF16 = jnp.bfloat16
F32 = jnp.float32


def round_up(value, unit):
    return (value + unit - 1) // unit * unit


def swap(value, axis, bit=1):
    size = lax.axis_size(axis)
    return lax.ppermute(value, axis, [(place, place ^ bit) for place in range(size)])


def either(first, when_true, when_false):
    return jnp.where(first, when_true, when_false)


def in_order(index, own, other, axis):
    return jnp.where(
        index == 0,
        jnp.concatenate([own, other], axis),
        jnp.concatenate([other, own], axis),
    )


def chosen(array, index, axis=0):
    return lax.dynamic_index_in_dim(array, index, axis, keepdims=False)


def contract(left, right, left_dim, right_dim):
    return lax.dot_general(
        left, right, (((left_dim,), (right_dim,)), ((), ())), preferred_element_type=F32
    )


def call(kernel, grid, in_specs, out_specs, out_shape, scratch=(), limit=48):
    return pl.pallas_call(
        kernel,
        grid=grid,
        in_specs=in_specs,
        out_specs=out_specs,
        out_shape=out_shape,
        scratch_shapes=list(scratch),
        compiler_params=pltpu.CompilerParams(
            dimension_semantics=("arbitrary",) * len(grid), vmem_limit_bytes=limit * MIB
        ),
    )


def whole(shape):
    return pl.BlockSpec(shape, lambda *_: (0,) * len(shape))


def stepped(shape, axis=0):
    return pl.BlockSpec(
        shape, lambda g: tuple(g if place == axis else 0 for place in range(len(shape)))
    )


def destinations(routes, capacity):
    labels = jnp.arange(EXPERTS, dtype=jnp.int32)
    named = (routes[:, :, None] == labels).astype(F32)
    count = routes.shape[0]
    place = jnp.arange(count, dtype=jnp.int32)
    earlier = (place[None, :] < place[:, None]).astype(BF16)
    before = jnp.dot(earlier, named.sum(axis=1).astype(BF16), preferred_element_type=F32)
    return jnp.sum(before[:, None, :] * named, axis=2).astype(jnp.int32)


def dispatch_kernel(gated, target_ref, gate_ref, own_ref, other_ref, out_ref):
    rows = out_ref.shape[0]
    count = own_ref.shape[0]
    place = lax.broadcasted_iota(jnp.int32, (rows, count), 0) + pl.program_id(0) * rows
    total = None
    for half, tokens in ((0, own_ref), (1, other_ref)):
        first = place == target_ref[2 * half : 2 * half + 1, :]
        second = place == target_ref[2 * half + 1 : 2 * half + 2, :]
        if gated:
            weight = jnp.where(
                first,
                gate_ref[2 * half : 2 * half + 1, :],
                jnp.where(second, gate_ref[2 * half + 1 : 2 * half + 2, :], 0.0),
            )
        else:
            weight = jnp.where(first | second, 1.0, 0.0)
        term = jnp.dot(weight.astype(BF16), tokens[...], preferred_element_type=F32)
        total = term if total is None else total + term
    out_ref[...] = total.astype(BF16)


def dispatch(target_rows, gate_rows, own, other, rows, gated):
    steps = 4
    return call(
        functools.partial(dispatch_kernel, gated),
        (steps,),
        [whole(target_rows.shape), whole(gate_rows.shape), whole(own.shape), whole(other.shape)],
        stepped((rows // steps, D)),
        jax.ShapeDtypeStruct((rows, D), BF16),
    )(target_rows, gate_rows, own, other)


def combine_kernel(gated, target_ref, gate_ref, slots_ref, out_ref):
    count, rows = out_ref.shape[0], slots_ref.shape[0]
    place = lax.broadcasted_iota(jnp.int32, (count, rows), 1)
    first = place == target_ref[:, 0:1]
    second = place == target_ref[:, 1:2]
    if gated:
        weight = jnp.where(first, gate_ref[:, 0:1], jnp.where(second, gate_ref[:, 1:2], 0.0))
    else:
        weight = jnp.where(first | second, 1.0, 0.0)
    out = jnp.dot(weight.astype(BF16), slots_ref[...], preferred_element_type=F32)
    out_ref[...] = out.astype(out_ref.dtype)


def combine(target_columns, gate_columns, slots, gated, dtype):
    steps = 2
    count = target_columns.shape[0]
    return call(
        functools.partial(combine_kernel, gated),
        (steps,),
        [
            stepped((count // steps, TOP)),
            stepped((count // steps, TOP)),
            whole(slots.shape),
        ],
        stepped((count // steps, D)),
        jax.ShapeDtypeStruct((count, D), dtype),
    )(target_columns, gate_columns, slots)


def normalized(value):
    center = jnp.mean(value, axis=-1, keepdims=True)
    spread = jnp.mean(value * value, axis=-1, keepdims=True) - center * center
    factor = lax.rsqrt(spread + EPS)
    return (value - center) * factor, factor


def norm_back(grad, scaled, factor, gain):
    upper = grad * gain
    return factor * (
        upper
        - jnp.mean(upper, axis=-1, keepdims=True)
        - scaled * jnp.mean(upper * scaled, axis=-1, keepdims=True)
    )


def forward_kernel(
    x_ref, wq_ref, bq_ref, wp_ref, bp_ref, norm_ref, low_ref, mid_ref, tri_ref, att_ref, lse_ref
):
    x = x_ref[0].astype(F32)
    scaled, _ = normalized(x)
    low = (scaled * norm_ref[0:1, :] + norm_ref[1:2, :]).astype(BF16)
    tri = jnp.dot(low, wq_ref[...], preferred_element_type=F32) + bq_ref[...]
    tri_ref[0] = tri.astype(BF16)
    lane = lax.broadcasted_iota(jnp.int32, (PAD, PAIR), 1)
    shut = lax.broadcasted_iota(jnp.int32, (PAD, PAD), 1) >= SEQ
    logs = jnp.zeros((PAD, 128), F32)
    column = lax.broadcasted_iota(jnp.int32, (PAD, 128), 1)
    for pair in range(HEADS // 2):
        at = pair * PAIR
        query = tri_ref[0, :, at : at + PAIR]
        keys = tri_ref[0, :, D + at : D + at + PAIR]
        values = tri_ref[0, :, 2 * D + at : 2 * D + at + PAIR]
        outs = []
        for side in range(2):
            mine = (lane // HEAD_DIM) == side
            scores = contract(jnp.where(mine, query, jnp.zeros_like(query)), keys, 1, 1) * SCALE
            scores = jnp.where(shut, FAR, scores)
            peak = jnp.max(scores, axis=-1, keepdims=True)
            expo = jnp.exp(scores - peak)
            total = jnp.sum(expo, axis=-1, keepdims=True)
            prob = (expo / total).astype(BF16)
            outs.append(jnp.dot(prob, values, preferred_element_type=F32))
            logs = jnp.where(column == 2 * pair + side, peak + jnp.log(total), logs)
        att_ref[0, :, at : at + PAIR] = jnp.where(lane < HEAD_DIM, outs[0], outs[1]).astype(BF16)
    lse_ref[0] = logs
    branch = jnp.dot(att_ref[0], wp_ref[...], preferred_element_type=F32) + bp_ref[...]
    middle = x + branch
    mid_ref[0] = middle
    scaled2, _ = normalized(middle)
    low_ref[0] = (scaled2 * norm_ref[2:3, :] + norm_ref[3:4, :]).astype(BF16)


def attention_forward(x, wq, bq, wp, bp, norms):
    images = x.shape[0]
    return call(
        forward_kernel,
        (images,),
        [
            stepped((1, PAD, D)),
            whole(wq.shape),
            whole(bq.shape),
            whole(wp.shape),
            whole(bp.shape),
            whole(norms.shape),
        ],
        [
            stepped((1, PAD, D)),
            stepped((1, PAD, D)),
            stepped((1, PAD, 3 * D)),
            stepped((1, PAD, D)),
            stepped((1, PAD, 128)),
        ],
        [
            jax.ShapeDtypeStruct((images, PAD, D), BF16),
            jax.ShapeDtypeStruct((images, PAD, D), F32),
            jax.ShapeDtypeStruct((images, PAD, 3 * D), BF16),
            jax.ShapeDtypeStruct((images, PAD, D), BF16),
            jax.ShapeDtypeStruct((images, PAD, 128), F32),
        ],
    )(x, wq, bq, wp, bp, norms)


def backward_kernel(
    x_ref,
    mid_ref,
    cot_ref,
    own_ref,
    got_ref,
    tri_ref,
    att_ref,
    lse_ref,
    wq_ref,
    wp_ref,
    norm_ref,
    grad_ref,
    dwq_ref,
    dwp_ref,
    sums_ref,
    tg_ref,
):
    @pl.when(pl.program_id(0) == 0)
    def _():
        dwq_ref[...] = jnp.zeros_like(dwq_ref)
        dwp_ref[...] = jnp.zeros_like(dwp_ref)
        sums_ref[...] = jnp.zeros_like(sums_ref)

    low_grad = own_ref[0] + got_ref[0].astype(F32)
    scaled2, factor2 = normalized(mid_ref[0])
    sums_ref[2:3, :] += jnp.sum(low_grad * scaled2, axis=0, keepdims=True)
    sums_ref[3:4, :] += jnp.sum(low_grad, axis=0, keepdims=True)
    mid_grad = cot_ref[0].astype(F32) + norm_back(low_grad, scaled2, factor2, norm_ref[2:3, :])
    branch = mid_grad.astype(BF16)
    sums_ref[4:5, :] += jnp.sum(branch.astype(F32), axis=0, keepdims=True)
    dwp_ref[...] += contract(att_ref[0], branch, 0, 0)
    att_grad = contract(branch, wp_ref[...], 1, 1).astype(BF16)
    lane = lax.broadcasted_iota(jnp.int32, (PAD, PAIR), 1)
    shut = lax.broadcasted_iota(jnp.int32, (PAD, PAD), 1) >= SEQ
    for pair in range(HEADS // 2):
        at = pair * PAIR
        query = tri_ref[0, :, at : at + PAIR]
        keys = tri_ref[0, :, D + at : D + at + PAIR]
        values = tri_ref[0, :, 2 * D + at : 2 * D + at + PAIR]
        upstream = att_grad[:, at : at + PAIR]
        query_grads = []
        key_grad = jnp.zeros((PAD, PAIR), F32)
        value_grad = jnp.zeros((PAD, PAIR), F32)
        for side in range(2):
            mine = (lane // HEAD_DIM) == side
            query_one = jnp.where(mine, query, jnp.zeros_like(query))
            grad_one = jnp.where(mine, upstream, jnp.zeros_like(upstream))
            scores = contract(query_one, keys, 1, 1) * SCALE
            scores = jnp.where(shut, FAR, scores)
            head = 2 * pair + side
            prob = jnp.exp(scores - lse_ref[0, :, head : head + 1])
            prob_grad = contract(grad_one, values, 1, 1)
            value_grad += contract(prob.astype(BF16), grad_one, 0, 0)
            inside = jnp.sum(prob * prob_grad, axis=-1, keepdims=True)
            score_grad = (prob * (prob_grad - inside)).astype(BF16)
            query_grads.append(jnp.dot(score_grad, keys, preferred_element_type=F32))
            key_grad += contract(score_grad, query_one, 0, 0)
        query_grad = jnp.where(lane < HEAD_DIM, query_grads[0], query_grads[1])
        tg_ref[:, at : at + PAIR] = (query_grad * SCALE).astype(BF16)
        tg_ref[:, D + at : D + at + PAIR] = (key_grad * SCALE).astype(BF16)
        tg_ref[:, 2 * D + at : 2 * D + at + PAIR] = value_grad.astype(BF16)
    tri_grad = tg_ref[...]
    sums_ref[5:6, :] += jnp.sum(tri_grad[:, :D].astype(F32), axis=0, keepdims=True)
    sums_ref[6:7, :] += jnp.sum(tri_grad[:, 2 * D :].astype(F32), axis=0, keepdims=True)
    scaled, factor = normalized(x_ref[0].astype(F32))
    low = (scaled * norm_ref[0:1, :] + norm_ref[1:2, :]).astype(BF16)
    dwq_ref[...] += contract(low, tri_grad, 0, 0)
    normed_grad = contract(tri_grad, wq_ref[...], 1, 1)
    sums_ref[0:1, :] += jnp.sum(normed_grad * scaled, axis=0, keepdims=True)
    sums_ref[1:2, :] += jnp.sum(normed_grad, axis=0, keepdims=True)
    grad_ref[0] = (mid_grad + norm_back(normed_grad, scaled, factor, norm_ref[0:1, :])).astype(BF16)


def attention_backward(x, middle, cot, own, got, tri, att, lse, wq, wp, norms):
    images = x.shape[0]
    return call(
        backward_kernel,
        (images,),
        [
            stepped((1, PAD, D)),
            stepped((1, PAD, D)),
            stepped((1, PAD, D)),
            stepped((1, PAD, D)),
            stepped((1, PAD, D)),
            stepped((1, PAD, 3 * D)),
            stepped((1, PAD, D)),
            stepped((1, PAD, 128)),
            whole(wq.shape),
            whole(wp.shape),
            whole(norms.shape),
        ],
        [
            stepped((1, PAD, D)),
            whole((D, 3 * D)),
            whole((D, D)),
            whole((8, D)),
        ],
        [
            jax.ShapeDtypeStruct((images, PAD, D), BF16),
            jax.ShapeDtypeStruct((D, 3 * D), F32),
            jax.ShapeDtypeStruct((D, D), F32),
            jax.ShapeDtypeStruct((8, D), F32),
        ],
        scratch=[pltpu.VMEM((PAD, 3 * D), BF16)],
    )(x, middle, cot, own, got, tri, att, lse, wq, wp, norms)


STEPS = 4


def active_grad_kernel(grad_ref, wc_ref, out_ref):
    features, hidden = wc_ref.shape[3], wc_ref.shape[2]
    left, right = grad_ref[:, :features], grad_ref[:, features:]
    for half in range(2):
        part = contract(left, wc_ref[0, half], 1, 1) + contract(right, wc_ref[1, half], 1, 1)
        out_ref[:, half * hidden : (half + 1) * hidden] = part.astype(BF16)


def expert_kernel(
    slots_ref, gact_ref, we_ref, be_ref, act_ref, inner_grad_ref, slot_grad_ref, bias_grad_ref
):
    @pl.when(pl.program_id(0) == 0)
    def _():
        bias_grad_ref[...] = jnp.zeros_like(bias_grad_ref)

    features, hidden = we_ref.shape[2], we_ref.shape[3]
    left, right = slots_ref[:, :features], slots_ref[:, features:]
    chunk = hidden // 2
    grads = [None, None]
    for half in range(2):
        for piece in range(2):
            lo = piece * chunk
            at = half * hidden + lo
            inner = (
                jnp.dot(left, we_ref[0, half, :, lo : lo + chunk], preferred_element_type=F32)
                + jnp.dot(right, we_ref[1, half, :, lo : lo + chunk], preferred_element_type=F32)
                + be_ref[:, at : at + chunk]
            )
            share = 0.5 * (1.0 + lax.erf(inner * ROOT_HALF))
            act_ref[:, at : at + chunk] = (inner * share).astype(BF16)
            slope = share + inner * (DENSITY * jnp.exp(-0.5 * inner * inner))
            grad = (gact_ref[:, at : at + chunk].astype(F32) * slope).astype(BF16)
            inner_grad_ref[:, at : at + chunk] = grad
            bias_grad_ref[:, at : at + chunk] += jnp.sum(
                grad.astype(F32), axis=0, keepdims=True
            )
            for side in range(2):
                term = contract(grad, we_ref[side, half, :, lo : lo + chunk], 1, 1)
                grads[side] = term if grads[side] is None else grads[side] + term
    for side in range(2):
        slot_grad_ref[:, side * features : (side + 1) * features] = grads[side].astype(BF16)


def outer_kernel(act_ref, wc_ref, bc_ref, out_ref):
    features, hidden = wc_ref.shape[3], wc_ref.shape[2]
    for side in range(2):
        at = side * features
        total = (
            jnp.dot(act_ref[:, :hidden], wc_ref[side, 0], preferred_element_type=F32)
            + jnp.dot(act_ref[:, hidden:], wc_ref[side, 1], preferred_element_type=F32)
            + bc_ref[:, at : at + features]
        )
        out_ref[:, at : at + features] = total.astype(BF16)


def contract_grad_kernel(act_ref, grad_ref, out_ref, bias_ref):
    features = out_ref.shape[3]
    product = contract(act_ref[...], grad_ref[...], 0, 0)
    for side in range(2):
        out_ref[side, 0] = product[:, side * features : (side + 1) * features].astype(BF16)

    @pl.when(pl.program_id(0) == 0)
    def _():
        bias_ref[...] = jnp.sum(grad_ref[...].astype(F32), axis=0, keepdims=True)


def expand_grad_kernel(slots_ref, grad_ref, out_ref):
    features = out_ref.shape[2]
    product = contract(slots_ref[...], grad_ref[...], 0, 0)
    for side in range(2):
        out_ref[side, 0] = product[side * features : (side + 1) * features, :].astype(BF16)


def active_grad(grad_slots, wc):
    rows, hidden = grad_slots.shape[0], 2 * wc.shape[2]
    return call(
        active_grad_kernel,
        (STEPS,),
        [stepped((rows // STEPS, D)), whole(wc.shape)],
        stepped((rows // STEPS, hidden)),
        jax.ShapeDtypeStruct((rows, hidden), BF16),
    )(grad_slots, wc)


def experts_middle(slots, gact, we, be):
    rows, hidden = gact.shape
    return call(
        expert_kernel,
        (STEPS,),
        [
            stepped((rows // STEPS, D)),
            stepped((rows // STEPS, hidden)),
            whole(we.shape),
            whole(be.shape),
        ],
        [
            stepped((rows // STEPS, hidden)),
            stepped((rows // STEPS, hidden)),
            stepped((rows // STEPS, D)),
            whole((1, hidden)),
        ],
        [
            jax.ShapeDtypeStruct((rows, hidden), BF16),
            jax.ShapeDtypeStruct((rows, hidden), BF16),
            jax.ShapeDtypeStruct((rows, D), BF16),
            jax.ShapeDtypeStruct((1, hidden), F32),
        ],
    )(slots, gact, we, be)


def experts_outer(act, wc, bc):
    rows, hidden = act.shape
    return call(
        outer_kernel,
        (STEPS,),
        [stepped((rows // STEPS, hidden)), whole(wc.shape), whole(bc.shape)],
        stepped((rows // STEPS, D)),
        jax.ShapeDtypeStruct((rows, D), BF16),
    )(act, wc, bc)


def contract_grad(act, grad_slots):
    rows, hidden = act.shape
    chunk = hidden // STEPS
    return call(
        contract_grad_kernel,
        (STEPS,),
        [stepped((rows, chunk), 1), whole(grad_slots.shape)],
        [
            pl.BlockSpec((2, 1, chunk, D // 2), lambda g: (0, g // 2, g % 2, 0)),
            whole((1, D)),
        ],
        [
            jax.ShapeDtypeStruct((2, 2, hidden // 2, D // 2), BF16),
            jax.ShapeDtypeStruct((1, D), F32),
        ],
    )(act, grad_slots)


def expand_grad(slots, inner_grad):
    rows, hidden = inner_grad.shape
    chunk = hidden // STEPS
    return call(
        expand_grad_kernel,
        (STEPS,),
        [whole(slots.shape), stepped((rows, chunk), 1)],
        pl.BlockSpec((2, 1, D // 2, chunk), lambda g: (0, g // 2, 0, g % 2)),
        jax.ShapeDtypeStruct((2, 2, D // 2, hidden // 2), BF16),
    )(slots, inner_grad)


def expert_weight(block, row, col):
    if block.shape[0] == 1:
        halves = in_order(col, block, swap(block, "col"), 0)
    else:
        split = block.reshape((2, 2) + block.shape[1:])
        got = swap(chosen(split, 1 - col, 1), "col")
        kept = chosen(split, col, 1)
        halves = in_order(col, kept[:, None], got[:, None], 1)
    if block.shape[0] == 1:
        return in_order(row, halves[None], swap(halves, "row")[None], 0)
    got = swap(chosen(halves, 1 - row), "row")
    return in_order(row, chosen(halves, row)[None], got[None], 0)


def expert_weight_grad(grad, row, col, experts):
    got = swap(chosen(grad, 1 - row), "row")
    kept = chosen(grad, row)
    if experts == 1:
        halves = (kept.astype(F32) + got.astype(F32)).astype(BF16)
        got = swap(chosen(halves, 1 - col), "col")
        return (chosen(halves, col).astype(F32) + got.astype(F32))[None]
    both = in_order(row, kept[None], got[None], 0)
    got = swap(chosen(both, 1 - col, 1), "col")
    kept = chosen(both, col, 1)
    return in_order(col, kept[:, None], got[:, None], 1).reshape((4,) + grad.shape[2:]).astype(F32)


def bits_of(size):
    bits = []
    bit = size // 2
    order = []
    while bit:
        order.append(bit)
        bit //= 2
    bits = order[1::-1] + order[2:] if len(order) > 2 else order
    return bits


def gathered(block, size):
    order = []
    bit = size // 2
    while bit:
        order.append(bit)
        bit //= 2
    held = block.reshape((1,) * (len(order) + 2) + block.shape)
    place = lax.axis_index("dp")
    for bit in bits_of(size):
        axis = order.index(bit)
        held = in_order((place // bit) % 2, held, swap(held, "dp", bit), axis)
    held = in_order(lax.axis_index("col"), held, swap(held, "col"), len(order))
    held = in_order(lax.axis_index("row"), held, swap(held, "row"), len(order) + 1)
    return held.reshape((size, 2, 2) + block.shape)


def summed(blocks, size):
    order = []
    bit = size // 2
    while bit:
        order.append(bit)
        bit //= 2
    held = blocks.reshape((2,) * (len(order) + 2) + blocks.shape[3:])

    def halve(held, axis_name, bit, index, axis):
        got = swap(lax.dynamic_slice_in_dim(held, 1 - index, 1, axis), axis_name, bit)
        kept = lax.dynamic_slice_in_dim(held, index, 1, axis)
        return kept.astype(F32) + got.astype(F32)

    held = halve(held, "row", 1, lax.axis_index("row"), len(order) + 1).astype(BF16)
    held = halve(held, "col", 1, lax.axis_index("col"), len(order)).astype(BF16)
    place = lax.axis_index("dp")
    bits = bits_of(size)[::-1]
    for bit in bits:
        held = halve(held, "dp", bit, (place // bit) % 2, order.index(bit))
        held = held if bit == bits[-1] else held.astype(BF16)
    return held.reshape(blocks.shape[3:])


def everywhere(value, size):
    value = value + swap(value, "row")
    value = value + swap(value, "col")
    for bit in bits_of(size)[::-1]:
        value = value + swap(value, "dp", bit)
    return value


def as_rows(value, width):
    flat = value.reshape(-1)
    return jnp.pad(flat, (0, round_up(flat.shape[0], width) - flat.shape[0])).reshape(-1, width)


def on_device(
    tokens_in,
    out_cotangent,
    expert_ids,
    gate_values,
    first_gain,
    first_shift,
    second_gain,
    second_shift,
    qkv_weight,
    qkv_bias,
    proj_weight,
    proj_bias,
    expand_weight,
    expand_bias,
    contract_weight,
    contract_bias,
):
    size = lax.axis_size("dp")
    row, col, place = lax.axis_index("row"), lax.axis_index("col"), lax.axis_index("dp")
    local_rows, width = tokens_in.shape[1:]
    group = expert_ids.shape[1]
    images = local_rows // SEQ
    capacity = (group * TOP * 4 + 3 * EXPERTS - 1) // (3 * EXPERTS)
    local_experts = EXPERTS // size
    share = local_experts * capacity // 4
    held_rows = round_up(share, 8)
    peers = 2 * size
    rows = peers * held_rows

    block = jnp.concatenate(
        [
            as_rows(qkv_weight.transpose(1, 0, 2), width),
            as_rows(proj_weight, width),
            as_rows(expand_bias.astype(BF16), width),
            as_rows(contract_bias.astype(BF16), width),
            as_rows(qkv_bias.astype(BF16), width),
            as_rows(proj_bias.astype(BF16), width),
        ],
        0,
    )
    block = jnp.pad(block, ((0, round_up(block.shape[0], 16) - block.shape[0]), (0, 0)))
    parts = gathered(block, size)

    def taken(start, like):
        count = like.size // width if like.size >= width else 1
        found = parts[:, :, :, start : start + count]
        flat = found.reshape(found.shape[:3] + (-1,))[..., : like.size]
        return flat.reshape(found.shape[:3] + like.shape), start + count

    depth = qkv_weight.shape[0]
    wq, at = taken(0, qkv_weight.transpose(1, 0, 2))
    wq = wq.transpose(2, 0, 4, 3, 1, 5).reshape(D, 3 * D)
    wp, at = taken(at, proj_weight)
    wp = wp.transpose(1, 0, 3, 2, 4).reshape(D, D)
    be, at = taken(at, expand_bias)
    expert = place * local_experts + (2 * row + col) * local_experts // 4
    be = chosen(be, expert // (EXPERTS // 2), 2)
    be = chosen(be, expert % (EXPERTS // 2), 2)
    be = be.transpose(1, 0, 2).reshape(1, -1).astype(F32)
    bc, at = taken(at, contract_bias)
    bc = chosen(bc[:, 0], expert, 2).transpose(1, 0, 2).reshape(1, D).astype(F32)
    bq, at = taken(at, qkv_bias)
    bq = bq[:, :, 0].transpose(2, 1, 0, 3).reshape(2, D).astype(F32)
    bq = jnp.concatenate([bq[0], jnp.zeros((D,), F32), bq[1]]).reshape(1, 3 * D)
    bp, at = taken(at, proj_bias)
    bp = bp[:, 0].transpose(1, 0, 2).reshape(1, D).astype(F32)
    norms = jnp.stack([first_gain, first_shift, second_gain, second_shift])
    norms = in_order(row, norms, swap(norms, "row"), 1)

    def by_image(array):
        shaped = array.reshape(2, images, SEQ, width)
        return jnp.pad(shaped, ((0, 0), (0, 0), (0, PAD - SEQ), (0, 0)))

    same = row == col

    def to_chip(array):
        own = chosen(array, col)
        got = swap(chosen(array, 1 - col), "col")
        return either(same, own, got), either(same, got, own)

    kept, sent = to_chip(by_image(tokens_in))
    x = in_order(row, kept, swap(sent, "row"), 2)
    kept, sent = to_chip(by_image(out_cotangent))
    cot = in_order(
        row, jnp.stack([kept, sent]), swap(jnp.stack([sent, kept]), "row"), 3
    )

    routes = chosen(expert_ids, col)
    gates = chosen(gate_values, col)
    slot = destinations(routes, capacity)
    unit = routes % local_experts * capacity + slot
    home = unit // share
    target = (routes // local_experts * 2 + home % 2) * held_rows + unit % share
    target = jnp.where(home // 2 == row, target, -1)

    def own_first(array, fill):
        shaped = array.reshape(2, images, SEQ, TOP)
        shaped = jnp.pad(
            shaped, ((0, 0), (0, 0), (0, PAD - SEQ), (0, 0)), constant_values=fill
        ).reshape(2, images * PAD, TOP)
        return jnp.where(row == 0, shaped, shaped[::-1])

    target = own_first(target, -1)
    gates = own_first(gates, 0)
    target_rows = target.transpose(0, 2, 1).reshape(2 * TOP, images * PAD)
    gate_rows = gates.transpose(0, 2, 1).reshape(2 * TOP, images * PAD)

    def exchange(slots):
        shaped = slots.reshape(peers, held_rows, D)
        return lax.all_to_all(shaped, ("dp", "col"), 0, 0, tiled=True).reshape(rows, D)

    def flat(array):
        return array.reshape(images * PAD, D)

    grad_slots = dispatch(target_rows, gate_rows, flat(cot[0]), flat(cot[1]), rows, True)
    grad_slots = exchange(grad_slots)
    we = expert_weight(expand_weight, row, col)
    wc = expert_weight(contract_weight, row, col)
    gact = active_grad(grad_slots, wc)

    low, middle, tri, att, lse = attention_forward(x, wq, bq, wp, bp, norms)
    low = flat(low)
    slots = dispatch(target_rows, gate_rows, low, swap(low, "row"), rows, False)
    slots = exchange(slots)
    act, inner_grad, slot_grad, be_grad = experts_middle(slots, gact, we, be)
    slot_grad = exchange(slot_grad)
    outer = exchange(experts_outer(act, wc, bc))
    wc_grad, bc_grad = contract_grad(act, grad_slots)
    we_grad = expand_grad(slots, inner_grad)
    we_grad = expert_weight_grad(we_grad, row, col, local_experts)
    wc_grad = expert_weight_grad(wc_grad, row, col, local_experts)

    def back(array, gated):
        sent = combine(target[1], gates[1], array, gated, BF16)
        got = swap(sent, "row")
        own = combine(target[0], gates[0], array, gated, F32)
        return own, got

    def to_image(array):
        return array.reshape(images, PAD, D)

    own, got = back(slot_grad, False)
    x_grad, wq_grad, wp_grad, sums = attention_backward(
        x, middle, cot[0], to_image(own), to_image(got), tri, att, lse, wq, wp, norms
    )
    own, got = back(outer, True)
    layer_out = (flat(middle) + own + got.astype(F32)).astype(BF16)

    def to_tokens(array):
        shaped = array.reshape(images, PAD, 2, width)[:, :SEQ].reshape(local_rows, 2, width)
        kept = chosen(shaped, row, 1)
        got = swap(chosen(shaped, 1 - row, 1), "row")
        own, other = either(same, kept, got), either(same, got, kept)
        return in_order(col, own[None], swap(other, "col")[None], 0)

    piece = wq_grad.reshape(2, size, depth, 3, 2, width).transpose(1, 4, 0, 3, 2, 5)
    pieces = [piece.astype(BF16)]
    pieces.append(wp_grad.reshape(2, size, -1, 2, width).transpose(1, 0, 3, 2, 4).astype(BF16))
    hidden_part = expand_bias.shape[1]
    mine = (jnp.arange(EXPERTS, dtype=jnp.int32) == expert).astype(F32)
    piece = mine.reshape(1, 1, 2, EXPERTS // 2, 1) * be_grad.reshape(
        2, size, hidden_part
    ).transpose(1, 0, 2).reshape(size, 2, 1, 1, hidden_part)
    pieces.append(piece.astype(BF16))
    feature_part = contract_bias.shape[1]
    piece = mine.reshape(1, 1, EXPERTS, 1) * bc_grad.reshape(2, size, feature_part).transpose(
        1, 0, 2
    ).reshape(size, 2, 1, feature_part)
    pieces.append(jnp.broadcast_to(piece[:, None], (size, 2) + piece.shape[1:]).astype(BF16))
    bias_grads = sums[5:7].reshape(2, 2, size, -1).transpose(2, 1, 0, 3)
    pieces.append(
        jnp.broadcast_to(bias_grads[:, :, None], (size, 2, 2) + bias_grads.shape[2:]).astype(BF16)
    )
    proj_grads = sums[4].reshape(2, size, -1).transpose(1, 0, 2)
    pieces.append(
        jnp.broadcast_to(proj_grads[:, None], (size, 2) + proj_grads.shape[1:]).astype(BF16)
    )

    def as_blocks(piece):
        shaped = piece.reshape(size, 2, 2, -1)
        count = shaped.shape[-1]
        shaped = jnp.pad(shaped, ((0, 0),) * 3 + ((0, round_up(count, width) - count),))
        return shaped.reshape(size, 2, 2, -1, width)

    blocks = jnp.concatenate([as_blocks(piece) for piece in pieces], 3)
    short = round_up(blocks.shape[3], 16) - blocks.shape[3]
    blocks = jnp.pad(blocks, ((0, 0),) * 3 + ((0, short), (0, 0)))
    reduced = summed(blocks, size)

    def given(start, like):
        count = like.size // width if like.size >= width else 1
        found = reduced[start : start + count].reshape(-1)[: like.size]
        return found.reshape(like.shape), start + count

    out_wq, at = given(0, qkv_weight.transpose(1, 0, 2))
    out_wq = out_wq.transpose(1, 0, 2)
    out_wp, at = given(at, proj_weight)
    out_be, at = given(at, expand_bias)
    out_bc, at = given(at, contract_bias)
    out_bq, at = given(at, qkv_bias)
    out_bp, at = given(at, proj_bias)
    norm_total = everywhere(sums[:4], size)
    norm_total = lax.dynamic_slice_in_dim(norm_total, row * width, width, 1)
    return (
        to_tokens(layer_out),
        to_tokens(x_grad).astype(F32),
        norm_total[0],
        norm_total[1],
        norm_total[2],
        norm_total[3],
        out_wq,
        out_bq,
        out_wp,
        out_bp,
        we_grad,
        out_be,
        wc_grad,
        out_bc,
    )


def solution(mesh):
    return jax.shard_map(
        on_device,
        mesh=mesh,
        in_specs=(
            P(None, ("dp", "col"), "row"),
            P(None, ("dp", "col"), "row"),
            P(None, "dp", None),
            P(None, "dp", None),
            P("row"),
            P("row"),
            P("row"),
            P("row"),
            P(("row", "dp"), None, "col"),
            P(None, ("col", "dp")),
            P(("col", "dp"), "row"),
            P(("row", "dp")),
            P("dp", "row", "col"),
            P("row", ("col", "dp")),
            P("dp", "col", "row"),
            P(None, ("row", "dp")),
        ),
        out_specs=(
            P(None, ("dp", "col"), "row"),
            P(None, ("dp", "col"), "row"),
            P("row"),
            P("row"),
            P("row"),
            P("row"),
            P(("row", "dp"), None, "col"),
            P(None, ("col", "dp")),
            P(("col", "dp"), "row"),
            P(("row", "dp")),
            P("dp", "row", "col"),
            P("row", ("col", "dp")),
            P("dp", "col", "row"),
            P(None, ("row", "dp")),
        ),
        check_vma=False,
    )
```

```python
import functools

import jax
import jax.numpy as jnp
from jax import lax
from jax.experimental import pallas as pl
from jax.experimental.pallas import tpu as pltpu
from jax.sharding import PartitionSpec as P

D = 512
HEADS = 8
EXPERTS = 32
TOP = 2
SEQ = 197
HEAD_DIM = D // HEADS
PAIR = 2 * HEAD_DIM
PAD = 208

EPS = 1e-06
HIGH = lax.Precision.HIGHEST
ROOT_HALF = 0.7071067811865476
DENSITY = 0.3989422804014327
SCALE = HEAD_DIM ** (-0.5)
FAR = -1e30
MIB = 1 << 20

BF16 = jnp.bfloat16
F32 = jnp.float32


def round_up(value, unit):
    return (value + unit - 1) // unit * unit


def swap(value, axis, bit=1):
    size = lax.axis_size(axis)
    return lax.ppermute(value, axis, [(place, place ^ bit) for place in range(size)])


def either(first, when_true, when_false):
    return jnp.where(first, when_true, when_false)


def in_order(index, own, other, axis):
    return jnp.where(
        index == 0,
        jnp.concatenate([own, other], axis),
        jnp.concatenate([other, own], axis),
    )


def chosen(array, index, axis=0):
    return lax.dynamic_index_in_dim(array, index, axis, keepdims=False)


def contract(left, right, left_dim, right_dim):
    return lax.dot_general(
        left, right, (((left_dim,), (right_dim,)), ((), ())), preferred_element_type=F32
    )


def after(value, *others):
    return lax.optimization_barrier((value,) + others)[0]


def call(
    kernel, micros, grid, in_specs, out_specs, out_shape, scratch=(), limit=48, scalars=0
):
    return pl.pallas_call(
        kernel,
        grid_spec=pltpu.PrefetchScalarGridSpec(
            num_scalar_prefetch=scalars,
            grid=grid,
            in_specs=in_specs,
            out_specs=out_specs,
            scratch_shapes=list(scratch),
        ),
        out_shape=out_shape,
        cost_estimate=pl.CostEstimate(
            flops=int(micros * 1e9), bytes_accessed=int(micros * 2e6), transcendentals=0
        ),
        compiler_params=pltpu.CompilerParams(
            dimension_semantics=("arbitrary",) * len(grid), vmem_limit_bytes=limit * MIB
        ),
    )


def whole(shape):
    return pl.BlockSpec(shape, lambda *_: (0,) * len(shape))


def stepped(shape, axis=0):
    return pl.BlockSpec(
        shape, lambda g, *_: tuple(g if place == axis else 0 for place in range(len(shape)))
    )


def destinations(routes, capacity):
    labels = jnp.arange(EXPERTS, dtype=jnp.int32)
    named = (routes[:, :, None] == labels).astype(F32)
    count = routes.shape[0]
    place = jnp.arange(count, dtype=jnp.int32)
    earlier = (place[None, :] < place[:, None]).astype(BF16)
    before = jnp.dot(earlier, named.sum(axis=1).astype(BF16), preferred_element_type=F32)
    return jnp.sum(before[:, None, :] * named, axis=2).astype(jnp.int32)


def dispatch_kernel(gated, target_ref, gate_ref, own_ref, other_ref, out_ref):
    rows = out_ref.shape[0]
    count = own_ref.shape[0]
    place = lax.broadcasted_iota(jnp.int32, (rows, count), 0) + pl.program_id(0) * rows
    total = None
    for half, tokens in ((0, own_ref), (1, other_ref)):
        first = place == target_ref[2 * half : 2 * half + 1, :]
        second = place == target_ref[2 * half + 1 : 2 * half + 2, :]
        if gated:
            weight = jnp.where(
                first,
                gate_ref[2 * half : 2 * half + 1, :],
                jnp.where(second, gate_ref[2 * half + 1 : 2 * half + 2, :], 0.0),
            )
        else:
            weight = jnp.where(first | second, 1.0, 0.0)
        term = jnp.dot(weight.astype(BF16), tokens[...], preferred_element_type=F32)
        total = term if total is None else total + term
    out_ref[...] = total.astype(BF16)


def dispatch(target_rows, gate_rows, own, other, rows, gated):
    steps = 4
    return call(
        functools.partial(dispatch_kernel, gated),
        5,
        (steps,),
        [whole(target_rows.shape), whole(gate_rows.shape), whole(own.shape), whole(other.shape)],
        stepped((rows // steps, D)),
        jax.ShapeDtypeStruct((rows, D), BF16),
    )(target_rows, gate_rows, own, other)


def combined(gated, target_ref, gate_ref, slots_ref):
    count, rows = target_ref.shape[1], slots_ref.shape[0]
    place = lax.broadcasted_iota(jnp.int32, (count, rows), 1)
    first = place == target_ref[0, :, 0:1]
    second = place == target_ref[0, :, 1:2]
    if gated:
        weight = jnp.where(first, gate_ref[0, :, 0:1], jnp.where(second, gate_ref[0, :, 1:2], 0.0))
    else:
        weight = jnp.where(first | second, 1.0, 0.0)
    return jnp.dot(weight.astype(BF16), slots_ref[...], preferred_element_type=F32)


def combine_kernel(place_ref, target_ref, gate_ref, slots_ref, out_ref):
    out_ref[...] = combined(False, target_ref, gate_ref, slots_ref).astype(out_ref.dtype)


def combine_out_kernel(
    place_ref, target_ref, gate_ref, slots_ref, middle_ref, kept_ref, sent_ref
):
    out = combined(True, target_ref, gate_ref, slots_ref)
    out = jnp.where(place_ref[1] == 0, out + middle_ref[...], out)
    kept_ref[...], sent_ref[...] = feature_halves(place_ref, out.astype(BF16))


def feature_halves(place_ref, value):
    half = value.shape[-1] // 2
    low, high = value[..., :half], value[..., half:]
    first = place_ref[0] == 0
    return jnp.where(first, low, high), jnp.where(first, high, low)


def combine(place, half, target, gates, slots, dtype=None, middle=None):
    steps = 2
    count = target.shape[1]
    column = pl.BlockSpec((1, count // steps, TOP), lambda g, place: (place[1], g, 0))
    ins, more = [column, column, whole(slots.shape)], ()
    if dtype is None:
        ins, more = ins + [stepped((count // steps, D))], (middle,)
        shape = (count // steps, D // 2)
        outs = [stepped(shape)] * 2
        shapes = [jax.ShapeDtypeStruct((count, D // 2), BF16)] * 2
    else:
        outs = stepped((count // steps, D))
        shapes = jax.ShapeDtypeStruct((count, D), dtype)
    return call(
        combine_out_kernel if dtype is None else combine_kernel,
        5,
        (steps,),
        ins,
        outs,
        shapes,
        scalars=1,
    )(jnp.stack([place[0], half]), target, gates, slots, *more)


def block_type(size):
    return BF16 if D // (2 * size) % 16 == 0 else F32


EXTRA = 16


def unpack_kernel(place_ref, own_ref, col_ref, row_ref, both_ref, wq_ref, wp_ref, bq_ref, bp_ref):
    size = own_ref.shape[0]
    depth, half = D // (2 * size), D // 2
    row, col = place_ref[0], place_ref[1]
    bq_ref[:, D : 2 * D] = jnp.zeros((1, D), F32)
    for ref, r, c in (
        (own_ref, row, col),
        (col_ref, row, 1 - col),
        (row_ref, 1 - row, col),
        (both_ref, 1 - row, 1 - col),
    ):
        at_r, at_c = pl.multiple_of(r * half, half), pl.multiple_of(c * half, half)
        biases = jnp.sum(ref[:, 4 * depth : 4 * depth + EXTRA, :].astype(F32), axis=0)
        bq_ref[:, pl.ds(at_c, half)] = biases[0:1]
        bq_ref[:, pl.ds(pl.multiple_of(2 * D + c * half, half), half)] = biases[1:2]
        bp_ref[:, pl.ds(at_r, half)] = biases[2:3]
        for dp in range(size):
            rows = pl.ds(pl.multiple_of(r * half + dp * depth, depth), depth)
            for part in range(3):
                lanes = pl.ds(pl.multiple_of(part * D + c * half, half), half)
                wq_ref[rows, lanes] = ref[dp, part * depth : (part + 1) * depth, :]
            rows = pl.ds(pl.multiple_of(c * half + dp * depth, depth), depth)
            wp_ref[rows, pl.ds(at_r, half)] = ref[dp, 3 * depth : 4 * depth, :]


def unpacked(place, parts):
    kind = block_type(parts[0].shape[0])
    shapes = [(D, 3 * D), (D, D), (1, 3 * D), (1, D)]
    wq, wp, bq, bp = call(
        unpack_kernel,
        2,
        (1,),
        [whole(part.shape) for part in parts],
        [whole(shape) for shape in shapes],
        [jax.ShapeDtypeStruct(shape, t) for shape, t in zip(shapes, (kind, kind, F32, F32))],
        scalars=1,
    )(place, *[part.astype(kind) for part in parts])
    return wq.astype(BF16), wp.astype(BF16), bq, bp


def normalized(value):
    center = jnp.mean(value, axis=-1, keepdims=True)
    spread = jnp.mean(value * value, axis=-1, keepdims=True) - center * center
    factor = lax.rsqrt(spread + EPS)
    return (value - center) * factor, factor


def norm_back(grad, scaled, factor, gain):
    upper = grad * gain
    return factor * (
        upper
        - jnp.mean(upper, axis=-1, keepdims=True)
        - scaled * jnp.mean(upper * scaled, axis=-1, keepdims=True)
    )


def forward_kernel(
    x_ref,
    wq_ref,
    bq_ref,
    wp_ref,
    bp_ref,
    norm_ref,
    low_ref,
    mid_ref,
    tri_ref,
    att_ref,
    lse_ref,
):
    x = x_ref[0].astype(F32)
    scaled, _ = normalized(x)
    low = (scaled * norm_ref[0:1, :] + norm_ref[1:2, :]).astype(BF16)
    tri = jnp.dot(low, wq_ref[...], preferred_element_type=F32) + bq_ref[...]
    tri_ref[0] = tri.astype(BF16)
    lane = lax.broadcasted_iota(jnp.int32, (PAD, PAIR), 1)
    shut = lax.broadcasted_iota(jnp.int32, (PAD, PAD), 1) >= SEQ
    logs = jnp.zeros((PAD, 128), F32)
    column = lax.broadcasted_iota(jnp.int32, (PAD, 128), 1)
    for pair in range(HEADS // 2):
        at = pair * PAIR
        query = tri_ref[0, :, at : at + PAIR]
        keys = tri_ref[0, :, D + at : D + at + PAIR]
        values = tri_ref[0, :, 2 * D + at : 2 * D + at + PAIR]
        outs = []
        for side in range(2):
            mine = (lane // HEAD_DIM) == side
            scores = contract(jnp.where(mine, query, jnp.zeros_like(query)), keys, 1, 1) * SCALE
            scores = jnp.where(shut, FAR, scores)
            peak = jnp.max(scores, axis=-1, keepdims=True)
            expo = jnp.exp(scores - peak)
            total = jnp.sum(expo, axis=-1, keepdims=True)
            prob = (expo / total).astype(BF16)
            outs.append(jnp.dot(prob, values, preferred_element_type=F32))
            logs = jnp.where(column == 2 * pair + side, peak + jnp.log(total), logs)
        att_ref[0, :, at : at + PAIR] = jnp.where(lane < HEAD_DIM, outs[0], outs[1]).astype(BF16)
    lse_ref[0] = logs
    branch = jnp.dot(att_ref[0], wp_ref[...], preferred_element_type=F32) + bp_ref[...]
    middle = x + branch
    mid_ref[0] = middle
    scaled2, _ = normalized(middle)
    low_ref[0] = (scaled2 * norm_ref[2:3, :] + norm_ref[3:4, :]).astype(BF16)


def attention_forward(x, wq, bq, wp, bp, norms):
    images = x.shape[0]
    return call(
        forward_kernel,
        9,
        (images,),
        [
            stepped((1, PAD, D)),
            whole(wq.shape),
            whole(bq.shape),
            whole(wp.shape),
            whole(bp.shape),
            whole(norms.shape),
        ],
        [
            stepped((1, PAD, D)),
            stepped((1, PAD, D)),
            stepped((1, PAD, 3 * D)),
            stepped((1, PAD, D)),
            stepped((1, PAD, 128)),
        ],
        [
            jax.ShapeDtypeStruct((images, PAD, D), BF16),
            jax.ShapeDtypeStruct((images, PAD, D), F32),
            jax.ShapeDtypeStruct((images, PAD, 3 * D), BF16),
            jax.ShapeDtypeStruct((images, PAD, D), BF16),
            jax.ShapeDtypeStruct((images, PAD, 128), F32),
        ],
    )(x, wq, bq, wp, bp, norms)


def backward_kernel(
    place_ref,
    x_ref,
    mid_ref,
    cot_ref,
    own_ref,
    got_ref,
    tri_ref,
    att_ref,
    lse_ref,
    wq_ref,
    wp_ref,
    norm_ref,
    extra_ref,
    kept_ref,
    sent_ref,
    blocks_ref,
    sums_ref,
    dwq_ref,
    dwp_ref,
    tg_ref,
):
    @pl.when(pl.program_id(0) == 0)
    def _():
        dwq_ref[...] = jnp.zeros_like(dwq_ref)
        dwp_ref[...] = jnp.zeros_like(dwp_ref)
        sums_ref[...] = jnp.zeros_like(sums_ref)

    low_grad = own_ref[0] + got_ref[0].astype(F32)
    scaled2, factor2 = normalized(mid_ref[0])
    sums_ref[2:3, :] += jnp.sum(low_grad * scaled2, axis=0, keepdims=True)
    sums_ref[3:4, :] += jnp.sum(low_grad, axis=0, keepdims=True)
    mid_grad = cot_ref[0].astype(F32) + norm_back(low_grad, scaled2, factor2, norm_ref[2:3, :])
    branch = mid_grad.astype(BF16)
    sums_ref[4:5, :] += jnp.sum(branch.astype(F32), axis=0, keepdims=True)
    dwp_ref[...] += contract(att_ref[0], branch, 0, 0)
    att_grad = contract(branch, wp_ref[...], 1, 1).astype(BF16)
    lane = lax.broadcasted_iota(jnp.int32, (PAD, PAIR), 1)
    shut = lax.broadcasted_iota(jnp.int32, (PAD, PAD), 1) >= SEQ
    for pair in range(HEADS // 2):
        at = pair * PAIR
        query = tri_ref[0, :, at : at + PAIR]
        keys = tri_ref[0, :, D + at : D + at + PAIR]
        values = tri_ref[0, :, 2 * D + at : 2 * D + at + PAIR]
        upstream = att_grad[:, at : at + PAIR]
        query_grads = []
        key_grad = jnp.zeros((PAD, PAIR), F32)
        value_grad = jnp.zeros((PAD, PAIR), F32)
        for side in range(2):
            mine = (lane // HEAD_DIM) == side
            query_one = jnp.where(mine, query, jnp.zeros_like(query))
            grad_one = jnp.where(mine, upstream, jnp.zeros_like(upstream))
            scores = contract(query_one, keys, 1, 1) * SCALE
            scores = jnp.where(shut, FAR, scores)
            head = 2 * pair + side
            prob = jnp.exp(scores - lse_ref[0, :, head : head + 1])
            prob_grad = contract(grad_one, values, 1, 1)
            value_grad += contract(prob.astype(BF16), grad_one, 0, 0)
            inside = jnp.sum(prob * prob_grad, axis=-1, keepdims=True)
            score_grad = (prob * (prob_grad - inside)).astype(BF16)
            query_grads.append(jnp.dot(score_grad, keys, preferred_element_type=F32))
            key_grad += contract(score_grad, query_one, 0, 0)
        query_grad = jnp.where(lane < HEAD_DIM, query_grads[0], query_grads[1])
        tg_ref[:, at : at + PAIR] = (query_grad * SCALE).astype(BF16)
        tg_ref[:, D + at : D + at + PAIR] = (key_grad * SCALE).astype(BF16)
        tg_ref[:, 2 * D + at : 2 * D + at + PAIR] = value_grad.astype(BF16)
    tri_grad = tg_ref[...]
    sums_ref[5:6, :] += jnp.sum(tri_grad[:, :D].astype(F32), axis=0, keepdims=True)
    sums_ref[6:7, :] += jnp.sum(tri_grad[:, 2 * D :].astype(F32), axis=0, keepdims=True)
    scaled, factor = normalized(x_ref[0].astype(F32))
    low = (scaled * norm_ref[0:1, :] + norm_ref[1:2, :]).astype(BF16)
    dwq_ref[...] += contract(low, tri_grad, 0, 0)
    normed_grad = contract(tri_grad, wq_ref[...], 1, 1)
    sums_ref[0:1, :] += jnp.sum(normed_grad * scaled, axis=0, keepdims=True)
    sums_ref[1:2, :] += jnp.sum(normed_grad, axis=0, keepdims=True)
    grad = mid_grad + norm_back(normed_grad, scaled, factor, norm_ref[0:1, :])
    kept_ref[0], sent_ref[0] = feature_halves(place_ref, grad.astype(BF16))

    @pl.when(pl.program_id(0) == pl.num_programs(0) - 1)
    def _():
        size = blocks_ref.shape[1]
        depth, half, kind = D // (2 * size), D // 2, blocks_ref.dtype
        sums = jnp.concatenate([sums_ref[:, :half], sums_ref[:, half:]], 0).astype(kind)
        blocks_ref[:, :, :, 4 * depth : 4 * depth + EXTRA, :] = extra_ref[...]
        for row in range(2):
            for dp in range(size):
                for col in range(2):
                    block = blocks_ref.at[row, dp, col]
                    rows = slice(row * half + dp * depth, row * half + (dp + 1) * depth)
                    for part in range(3):
                        at = part * D + col * half
                        block[part * depth : (part + 1) * depth, :] = dwq_ref[
                            rows, at : at + half
                        ].astype(kind)
                    rows = slice(col * half + dp * depth, col * half + (dp + 1) * depth)
                    block[3 * depth : 4 * depth, :] = dwp_ref[
                        rows, row * half : (row + 1) * half
                    ].astype(kind)
                    block[4 * depth + EXTRA :, :] = sums


def attention_backward(place, x, middle, cot, own, got, tri, att, lse, wq, wp, norms, extra):
    images = x.shape[0]
    size = extra.shape[1]
    blocks = (2, size, 2, 2 * D // size + EXTRA + 16, D // 2)
    return call(
        backward_kernel,
        21,
        (images,),
        [
            stepped((1, PAD, D)),
            stepped((1, PAD, D)),
            stepped((1, PAD, D)),
            stepped((1, PAD, D)),
            stepped((1, PAD, D)),
            stepped((1, PAD, 3 * D)),
            stepped((1, PAD, D)),
            stepped((1, PAD, 128)),
            whole(wq.shape),
            whole(wp.shape),
            whole(norms.shape),
            whole(extra.shape),
        ],
        [
            stepped((1, PAD, D // 2)),
            stepped((1, PAD, D // 2)),
            whole(blocks),
        ],
        [
            jax.ShapeDtypeStruct((images, PAD, D // 2), BF16),
            jax.ShapeDtypeStruct((images, PAD, D // 2), BF16),
            jax.ShapeDtypeStruct(blocks, block_type(size)),
        ],
        scratch=[
            pltpu.VMEM((8, D), F32),
            pltpu.VMEM((D, 3 * D), F32),
            pltpu.VMEM((D, D), F32),
            pltpu.VMEM((PAD, 3 * D), BF16),
        ],
        scalars=1,
    )(place, x, middle, cot, own, got, tri, att, lse, wq, wp, norms, extra)


STEPS = 4


def halves_of(place_ref, features):
    first = pl.multiple_of(place_ref[2] * features, features)
    return first, pl.multiple_of(features - first, features)


def active_grad_kernel(place_ref, grad_ref, own_ref, other_ref, out_ref):
    features = own_ref.shape[2]
    first, second = halves_of(place_ref, features)
    total = contract(grad_ref[:, pl.ds(first, features)], own_ref[0], 1, 1)
    total += contract(grad_ref[:, pl.ds(second, features)], other_ref[0], 1, 1)
    out_ref[...] = total.astype(BF16)


def expert_kernel(place_ref, slots_ref, gact_ref, own_ref, other_ref, be_ref, *refs):
    *before, act_ref, inner_grad_ref, slot_grad_ref, bias_grad_ref = refs

    @pl.when(pl.program_id(0) == 0)
    def _():
        bias_grad_ref[...] = jnp.zeros_like(bias_grad_ref)

    features, hidden = own_ref.shape[1], own_ref.shape[2]
    first, second = halves_of(place_ref, features)
    left, right = slots_ref[:, pl.ds(first, features)], slots_ref[:, pl.ds(second, features)]
    chunk = hidden // 2
    grads = [ref[:, pl.ds(at, features)].astype(F32) for ref in before for at in (first, second)]
    for at in range(0, hidden, chunk):
        inner = (
            jnp.dot(left, own_ref[0, :, at : at + chunk], preferred_element_type=F32)
            + jnp.dot(right, other_ref[0, :, at : at + chunk], preferred_element_type=F32)
            + be_ref[:, at : at + chunk]
        )
        share = 0.5 * (1.0 + lax.erf(inner * ROOT_HALF))
        act_ref[:, at : at + chunk] = (inner * share).astype(BF16)
        slope = share + inner * (DENSITY * jnp.exp(-0.5 * inner * inner))
        grad = (gact_ref[:, at : at + chunk].astype(F32) * slope).astype(BF16)
        inner_grad_ref[:, at : at + chunk] = grad
        bias_grad_ref[:, at : at + chunk] += jnp.sum(grad.astype(F32), axis=0, keepdims=True)
        terms = [contract(grad, ref[0, :, at : at + chunk], 1, 1) for ref in (own_ref, other_ref)]
        grads = [a + b for a, b in zip(grads, terms)] if grads else terms
    slot_grad_ref[:, pl.ds(first, features)] = grads[0].astype(BF16)
    slot_grad_ref[:, pl.ds(second, features)] = grads[1].astype(BF16)


def outer_kernel(place_ref, act0_ref, act1_ref, wc0_ref, wc1_ref, wc2_ref, wc3_ref, bc_ref, out_ref):
    features = wc0_ref.shape[2]
    first, second = halves_of(place_ref, features)
    for at, one, two in ((first, wc0_ref, wc2_ref), (second, wc1_ref, wc3_ref)):
        total = (
            jnp.dot(act0_ref[...], one[0], preferred_element_type=F32)
            + jnp.dot(act1_ref[...], two[0], preferred_element_type=F32)
            + bc_ref[:, pl.ds(at, features)]
        )
        out_ref[:, pl.ds(at, features)] = total.astype(BF16)


def contract_grad_kernel(place_ref, act_ref, grad_ref, out_ref, bias_ref):
    product = contract(act_ref[...], grad_ref[...], 0, 0).astype(BF16)
    half = product.shape[1] // 2
    low, high = product[:, :half], product[:, half:]
    out_ref[0] = jnp.where(place_ref[2] == 0, low, high)
    out_ref[1] = jnp.where(place_ref[2] == 0, high, low)

    @pl.when(pl.program_id(0) == 0)
    def _():
        bias_ref[...] = jnp.sum(grad_ref[...].astype(F32), axis=0, keepdims=True)


def expand_grad_kernel(place_ref, slots_ref, grad_ref, out_ref):
    product = contract(slots_ref[...], grad_ref[...], 0, 0).astype(BF16)
    half = product.shape[0] // 2
    low, high = product[:half], product[half:]
    out_ref[0] = jnp.where(place_ref[2] == 0, low, high)
    out_ref[1] = jnp.where(place_ref[2] == 0, high, low)


def weight_specs(pieces, half):
    shape = (1,) + pieces[0].shape[1:]
    places = [lambda g, place: (place[0], 0, 0), lambda g, place: (place[1], 0, 0)]
    if half:
        places = [lambda g, place: (0, 0, 0), lambda g, place: (1, 0, 0)]
    return [pl.BlockSpec(shape, place) for place in places]


def active_grad(place, grad_slots, wc, half):
    rows, hidden = grad_slots.shape[0], wc[0].shape[1]
    return call(
        active_grad_kernel,
        5,
        (STEPS,),
        [stepped((rows // STEPS, D))] + weight_specs(wc, half),
        stepped((rows // STEPS, hidden)),
        jax.ShapeDtypeStruct((rows, hidden), BF16),
        scalars=1,
    )(place, grad_slots, *wc[2 * half : 2 * half + 2])


def experts_middle(place, slots, gact, we, be, half, *before):
    rows, hidden = gact.shape
    return call(
        expert_kernel,
        11,
        (STEPS,),
        [stepped((rows // STEPS, D)), stepped((rows // STEPS, hidden))]
        + weight_specs(we, half)
        + [whole((1, hidden))]
        + [stepped((rows // STEPS, D))] * len(before),
        [
            stepped((rows // STEPS, hidden)),
            stepped((rows // STEPS, hidden)),
            stepped((rows // STEPS, D)),
            whole((1, hidden)),
        ],
        [
            jax.ShapeDtypeStruct((rows, hidden), BF16),
            jax.ShapeDtypeStruct((rows, hidden), BF16),
            jax.ShapeDtypeStruct((rows, D), BF16),
            jax.ShapeDtypeStruct((1, hidden), F32),
        ],
        scalars=1,
    )(place, slots, gact, *we[2 * half : 2 * half + 2], be[half : half + 1], *before)


def experts_outer(place, acts, wc, bc):
    rows, hidden = acts[0].shape
    return call(
        outer_kernel,
        9,
        (STEPS,),
        [stepped((rows // STEPS, hidden))] * 2
        + weight_specs(wc, 0)
        + weight_specs(wc, 1)
        + [whole(bc.shape)],
        stepped((rows // STEPS, D)),
        jax.ShapeDtypeStruct((rows, D), BF16),
        scalars=1,
    )(place, *acts, *wc, bc)


def contract_grad(place, act, grad_slots):
    rows, hidden = act.shape
    chunk = hidden // 2
    return call(
        contract_grad_kernel,
        5,
        (2,),
        [stepped((rows, chunk), 1), whole(grad_slots.shape)],
        [stepped((2, chunk, D // 2), 1), whole((1, D))],
        [
            jax.ShapeDtypeStruct((2, hidden, D // 2), BF16),
            jax.ShapeDtypeStruct((1, D), F32),
        ],
        scalars=1,
    )(place, act, grad_slots)


def expand_grad(place, slots, inner_grad):
    rows, hidden = inner_grad.shape
    chunk = hidden // 2
    return call(
        expand_grad_kernel,
        5,
        (2,),
        [whole(slots.shape), stepped((rows, chunk), 1)],
        stepped((2, D // 2, chunk), 2),
        jax.ShapeDtypeStruct((2, D // 2, hidden), BF16),
        scalars=1,
    )(place, slots, inner_grad)


def other_core(block, row):
    if block.shape[0] == 1:
        return swap(block, "row")
    return swap(lax.dynamic_slice_in_dim(block, 2 * (1 - row), 2, 0), "row")


def other_chip(block, got, row, col):
    own, other = block, got
    if block.shape[0] > 1:
        own = lax.dynamic_slice_in_dim(own, 2 * row + 1 - col, 1, 0)
        other = lax.dynamic_slice_in_dim(other, 1 - col, 1, 0)
    far = swap(jnp.concatenate([own, other], 0), "col")
    return block, got, far, far


def assemble_kernel(place_ref, *refs):
    for step, ref in enumerate(refs[:4]):

        @pl.when(pl.program_id(0) == step)
        def _(ref=ref):
            refs[4][0] = ref[...].astype(F32)


def grad_block(pieces, row, col):
    shape = pieces[0].shape
    order = jnp.stack([2 * row + col, 2 * row + 1 - col, 2 * (1 - row) + col, 3 - 2 * row - col])
    return call(
        assemble_kernel,
        4,
        (4,),
        [whole(shape)] * 4,
        pl.BlockSpec((1,) + shape, lambda g, order: (order[g], 0, 0)),
        jax.ShapeDtypeStruct((4,) + shape, F32),
        scalars=1,
    )(order, *pieces)


def weight_grad(grad, far, row, col, experts):
    if experts == 1:
        own, near = (grad[side].astype(F32) + far[side].astype(F32) for side in range(2))
        return (own + swap(near.astype(BF16), "row").astype(F32))[None]
    return grad_block((grad[0], far[0], swap(grad[1], "row"), swap(far[1], "row")), row, col)


def as_rows(value, width):
    flat = value.reshape(-1)
    return jnp.pad(flat, (0, round_up(flat.shape[0], width) - flat.shape[0])).reshape(-1, width)


def on_device(
    tokens_in,
    out_cotangent,
    expert_ids,
    gate_values,
    first_gain,
    first_shift,
    second_gain,
    second_shift,
    qkv_weight,
    qkv_bias,
    proj_weight,
    proj_bias,
    expand_weight,
    expand_bias,
    contract_weight,
    contract_bias,
):
    size = lax.axis_size("dp")
    row, col, place = lax.axis_index("row"), lax.axis_index("col"), lax.axis_index("dp")
    local_rows, width = tokens_in.shape[1:]
    group = expert_ids.shape[1]
    images = local_rows // SEQ
    capacity = (group * TOP * 4 + 3 * EXPERTS - 1) // (3 * EXPERTS)
    local_experts = EXPERTS // size
    share = local_experts * capacity // 4
    held_rows = round_up(share, 8)
    peers = 2 * size
    rows = peers * held_rows

    def at_place(array):
        mine = (jnp.arange(size, dtype=jnp.int32) == place).astype(F32)
        return (mine[None, :, None] * array[:, None, :]).reshape(-1, width)

    biases = jnp.concatenate(
        [
            at_place(qkv_bias),
            at_place(proj_bias[None]),
            expand_bias.reshape(-1, width),
            contract_bias.reshape(-1, width),
        ],
        0,
    )
    biases = jnp.pad(biases, ((0, EXTRA - biases.shape[0]), (0, 0)))
    block = jnp.concatenate(
        [qkv_weight.transpose(1, 0, 2).reshape(-1, width), proj_weight, biases.astype(BF16)], 0
    )
    parts = jnp.broadcast_to(block[None], (size,) + block.shape)
    parts = lax.all_to_all(parts, "dp", 0, 0, tiled=True)

    def by_image(array):
        shaped = array.reshape(2, images, SEQ, width)
        return jnp.pad(shaped, ((0, 0), (0, 0), (0, PAD - SEQ), (0, 0)))

    same = row == col

    tokens = jnp.stack([by_image(out_cotangent), by_image(tokens_in)], 1)
    own = chosen(tokens, col)
    got = swap(chosen(tokens, 1 - col), "col")
    kept, sent = either(same, own, got), either(same, got, own)
    got = swap(jnp.stack([sent[0], kept[0], sent[1]]), "row")
    cot = in_order(row, jnp.stack([kept[0], sent[0]]), got[:2], 3)
    x = in_order(row, kept[1], got[2], 2)

    routes = chosen(expert_ids, col)
    gates = chosen(gate_values, col)
    slot = destinations(routes, capacity)
    unit = routes % local_experts * capacity + slot
    home = unit // share
    target = (routes // local_experts * 2 + home % 2) * held_rows + unit % share
    target = jnp.where(home // 2 == row, target, -1)

    def own_first(array, fill):
        shaped = array.reshape(2, images, SEQ, TOP)
        shaped = jnp.pad(
            shaped, ((0, 0), (0, 0), (0, PAD - SEQ), (0, 0)), constant_values=fill
        ).reshape(2, images * PAD, TOP)
        return jnp.where(row == 0, shaped, shaped[::-1])

    target = own_first(target, -1)
    gates = own_first(gates, 0)
    target_rows = target.transpose(0, 2, 1).reshape(2 * TOP, images * PAD)
    gate_rows = gates.transpose(0, 2, 1).reshape(2 * TOP, images * PAD)

    def exchange(slots):
        shaped = slots.reshape(peers, held_rows, D)
        return lax.all_to_all(shaped, ("dp", "col"), 0, 0, tiled=True).reshape(rows, D)

    def flat(array):
        return array.reshape(images * PAD, D)

    if local_experts == 1:
        where = jnp.stack([jnp.zeros_like(row), jnp.zeros_like(row), row])
    else:
        where = jnp.stack([2 * row + col, col, row])
    norms = jnp.stack([first_gain, first_shift, second_gain, second_shift])
    norms = in_order(row, norms, swap(norms, "row"), 1)
    we_got = other_core(expand_weight, row)
    wc_got = other_core(contract_weight, row)
    wc = other_chip(contract_weight, wc_got, row, col)
    we = other_chip(expand_weight, we_got, row, col)
    cot = after(cot, norms)
    grad_slots = dispatch(target_rows, gate_rows, flat(cot[0]), flat(cot[1]), rows, True)
    grad_slots = exchange(grad_slots)

    parts = [parts, swap(parts, "col")]
    parts += [swap(part, "row") for part in parts]
    here = jnp.stack([row, col])
    wq, wp, bq, bp = unpacked(here, parts)
    bias_rows = [part[:, 2 * D // size + 3 :].astype(F32) for part in parts]
    bias_rows = in_order(
        row,
        in_order(col, bias_rows[0][:, None], bias_rows[1][:, None], 1)[:, :, None],
        in_order(col, bias_rows[2][:, None], bias_rows[3][:, None], 1)[:, :, None],
        2,
    )

    def taken(start, like):
        count = like.size // width
        found = bias_rows[:, :, :, start : start + count]
        return found.reshape(found.shape[:3] + like.shape), start + count

    expert = place * local_experts + (2 * row + col) * local_experts // 4
    be, at = taken(0, expand_bias)
    be = chosen(be, expert // (EXPERTS // 2), 2)
    be = chosen(be, expert % (EXPERTS // 2), 2).transpose(1, 0, 2).reshape(2, -1)
    be = either(col == 0, be, be[::-1])
    bc, at = taken(at, contract_bias)
    bc = chosen(bc[:, 0], expert, 2).transpose(1, 0, 2).reshape(1, D)

    low, middle, tri, att, lse = attention_forward(x, wq, bq, wp, bp, norms)
    low = flat(low)
    slots = dispatch(target_rows, gate_rows, low, swap(low, "row"), rows, False)
    slots = exchange(slots)
    gact = active_grad(where, grad_slots, wc, 0)
    slots = after(slots, gact)
    act, inner_grad, slot_grad, be_grad = experts_middle(where, slots, gact, we, be, 0)
    gact = active_grad(where, after(grad_slots, slot_grad), wc, 1)
    act_far, inner_grad_far, slot_grad, be_grad_far = experts_middle(
        where, slots, gact, we, be, 1, slot_grad
    )
    slot_grad = exchange(slot_grad)
    wc_grad_far, bc_grad = contract_grad(where, act_far, grad_slots)
    we_grad_far = expand_grad(where, slots, inner_grad_far)
    wc_far, we_far = swap(wc_grad_far, "col"), swap(we_grad_far, "col")
    wc_grad, _ = contract_grad(where, after(act, we_grad_far), grad_slots)
    we_grad = expand_grad(where, after(slots, we_grad_far), inner_grad)
    outer = experts_outer(where, (act, act_far), wc, bc)
    slot_grad = after(slot_grad, wc_grad, we_grad, outer)
    outer = exchange(after(outer, slot_grad))

    mine = (jnp.arange(EXPERTS, dtype=jnp.int32) == expert).astype(F32)
    be_grad = jnp.stack([be_grad, be_grad_far]).reshape(2, size, -1)
    be_grad = either(col == 0, be_grad, be_grad[::-1]).transpose(1, 0, 2)
    be_grad = mine.reshape(2, 1, 1, -1, 1) * be_grad[None, :, :, None, :]
    bc_grad = mine.reshape(1, 1, 1, -1, 1) * bc_grad.reshape(2, size, 1, 1, -1)
    bc_grad = jnp.broadcast_to(bc_grad, (2, size, 2) + bc_grad.shape[3:])
    extra = jnp.concatenate(
        [
            be_grad.reshape(2, size, 2, -1, width),
            bc_grad.reshape(2, size, 2, -1, width),
        ],
        3,
    )
    short = EXTRA - extra.shape[3]
    extra = jnp.pad(extra, ((0, 0),) * 3 + ((0, short), (0, 0))).astype(block_type(size))

    def to_image(array):
        return array.reshape(images, PAD, -1)

    got = swap(combine(here, 1, target, gates, slot_grad, BF16), "row")
    own = after(combine(here, 0, target, gates, slot_grad, F32), wc_far)
    grad_kept, grad_sent, blocks = attention_backward(
        here, x, middle, cot[0], to_image(own), to_image(got), tri, att, lse, wq, wp, norms, extra
    )
    blocks = after(blocks.astype(BF16), we_far)
    kept = chosen(blocks, row).astype(F32)
    blocks = (kept + swap(chosen(blocks, 1 - row), "row").astype(F32)).astype(BF16)
    blocks = after(blocks.reshape((peers,) + blocks.shape[2:]), outer)
    reduced = lax.all_to_all(blocks, ("dp", "col"), 0, 0, tiled=True)
    reduced = jnp.sum(reduced.astype(F32), axis=0)
    wc_grad = weight_grad(wc_grad, wc_far, row, col, local_experts)
    we_grad = weight_grad(we_grad, we_far, row, col, local_experts)

    def to_tokens(kept, sent):
        got = swap(sent, "row")
        own, other = either(same, kept, got), either(same, got, kept)
        return own, swap(other, "col")

    def placed(own, other, dtype):
        both = in_order(col, own[None].astype(F32), other[None].astype(F32), 0)[:, :, :SEQ]
        return both.reshape(2, local_rows, width).astype(dtype)

    input_grad = placed(*to_tokens(grad_kept, grad_sent), F32)

    def out_half(half):
        kept, sent = combine(here, half, target, gates, outer, middle=flat(middle))
        return to_image(kept.astype(F32) + swap(sent, "row").astype(F32))

    leaves = either(same, 1, 0)
    other = swap(out_half(leaves).astype(BF16), "col")
    layer_out = placed(out_half(1 - leaves), other, BF16)

    depth = qkv_weight.shape[0]
    out_wq = reduced[: 3 * depth].reshape(3, depth, width).transpose(1, 0, 2)
    out_wp = reduced[3 * depth : 4 * depth]
    be_rows = expand_bias.size // width
    out_be = reduced[4 * depth : 4 * depth + be_rows].reshape(expand_bias.shape)
    bc_rows = contract_bias.size // width
    out_bc = reduced[4 * depth + be_rows : 4 * depth + be_rows + bc_rows]
    out_bc = out_bc.reshape(contract_bias.shape)
    sums = reduced[4 * depth + EXTRA :].reshape(2, 8, width)
    norm_total = chosen(sums, row)
    out_bp = chosen(norm_total[4].reshape(size, -1), place)
    out_bq = chosen(chosen(sums, col)[5:7].reshape(2, size, -1), place, 1)
    return (
        layer_out,
        input_grad,
        norm_total[0],
        norm_total[1],
        norm_total[2],
        norm_total[3],
        out_wq,
        out_bq,
        out_wp,
        out_bp,
        we_grad,
        out_be,
        wc_grad,
        out_bc,
    )


def solution(mesh):
    return jax.shard_map(
        on_device,
        mesh=mesh,
        in_specs=(
            P(None, ("dp", "col"), "row"),
            P(None, ("dp", "col"), "row"),
            P(None, "dp", None),
            P(None, "dp", None),
            P("row"),
            P("row"),
            P("row"),
            P("row"),
            P(("row", "dp"), None, "col"),
            P(None, ("col", "dp")),
            P(("col", "dp"), "row"),
            P(("row", "dp")),
            P("dp", "row", "col"),
            P("row", ("col", "dp")),
            P("dp", "col", "row"),
            P(None, ("row", "dp")),
        ),
        out_specs=(
            P(None, ("dp", "col"), "row"),
            P(None, ("dp", "col"), "row"),
            P("row"),
            P("row"),
            P("row"),
            P("row"),
            P(("row", "dp"), None, "col"),
            P(None, ("col", "dp")),
            P(("col", "dp"), "row"),
            P(("row", "dp")),
            P("dp", "row", "col"),
            P("row", ("col", "dp")),
            P("dp", "col", "row"),
            P(None, ("row", "dp")),
        ),
        check_vma=False,
    )
```

```python
import functools

import jax
import jax.numpy as jnp
from jax import lax
from jax.experimental import pallas as pl
from jax.experimental.pallas import tpu as pltpu
from jax.sharding import PartitionSpec as P

D = 512
HEADS = 8
EXPERTS = 32
TOP = 2
SEQ = 197
HEAD_DIM = D // HEADS
PAIR = 2 * HEAD_DIM
PAD = 208

EPS = 1e-06
HIGH = lax.Precision.HIGHEST
ROOT_HALF = 0.7071067811865476
DENSITY = 0.3989422804014327
SCALE = HEAD_DIM ** (-0.5)
FAR = -1e30
MIB = 1 << 20

BF16 = jnp.bfloat16
F32 = jnp.float32


def round_up(value, unit):
    return (value + unit - 1) // unit * unit


def swap(value, axis, bit=1):
    size = lax.axis_size(axis)
    return lax.ppermute(value, axis, [(place, place ^ bit) for place in range(size)])


def either(first, when_true, when_false):
    return jnp.where(first, when_true, when_false)


def in_order(index, own, other, axis):
    return jnp.where(
        index == 0,
        jnp.concatenate([own, other], axis),
        jnp.concatenate([other, own], axis),
    )


def chosen(array, index, axis=0):
    return lax.dynamic_index_in_dim(array, index, axis, keepdims=False)


def contract(left, right, left_dim, right_dim):
    return lax.dot_general(
        left, right, (((left_dim,), (right_dim,)), ((), ())), preferred_element_type=F32
    )


def after(value, *others):
    return lax.optimization_barrier((value,) + others)[0]


def call(
    kernel, micros, grid, in_specs, out_specs, out_shape, scratch=(), limit=48, scalars=0
):
    return pl.pallas_call(
        kernel,
        grid_spec=pltpu.PrefetchScalarGridSpec(
            num_scalar_prefetch=scalars,
            grid=grid,
            in_specs=in_specs,
            out_specs=out_specs,
            scratch_shapes=list(scratch),
        ),
        out_shape=out_shape,
        cost_estimate=pl.CostEstimate(
            flops=int(micros * 1e9), bytes_accessed=int(micros * 2e6), transcendentals=0
        ),
        compiler_params=pltpu.CompilerParams(
            dimension_semantics=("arbitrary",) * len(grid), vmem_limit_bytes=limit * MIB
        ),
    )


def whole(shape):
    return pl.BlockSpec(shape, lambda *_: (0,) * len(shape))


def stepped(shape, axis=0):
    return pl.BlockSpec(
        shape, lambda g, *_: tuple(g if place == axis else 0 for place in range(len(shape)))
    )


def destinations(routes, capacity):
    labels = jnp.arange(EXPERTS, dtype=jnp.int32)
    named = (routes[:, :, None] == labels).astype(F32)
    count = routes.shape[0]
    place = jnp.arange(count, dtype=jnp.int32)
    earlier = (place[None, :] < place[:, None]).astype(BF16)
    before = jnp.dot(earlier, named.sum(axis=1).astype(BF16), preferred_element_type=F32)
    return jnp.sum(before[:, None, :] * named, axis=2).astype(jnp.int32)


def dispatch_kernel(gated, target_ref, gate_ref, own_ref, other_ref, out_ref):
    rows = out_ref.shape[0]
    count = own_ref.shape[0]
    place = lax.broadcasted_iota(jnp.int32, (rows, count), 0) + pl.program_id(0) * rows
    total = None
    for half, tokens in ((0, own_ref), (1, other_ref)):
        first = place == target_ref[2 * half : 2 * half + 1, :]
        second = place == target_ref[2 * half + 1 : 2 * half + 2, :]
        if gated:
            weight = jnp.where(
                first,
                gate_ref[2 * half : 2 * half + 1, :],
                jnp.where(second, gate_ref[2 * half + 1 : 2 * half + 2, :], 0.0),
            )
        else:
            weight = jnp.where(first | second, 1.0, 0.0)
        term = jnp.dot(weight.astype(BF16), tokens[...], preferred_element_type=F32)
        total = term if total is None else total + term
    out_ref[...] = total.astype(BF16)


def dispatch(target_rows, gate_rows, own, other, rows, gated):
    steps = 4
    return call(
        functools.partial(dispatch_kernel, gated),
        5,
        (steps,),
        [whole(target_rows.shape), whole(gate_rows.shape), whole(own.shape), whole(other.shape)],
        stepped((rows // steps, D)),
        pltpu.HBM((rows, D), BF16),
    )(target_rows, gate_rows, own, other)


def combined(target_ref, gate_ref, slots_ref):
    count, rows = target_ref.shape[1], slots_ref.shape[0]
    place = lax.broadcasted_iota(jnp.int32, (count, rows), 1)
    first = place == target_ref[0, :, 0:1]
    second = place == target_ref[0, :, 1:2]
    weight = jnp.where(first, gate_ref[0, :, 0:1], jnp.where(second, gate_ref[0, :, 1:2], 0.0))
    return jnp.dot(weight.astype(BF16), slots_ref[...], preferred_element_type=F32)


def selection_kernel(target_ref, out_ref):
    place = lax.broadcasted_iota(jnp.int32, out_ref.shape[1:], 1)
    first = place == target_ref[0, :, 0:1]
    second = place == target_ref[0, :, 1:2]
    out_ref[0] = jnp.where(first | second, 1.0, 0.0).astype(BF16)


def selection(target, rows):
    steps = 4
    count = 2 * target.shape[1] // steps
    return call(
        selection_kernel,
        8,
        (steps,),
        [pl.BlockSpec((1, count, TOP), lambda g: (g // 2, g % 2, 0))],
        pl.BlockSpec((1, count, rows), lambda g: (g // 2, g % 2, 0)),
        jax.ShapeDtypeStruct((2, target.shape[1], rows), BF16),
    )(target)


def select_kernel(chosen_ref, slots_ref, out_ref):
    out = jnp.dot(chosen_ref[0], slots_ref[...], preferred_element_type=F32)
    out_ref[...] = out.astype(out_ref.dtype)


def selected(selection, half, slots, dtype):
    steps = 2
    rows = selection.shape[1] // steps
    return call(
        select_kernel,
        3,
        (steps,),
        [
            pl.BlockSpec((1, rows, selection.shape[2]), lambda g: (half, g, 0)),
            whole(slots.shape),
        ],
        stepped((rows, D)),
        jax.ShapeDtypeStruct((selection.shape[1], D), dtype),
    )(selection, slots)


def combine_out_kernel(
    place_ref, target_ref, gate_ref, slots_ref, middle_ref, kept_ref, sent_ref
):
    out = combined(target_ref, gate_ref, slots_ref)
    out = jnp.where(place_ref[1] == 0, out + middle_ref[...], out)
    kept_ref[...], sent_ref[...] = feature_halves(place_ref, out.astype(BF16))


def feature_halves(place_ref, value):
    half = value.shape[-1] // 2
    low, high = value[..., :half], value[..., half:]
    first = place_ref[0] == 0
    return jnp.where(first, low, high), jnp.where(first, high, low)


def combine(place, half, target, gates, slots, middle):
    steps = 2
    count = target.shape[1]
    column = pl.BlockSpec((1, count // steps, TOP), lambda g, place: (place[1], g, 0))
    return call(
        combine_out_kernel,
        5,
        (steps,),
        [column, column, whole(slots.shape), stepped((count // steps, D))],
        [stepped((count // steps, D // 2))] * 2,
        [jax.ShapeDtypeStruct((count, D // 2), BF16)] * 2,
        scalars=1,
    )(jnp.stack([place[0], half]), target, gates, slots, middle)


def block_type(size):
    return BF16 if D // (2 * size) % 16 == 0 else F32


EXTRA = 16


def unpack_kernel(place_ref, own_ref, other_ref, wq_ref, wp_ref, bq_ref, bp_ref):
    size = own_ref.shape[0]
    depth, half = D // (2 * size), D // 2
    row = place_ref[0]
    bq_ref[:, D : 2 * D] = jnp.zeros((1, D), F32)
    for ref, r in ((own_ref, row), (other_ref, 1 - row)):
        at_r = pl.multiple_of(r * half, half)
        for c in range(2):
            at_c = c * half
            biases = jnp.sum(ref[:, c, 4 * depth : 4 * depth + EXTRA, :].astype(F32), axis=0)
            bq_ref[:, at_c : at_c + half] = biases[0:1]
            bq_ref[:, 2 * D + at_c : 2 * D + at_c + half] = biases[1:2]
            bp_ref[:, pl.ds(at_r, half)] = biases[2:3]
            for dp in range(size):
                rows = pl.ds(pl.multiple_of(r * half + dp * depth, depth), depth)
                for part in range(3):
                    at = part * D + at_c
                    wq_ref[rows, at : at + half] = ref[dp, c, part * depth : (part + 1) * depth, :]
                rows = slice(at_c + dp * depth, at_c + (dp + 1) * depth)
                wp_ref[rows, pl.ds(at_r, half)] = ref[dp, c, 3 * depth : 4 * depth, :]


def unpacked(place, parts):
    kind = block_type(parts[0].shape[0])
    shapes = [(D, 3 * D), (D, D), (1, 3 * D), (1, D)]
    wq, wp, bq, bp = call(
        unpack_kernel,
        2,
        (1,),
        [whole(part.shape) for part in parts],
        [whole(shape) for shape in shapes],
        [jax.ShapeDtypeStruct(shape, t) for shape, t in zip(shapes, (kind, kind, F32, F32))],
        scalars=1,
    )(place, *[part.astype(kind) for part in parts])
    return wq.astype(BF16), wp.astype(BF16), bq, bp


def normalized(value):
    center = jnp.mean(value, axis=-1, keepdims=True)
    spread = jnp.mean(value * value, axis=-1, keepdims=True) - center * center
    factor = lax.rsqrt(spread + EPS)
    return (value - center) * factor, factor


def norm_back(grad, scaled, factor, gain):
    upper = grad * gain
    return factor * (
        upper
        - jnp.mean(upper, axis=-1, keepdims=True)
        - scaled * jnp.mean(upper * scaled, axis=-1, keepdims=True)
    )


def forward_kernel(
    x_ref,
    wq_ref,
    bq_ref,
    wp_ref,
    bp_ref,
    norm_ref,
    low_ref,
    mid_ref,
    tri_ref,
    att_ref,
    lse_ref,
):
    x = x_ref[0].astype(F32)
    scaled, _ = normalized(x)
    low = (scaled * norm_ref[0:1, :] + norm_ref[1:2, :]).astype(BF16)
    tri = jnp.dot(low, wq_ref[...], preferred_element_type=F32) + bq_ref[...]
    tri_ref[0] = tri.astype(BF16)
    lane = lax.broadcasted_iota(jnp.int32, (PAD, PAIR), 1)
    shut = lax.broadcasted_iota(jnp.int32, (PAD, PAD), 1) >= SEQ
    logs = jnp.zeros((PAD, 128), F32)
    column = lax.broadcasted_iota(jnp.int32, (PAD, 128), 1)
    for pair in range(HEADS // 2):
        at = pair * PAIR
        query = tri_ref[0, :, at : at + PAIR]
        keys = tri_ref[0, :, D + at : D + at + PAIR]
        values = tri_ref[0, :, 2 * D + at : 2 * D + at + PAIR]
        outs = []
        for side in range(2):
            mine = (lane // HEAD_DIM) == side
            scores = contract(jnp.where(mine, query, jnp.zeros_like(query)), keys, 1, 1) * SCALE
            scores = jnp.where(shut, FAR, scores)
            peak = jnp.max(scores, axis=-1, keepdims=True)
            expo = jnp.exp(scores - peak)
            total = jnp.sum(expo, axis=-1, keepdims=True)
            prob = (expo / total).astype(BF16)
            outs.append(jnp.dot(prob, values, preferred_element_type=F32))
            logs = jnp.where(column == 2 * pair + side, peak + jnp.log(total), logs)
        att_ref[0, :, at : at + PAIR] = jnp.where(lane < HEAD_DIM, outs[0], outs[1]).astype(BF16)
    lse_ref[0] = logs
    branch = jnp.dot(att_ref[0], wp_ref[...], preferred_element_type=F32) + bp_ref[...]
    middle = x + branch
    mid_ref[0] = middle
    scaled2, _ = normalized(middle)
    low_ref[0] = (scaled2 * norm_ref[2:3, :] + norm_ref[3:4, :]).astype(BF16)


def attention_forward(x, wq, bq, wp, bp, norms):
    images = x.shape[0]
    return call(
        forward_kernel,
        9,
        (images,),
        [
            stepped((1, PAD, D)),
            whole(wq.shape),
            whole(bq.shape),
            whole(wp.shape),
            whole(bp.shape),
            whole(norms.shape),
        ],
        [
            stepped((1, PAD, D)),
            stepped((1, PAD, D)),
            stepped((1, PAD, 3 * D)),
            stepped((1, PAD, D)),
            stepped((1, PAD, 128)),
        ],
        [
            jax.ShapeDtypeStruct((images, PAD, D), BF16),
            jax.ShapeDtypeStruct((images, PAD, D), F32),
            jax.ShapeDtypeStruct((images, PAD, 3 * D), BF16),
            jax.ShapeDtypeStruct((images, PAD, D), BF16),
            jax.ShapeDtypeStruct((images, PAD, 128), F32),
        ],
    )(x, wq, bq, wp, bp, norms)


def backward_kernel(
    place_ref,
    x_ref,
    mid_ref,
    cot_ref,
    own_ref,
    got_ref,
    tri_ref,
    att_ref,
    lse_ref,
    wq_ref,
    wp_ref,
    norm_ref,
    extra_ref,
    kept_ref,
    sent_ref,
    blocks_ref,
    sums_ref,
    dwq_ref,
    dwp_ref,
    tg_ref,
):
    @pl.when(pl.program_id(0) == 0)
    def _():
        dwq_ref[...] = jnp.zeros_like(dwq_ref)
        dwp_ref[...] = jnp.zeros_like(dwp_ref)
        sums_ref[...] = jnp.zeros_like(sums_ref)

    low_grad = own_ref[0] + got_ref[0].astype(F32)
    scaled2, factor2 = normalized(mid_ref[0])
    sums_ref[2:3, :] += jnp.sum(low_grad * scaled2, axis=0, keepdims=True)
    sums_ref[3:4, :] += jnp.sum(low_grad, axis=0, keepdims=True)
    mid_grad = cot_ref[0].astype(F32) + norm_back(low_grad, scaled2, factor2, norm_ref[2:3, :])
    branch = mid_grad.astype(BF16)
    sums_ref[4:5, :] += jnp.sum(branch.astype(F32), axis=0, keepdims=True)
    dwp_ref[...] += contract(att_ref[0], branch, 0, 0)
    att_grad = contract(branch, wp_ref[...], 1, 1).astype(BF16)
    lane = lax.broadcasted_iota(jnp.int32, (PAD, PAIR), 1)
    shut = lax.broadcasted_iota(jnp.int32, (PAD, PAD), 1) >= SEQ
    for pair in range(HEADS // 2):
        at = pair * PAIR
        query = tri_ref[0, :, at : at + PAIR]
        keys = tri_ref[0, :, D + at : D + at + PAIR]
        values = tri_ref[0, :, 2 * D + at : 2 * D + at + PAIR]
        upstream = att_grad[:, at : at + PAIR]
        query_grads = []
        key_grad = jnp.zeros((PAD, PAIR), F32)
        value_grad = jnp.zeros((PAD, PAIR), F32)
        for side in range(2):
            mine = (lane // HEAD_DIM) == side
            query_one = jnp.where(mine, query, jnp.zeros_like(query))
            grad_one = jnp.where(mine, upstream, jnp.zeros_like(upstream))
            scores = contract(query_one, keys, 1, 1) * SCALE
            scores = jnp.where(shut, FAR, scores)
            head = 2 * pair + side
            prob = jnp.exp(scores - lse_ref[0, :, head : head + 1])
            prob_grad = contract(grad_one, values, 1, 1)
            value_grad += contract(prob.astype(BF16), grad_one, 0, 0)
            inside = jnp.sum(prob * prob_grad, axis=-1, keepdims=True)
            score_grad = (prob * (prob_grad - inside)).astype(BF16)
            query_grads.append(jnp.dot(score_grad, keys, preferred_element_type=F32))
            key_grad += contract(score_grad, query_one, 0, 0)
        query_grad = jnp.where(lane < HEAD_DIM, query_grads[0], query_grads[1])
        tg_ref[:, at : at + PAIR] = (query_grad * SCALE).astype(BF16)
        tg_ref[:, D + at : D + at + PAIR] = (key_grad * SCALE).astype(BF16)
        tg_ref[:, 2 * D + at : 2 * D + at + PAIR] = value_grad.astype(BF16)
    tri_grad = tg_ref[...]
    sums_ref[5:6, :] += jnp.sum(tri_grad[:, :D].astype(F32), axis=0, keepdims=True)
    sums_ref[6:7, :] += jnp.sum(tri_grad[:, 2 * D :].astype(F32), axis=0, keepdims=True)
    scaled, factor = normalized(x_ref[0].astype(F32))
    low = (scaled * norm_ref[0:1, :] + norm_ref[1:2, :]).astype(BF16)
    dwq_ref[...] += contract(low, tri_grad, 0, 0)
    normed_grad = contract(tri_grad, wq_ref[...], 1, 1)
    sums_ref[0:1, :] += jnp.sum(normed_grad * scaled, axis=0, keepdims=True)
    sums_ref[1:2, :] += jnp.sum(normed_grad, axis=0, keepdims=True)
    grad = mid_grad + norm_back(normed_grad, scaled, factor, norm_ref[0:1, :])
    kept_ref[0], sent_ref[0] = feature_halves(place_ref, grad.astype(BF16))

    @pl.when(pl.program_id(0) == pl.num_programs(0) - 1)
    def _():
        size = blocks_ref.shape[1]
        depth, half, kind = D // (2 * size), D // 2, blocks_ref.dtype
        sums = jnp.concatenate([sums_ref[:, :half], sums_ref[:, half:]], 0).astype(kind)
        blocks_ref[:, :, :, 4 * depth : 4 * depth + EXTRA, :] = extra_ref[...]
        for row in range(2):
            for dp in range(size):
                for col in range(2):
                    block = blocks_ref.at[row, dp, col]
                    rows = slice(row * half + dp * depth, row * half + (dp + 1) * depth)
                    for part in range(3):
                        at = part * D + col * half
                        block[part * depth : (part + 1) * depth, :] = dwq_ref[
                            rows, at : at + half
                        ].astype(kind)
                    rows = slice(col * half + dp * depth, col * half + (dp + 1) * depth)
                    block[3 * depth : 4 * depth, :] = dwp_ref[
                        rows, row * half : (row + 1) * half
                    ].astype(kind)
                    block[4 * depth + EXTRA :, :] = sums


def attention_backward(place, x, middle, cot, own, got, tri, att, lse, wq, wp, norms, extra):
    images = x.shape[0]
    size = extra.shape[1]
    blocks = (2, size, 2, 2 * D // size + EXTRA + 16, D // 2)
    return call(
        backward_kernel,
        21,
        (images,),
        [
            stepped((1, PAD, D)),
            stepped((1, PAD, D)),
            stepped((1, PAD, D)),
            stepped((1, PAD, D)),
            stepped((1, PAD, D)),
            stepped((1, PAD, 3 * D)),
            stepped((1, PAD, D)),
            stepped((1, PAD, 128)),
            whole(wq.shape),
            whole(wp.shape),
            whole(norms.shape),
            whole(extra.shape),
        ],
        [
            stepped((1, PAD, D // 2)),
            stepped((1, PAD, D // 2)),
            whole(blocks),
        ],
        [
            jax.ShapeDtypeStruct((images, PAD, D // 2), BF16),
            jax.ShapeDtypeStruct((images, PAD, D // 2), BF16),
            jax.ShapeDtypeStruct(blocks, block_type(size)),
        ],
        scratch=[
            pltpu.VMEM((8, D), F32),
            pltpu.VMEM((D, 3 * D), F32),
            pltpu.VMEM((D, D), F32),
            pltpu.VMEM((PAD, 3 * D), BF16),
        ],
        scalars=1,
    )(place, x, middle, cot, own, got, tri, att, lse, wq, wp, norms, extra)


STEPS = 4


def own_first(place_ref, value):
    half = value.shape[-1] // 2
    low, high = value[..., :half], value[..., half:]
    first = place_ref[2] == 0
    return jnp.concatenate([jnp.where(first, low, high), jnp.where(first, high, low)], -1)


def active_grad_kernel(place_ref, grad_ref, own_ref, other_ref, out_ref):
    weight = jnp.concatenate([own_ref[0], other_ref[0]], 1)
    out_ref[...] = contract(own_first(place_ref, grad_ref[...]), weight, 1, 1).astype(BF16)


def expert_kernel(place_ref, slots_ref, gact_ref, own_ref, other_ref, be_ref, *refs):
    *before, act_ref, inner_grad_ref, slot_grad_ref = refs
    weight = jnp.concatenate([own_ref[0], other_ref[0]], 0)
    tokens = own_first(place_ref, slots_ref[...])
    inner = jnp.dot(tokens, weight, preferred_element_type=F32) + be_ref[...]
    share = 0.5 * (1.0 + lax.erf(inner * ROOT_HALF))
    act_ref[...] = (inner * share).astype(BF16)
    slope = share + inner * (DENSITY * jnp.exp(-0.5 * inner * inner))
    grad = (gact_ref[...].astype(F32) * slope).astype(BF16)
    inner_grad_ref[...] = grad
    total = own_first(place_ref, contract(grad, weight, 1, 1))
    for ref in before:
        total += ref[...].astype(F32)
    slot_grad_ref[...] = total.astype(BF16)


def outer_kernel(place_ref, act0_ref, act1_ref, wc0_ref, wc1_ref, wc2_ref, wc3_ref, bc_ref, out_ref):
    total = jnp.dot(
        act0_ref[...], jnp.concatenate([wc0_ref[0], wc1_ref[0]], 1), preferred_element_type=F32
    )
    total += jnp.dot(
        act1_ref[...], jnp.concatenate([wc2_ref[0], wc3_ref[0]], 1), preferred_element_type=F32
    )
    out_ref[...] = (own_first(place_ref, total) + bc_ref[...]).astype(BF16)


def contract_grad_kernel(place_ref, act_ref, grad_ref, out_ref, bias_ref):
    product = contract(act_ref[...], grad_ref[...], 0, 0).astype(BF16)
    half = product.shape[1] // 2
    low, high = product[:, :half], product[:, half:]
    out_ref[0] = jnp.where(place_ref[2] == 0, low, high)
    out_ref[1] = jnp.where(place_ref[2] == 0, high, low)

    @pl.when(pl.program_id(0) == 0)
    def _():
        bias_ref[...] = jnp.sum(grad_ref[...].astype(F32), axis=0, keepdims=True)


def expand_grad_kernel(place_ref, slots_ref, grad_ref, out_ref, bias_ref):
    product = contract(slots_ref[...], grad_ref[...], 0, 0).astype(BF16)
    half = product.shape[0] // 2
    low, high = product[:half], product[half:]
    out_ref[0] = jnp.where(place_ref[2] == 0, low, high)
    out_ref[1] = jnp.where(place_ref[2] == 0, high, low)
    bias_ref[...] = jnp.sum(grad_ref[...].astype(F32), axis=0, keepdims=True)


def weight_specs(pieces, half):
    shape = (1,) + pieces[0].shape[1:]
    places = [lambda g, place: (place[0], 0, 0), lambda g, place: (place[1], 0, 0)]
    if half:
        places = [lambda g, place: (0, 0, 0)] * 2
    return [pl.BlockSpec(shape, place) for place in places]


def active_grad(place, grad_slots, wc, half):
    rows, hidden = grad_slots.shape[0], wc[0].shape[1]
    return call(
        active_grad_kernel,
        5,
        (STEPS,),
        [stepped((rows // STEPS, D))] + weight_specs(wc, half),
        stepped((rows // STEPS, hidden)),
        jax.ShapeDtypeStruct((rows, hidden), BF16),
        scalars=1,
    )(place, grad_slots, *wc[2 * half : 2 * half + 2])


def experts_middle(place, slots, gact, we, be, half, *before):
    rows, hidden = gact.shape
    return call(
        expert_kernel,
        11,
        (STEPS,),
        [stepped((rows // STEPS, D)), stepped((rows // STEPS, hidden))]
        + weight_specs(we, half)
        + [whole((1, hidden))]
        + [stepped((rows // STEPS, D))] * len(before),
        [
            stepped((rows // STEPS, hidden)),
            stepped((rows // STEPS, hidden)),
            stepped((rows // STEPS, D)),
        ],
        [
            jax.ShapeDtypeStruct((rows, hidden), BF16),
            jax.ShapeDtypeStruct((rows, hidden), BF16),
            pltpu.HBM((rows, D), BF16),
        ],
        scalars=1,
    )(place, slots, gact, *we[2 * half : 2 * half + 2], be[half : half + 1], *before)


def experts_outer(place, acts, wc, bc):
    rows, hidden = acts[0].shape
    return call(
        outer_kernel,
        9,
        (STEPS,),
        [stepped((rows // STEPS, hidden))] * 2
        + weight_specs(wc, 0)
        + weight_specs(wc, 1)
        + [whole(bc.shape)],
        stepped((rows // STEPS, D)),
        jax.ShapeDtypeStruct((rows, D), BF16),
        scalars=1,
    )(place, *acts, *wc, bc)


def contract_grad(place, act, grad_slots):
    rows, hidden = act.shape
    chunk = hidden // 2
    return call(
        contract_grad_kernel,
        5,
        (2,),
        [stepped((rows, chunk), 1), whole(grad_slots.shape)],
        [stepped((2, chunk, D // 2), 1), whole((1, D))],
        [
            jax.ShapeDtypeStruct((2, hidden, D // 2), BF16),
            jax.ShapeDtypeStruct((1, D), F32),
        ],
        scalars=1,
    )(place, act, grad_slots)


def expand_grad(place, slots, inner_grad):
    rows, hidden = inner_grad.shape
    chunk = hidden // 2
    return call(
        expand_grad_kernel,
        5,
        (2,),
        [whole(slots.shape), stepped((rows, chunk), 1)],
        [stepped((2, D // 2, chunk), 2), stepped((1, chunk), 1)],
        [
            jax.ShapeDtypeStruct((2, D // 2, hidden), BF16),
            jax.ShapeDtypeStruct((1, hidden), F32),
        ],
        scalars=1,
    )(place, slots, inner_grad)


def other_core(block, row):
    if block.shape[0] == 1:
        return swap(block, "row")
    return swap(lax.dynamic_slice_in_dim(block, 2 * (1 - row), 2, 0), "row")


def other_chip(block, got, row, col, earlier=()):
    own, other = block, got
    if block.shape[0] > 1:
        own = lax.dynamic_slice_in_dim(own, 2 * row + 1 - col, 1, 0)
        other = lax.dynamic_slice_in_dim(other, 1 - col, 1, 0)
    own = swap(own, "col")
    return block, got, own, swap(after(other, earlier), "col")


def assemble_kernel(place_ref, *refs):
    for step, ref in enumerate(refs[:4]):

        @pl.when(pl.program_id(0) == step)
        def _(ref=ref):
            refs[4][0] = ref[...].astype(F32)


def grad_block(pieces, row, col):
    shape = pieces[0].shape
    order = jnp.stack([2 * row + col, 2 * row + 1 - col, 2 * (1 - row) + col, 3 - 2 * row - col])
    return call(
        assemble_kernel,
        4,
        (4,),
        [whole(shape)] * 4,
        pl.BlockSpec((1,) + shape, lambda g, order: (order[g], 0, 0)),
        jax.ShapeDtypeStruct((4,) + shape, F32),
        scalars=1,
    )(order, *pieces)


def weight_grad(grad, far, row, col, experts):
    if experts == 1:
        own, near = (grad[side].astype(F32) + far[side].astype(F32) for side in range(2))
        return (own + swap(near.astype(BF16), "row").astype(F32))[None]
    return grad_block((grad[0], far[0], swap(grad[1], "row"), swap(far[1], "row")), row, col)


def as_rows(value, width):
    flat = value.reshape(-1)
    return jnp.pad(flat, (0, round_up(flat.shape[0], width) - flat.shape[0])).reshape(-1, width)


def on_device(
    tokens_in,
    out_cotangent,
    expert_ids,
    gate_values,
    first_gain,
    first_shift,
    second_gain,
    second_shift,
    qkv_weight,
    qkv_bias,
    proj_weight,
    proj_bias,
    expand_weight,
    expand_bias,
    contract_weight,
    contract_bias,
):
    size = lax.axis_size("dp")
    row, col, place = lax.axis_index("row"), lax.axis_index("col"), lax.axis_index("dp")
    local_rows, width = tokens_in.shape[1:]
    group = expert_ids.shape[1]
    images = local_rows // SEQ
    capacity = (group * TOP * 4 + 3 * EXPERTS - 1) // (3 * EXPERTS)
    local_experts = EXPERTS // size
    share = local_experts * capacity // 4
    held_rows = round_up(share, 8)
    peers = 2 * size
    rows = peers * held_rows

    def at_place(array):
        mine = (jnp.arange(size, dtype=jnp.int32) == place).astype(F32)
        return (mine[None, :, None] * array[:, None, :]).reshape(-1, width)

    biases = jnp.concatenate(
        [
            at_place(qkv_bias),
            at_place(proj_bias[None]),
            expand_bias.reshape(-1, width),
            contract_bias.reshape(-1, width),
        ],
        0,
    )
    biases = jnp.pad(biases, ((0, EXTRA - biases.shape[0]), (0, 0)))
    block = jnp.concatenate(
        [qkv_weight.transpose(1, 0, 2).reshape(-1, width), proj_weight, biases.astype(BF16)], 0
    )
    parts = jnp.broadcast_to(block[None], (peers,) + block.shape)
    parts = lax.all_to_all(parts, ("dp", "col"), 0, 0, tiled=True)
    parts = parts.reshape((size, 2) + block.shape)

    def by_image(array):
        shaped = array.reshape(2, images, SEQ, width)
        return jnp.pad(shaped, ((0, 0), (0, 0), (0, PAD - SEQ), (0, 0)))

    same = row == col

    routes = chosen(expert_ids, col)
    gates = chosen(gate_values, col)
    slot = destinations(routes, capacity)
    unit = routes % local_experts * capacity + slot
    home = unit // share
    target = (routes // local_experts * 2 + home % 2) * held_rows + unit % share
    target = jnp.where(home // 2 == row, target, -1)

    def own_first(array, fill):
        shaped = array.reshape(2, images, SEQ, TOP)
        shaped = jnp.pad(
            shaped, ((0, 0), (0, 0), (0, PAD - SEQ), (0, 0)), constant_values=fill
        ).reshape(2, images * PAD, TOP)
        return jnp.where(row == 0, shaped, shaped[::-1])

    target = own_first(target, -1)
    gates = own_first(gates, 0)
    target_rows = target.transpose(0, 2, 1).reshape(2 * TOP, images * PAD)
    gate_rows = gates.transpose(0, 2, 1).reshape(2 * TOP, images * PAD)

    def by_chip(array, earlier):
        own = chosen(array, col)
        got = swap(after(chosen(array, 1 - col), earlier), "col")
        return either(same, own, got), either(same, got, own)

    kept, sent = by_chip(by_image(out_cotangent), ())
    kept = after(kept, target_rows, gate_rows)
    cot = in_order(row, jnp.stack([kept, sent]), swap(jnp.stack([sent, kept]), "row"), 3)
    kept, sent = by_chip(by_image(tokens_in), kept)
    x = in_order(row, kept, swap(after(sent, parts), "row"), 2)

    def exchange(slots):
        shaped = slots.reshape(peers, held_rows, D)
        return lax.all_to_all(shaped, ("dp", "col"), 0, 0, tiled=True).reshape(rows, D)

    def flat(array):
        return array.reshape(images * PAD, D)

    if local_experts == 1:
        where = jnp.stack([jnp.zeros_like(row), jnp.zeros_like(row), row])
    else:
        where = jnp.stack([2 * row + col, col, row])
    norms = jnp.stack([first_gain, first_shift, second_gain, second_shift])
    norms = in_order(row, norms, swap(norms, "row"), 1)
    we_got = other_core(expand_weight, row)
    wc_got = other_core(contract_weight, row)
    wc = other_chip(contract_weight, wc_got, row, col)
    we = other_chip(expand_weight, we_got, row, col)
    cot = after(cot, norms)
    grad_slots = dispatch(target_rows, gate_rows, flat(cot[0]), flat(cot[1]), rows, True)
    grad_slots = exchange(grad_slots)

    parts = [parts, swap(parts, "row")]
    here = jnp.stack([row, col])
    wq, wp, bq, bp = unpacked(here, parts)
    bias_rows = [part[:, :, 2 * D // size + 3 :].astype(F32)[:, :, None] for part in parts]
    bias_rows = in_order(row, *bias_rows, 2)

    def taken(start, like):
        count = like.size // width
        found = bias_rows[:, :, :, start : start + count]
        return found.reshape(found.shape[:3] + like.shape), start + count

    expert = place * local_experts + (2 * row + col) * local_experts // 4
    be, at = taken(0, expand_bias)
    be = chosen(be, expert // (EXPERTS // 2), 2)
    be = chosen(be, expert % (EXPERTS // 2), 2).transpose(1, 0, 2).reshape(2, -1)
    be = either(col == 0, be, be[::-1])
    bc, at = taken(at, contract_bias)
    bc = chosen(bc[:, 0], expert, 2).transpose(1, 0, 2).reshape(1, D)

    x = after(x, wc_got, we_got)
    low, middle, tri, att, lse = attention_forward(x, wq, bq, wp, bp, norms)
    low = flat(low)
    slots = dispatch(target_rows, gate_rows, low, swap(low, "row"), rows, False)
    slots = exchange(slots)
    gact = active_grad(where, grad_slots, wc, 0)
    where_slots = selection(target, rows)
    slots = after(slots, gact, where_slots)
    act, inner_grad, slot_grad = experts_middle(where, slots, gact, we, be, 0)
    gact = active_grad(where, after(grad_slots, slot_grad), wc, 1)
    act_far, inner_grad_far, slot_grad = experts_middle(
        where, slots, gact, we, be, 1, slot_grad
    )
    slot_grad = exchange(slot_grad)
    wc_grad_far, bc_grad = contract_grad(where, act_far, grad_slots)
    we_grad_far, be_grad_far = expand_grad(where, slots, inner_grad_far)
    wc_far, we_far = swap(wc_grad_far, "col"), swap(we_grad_far, "col")
    wc_grad, _ = contract_grad(where, after(act, we_grad_far, wc_grad_far), grad_slots)
    we_grad, be_grad = expand_grad(where, after(slots, we_grad_far, wc_grad_far), inner_grad)
    outer = experts_outer(where, (act, act_far), wc, bc)
    slot_grad = after(slot_grad, wc_grad, we_grad, outer)
    outer = exchange(after(outer, slot_grad))

    mine = (jnp.arange(EXPERTS, dtype=jnp.int32) == expert).astype(F32)
    be_grad = jnp.stack([be_grad, be_grad_far]).reshape(2, size, -1)
    be_grad = either(col == 0, be_grad, be_grad[::-1]).transpose(1, 0, 2)
    be_grad = mine.reshape(2, 1, 1, -1, 1) * be_grad[None, :, :, None, :]
    bc_grad = mine.reshape(1, 1, 1, -1, 1) * bc_grad.reshape(2, size, 1, 1, -1)
    bc_grad = jnp.broadcast_to(bc_grad, (2, size, 2) + bc_grad.shape[3:])
    extra = jnp.concatenate(
        [
            be_grad.reshape(2, size, 2, -1, width),
            bc_grad.reshape(2, size, 2, -1, width),
        ],
        3,
    )
    short = EXTRA - extra.shape[3]
    extra = jnp.pad(extra, ((0, 0),) * 3 + ((0, short), (0, 0))).astype(block_type(size))

    def to_image(array):
        return array.reshape(images, PAD, -1)

    got = swap(selected(where_slots, 1, slot_grad, BF16), "row")
    own = selected(where_slots, 0, slot_grad, F32)
    grad_kept, grad_sent, blocks = attention_backward(
        here, x, middle, cot[0], to_image(own), to_image(got), tri, att, lse, wq, wp, norms, extra
    )
    blocks = after(blocks.astype(BF16), we_far, wc_far)
    kept = chosen(blocks, row).astype(F32)
    blocks = (kept + swap(chosen(blocks, 1 - row), "row").astype(F32)).astype(BF16)
    blocks = after(blocks.reshape((peers,) + blocks.shape[2:]), outer)
    reduced = lax.all_to_all(blocks, ("dp", "col"), 0, 0, tiled=True)
    reduced = jnp.sum(reduced.astype(F32), axis=0)
    wc_grad = weight_grad(wc_grad, wc_far, row, col, local_experts)
    we_grad = weight_grad(we_grad, we_far, row, col, local_experts)

    def to_tokens(kept, sent):
        got = swap(sent, "row")
        own, other = either(same, kept, got), either(same, got, kept)
        return own, swap(other, "col")

    def placed(own, other, dtype):
        both = in_order(col, own[None].astype(F32), other[None].astype(F32), 0)[:, :, :SEQ]
        return both.reshape(2, local_rows, width).astype(dtype)

    input_grad = placed(*to_tokens(grad_kept, grad_sent), F32)

    def out_half(half):
        kept, sent = combine(here, half, target, gates, outer, flat(middle))
        return to_image(kept.astype(F32) + swap(sent, "row").astype(F32))

    leaves = either(same, 1, 0)
    other = swap(out_half(leaves).astype(BF16), "col")
    layer_out = placed(out_half(1 - leaves), other, BF16)

    depth = qkv_weight.shape[0]
    out_wq = reduced[: 3 * depth].reshape(3, depth, width).transpose(1, 0, 2)
    out_wp = reduced[3 * depth : 4 * depth]
    be_rows = expand_bias.size // width
    out_be = reduced[4 * depth : 4 * depth + be_rows].reshape(expand_bias.shape)
    bc_rows = contract_bias.size // width
    out_bc = reduced[4 * depth + be_rows : 4 * depth + be_rows + bc_rows]
    out_bc = out_bc.reshape(contract_bias.shape)
    sums = reduced[4 * depth + EXTRA :].reshape(2, 8, width)
    norm_total = chosen(sums, row)
    out_bp = chosen(norm_total[4].reshape(size, -1), place)
    out_bq = chosen(chosen(sums, col)[5:7].reshape(2, size, -1), place, 1)
    return (
        layer_out,
        input_grad,
        norm_total[0],
        norm_total[1],
        norm_total[2],
        norm_total[3],
        out_wq,
        out_bq,
        out_wp,
        out_bp,
        we_grad,
        out_be,
        wc_grad,
        out_bc,
    )


def solution(mesh):
    return jax.shard_map(
        on_device,
        mesh=mesh,
        in_specs=(
            P(None, ("dp", "col"), "row"),
            P(None, ("dp", "col"), "row"),
            P(None, "dp", None),
            P(None, "dp", None),
            P("row"),
            P("row"),
            P("row"),
            P("row"),
            P(("row", "dp"), None, "col"),
            P(None, ("col", "dp")),
            P(("col", "dp"), "row"),
            P(("row", "dp")),
            P("dp", "row", "col"),
            P("row", ("col", "dp")),
            P("dp", "col", "row"),
            P(None, ("row", "dp")),
        ),
        out_specs=(
            P(None, ("dp", "col"), "row"),
            P(None, ("dp", "col"), "row"),
            P("row"),
            P("row"),
            P("row"),
            P("row"),
            P(("row", "dp"), None, "col"),
            P(None, ("col", "dp")),
            P(("col", "dp"), "row"),
            P(("row", "dp")),
            P("dp", "row", "col"),
            P("row", ("col", "dp")),
            P("dp", "col", "row"),
            P(None, ("row", "dp")),
        ),
        check_vma=False,
    )
```

```python
import functools

import jax
import jax.numpy as jnp
from jax import lax
from jax.experimental import pallas as pl
from jax.experimental.pallas import tpu as pltpu
from jax.sharding import PartitionSpec as P

D = 512
HEADS = 8
EXPERTS = 32
TOP = 2
SEQ = 197
HEAD_DIM = D // HEADS
PAIR = 2 * HEAD_DIM
PAD = 208

EPS = 1e-06
HIGH = lax.Precision.HIGHEST
ROOT_HALF = 0.7071067811865476
DENSITY = 0.3989422804014327
SCALE = HEAD_DIM ** (-0.5)
FAR = -1e30
MIB = 1 << 20

BF16 = jnp.bfloat16
F32 = jnp.float32


def round_up(value, unit):
    return (value + unit - 1) // unit * unit


def swap(value, axis, bit=1):
    size = lax.axis_size(axis)
    return lax.ppermute(value, axis, [(place, place ^ bit) for place in range(size)])


def either(first, when_true, when_false):
    return jnp.where(first, when_true, when_false)


def in_order(index, own, other, axis):
    return jnp.where(
        index == 0,
        jnp.concatenate([own, other], axis),
        jnp.concatenate([other, own], axis),
    )


def chosen(array, index, axis=0):
    return lax.dynamic_index_in_dim(array, index, axis, keepdims=False)


def contract(left, right, left_dim, right_dim):
    return lax.dot_general(
        left, right, (((left_dim,), (right_dim,)), ((), ())), preferred_element_type=F32
    )


def after(value, *others):
    return lax.optimization_barrier((value,) + others)[0]


def call(
    kernel, micros, grid, in_specs, out_specs, out_shape, scratch=(), limit=48, scalars=0
):
    return pl.pallas_call(
        kernel,
        grid_spec=pltpu.PrefetchScalarGridSpec(
            num_scalar_prefetch=scalars,
            grid=grid,
            in_specs=in_specs,
            out_specs=out_specs,
            scratch_shapes=list(scratch),
        ),
        out_shape=out_shape,
        cost_estimate=pl.CostEstimate(
            flops=int(micros * 1e9), bytes_accessed=int(micros * 2e6), transcendentals=0
        ),
        compiler_params=pltpu.CompilerParams(
            dimension_semantics=("arbitrary",) * len(grid), vmem_limit_bytes=limit * MIB
        ),
    )


def whole(shape):
    return pl.BlockSpec(shape, lambda *_: (0,) * len(shape))


def stepped(shape, axis=0):
    return pl.BlockSpec(
        shape, lambda g, *_: tuple(g if place == axis else 0 for place in range(len(shape)))
    )


def destinations(routes, capacity):
    labels = jnp.arange(EXPERTS, dtype=jnp.int32)
    named = (routes[:, :, None] == labels).astype(F32)
    count = routes.shape[0]
    place = jnp.arange(count, dtype=jnp.int32)
    earlier = (place[None, :] < place[:, None]).astype(BF16)
    before = jnp.dot(earlier, named.sum(axis=1).astype(BF16), preferred_element_type=F32)
    return jnp.sum(before[:, None, :] * named, axis=2).astype(jnp.int32)


def dispatch_kernel(gated, target_ref, gate_ref, own_ref, other_ref, out_ref):
    rows = out_ref.shape[0]
    count = own_ref.shape[0]
    place = lax.broadcasted_iota(jnp.int32, (rows, count), 0) + pl.program_id(0) * rows
    total = None
    for half, tokens in ((0, own_ref), (1, other_ref)):
        first = place == target_ref[2 * half : 2 * half + 1, :]
        second = place == target_ref[2 * half + 1 : 2 * half + 2, :]
        if gated:
            weight = jnp.where(
                first,
                gate_ref[2 * half : 2 * half + 1, :],
                jnp.where(second, gate_ref[2 * half + 1 : 2 * half + 2, :], 0.0),
            )
        else:
            weight = jnp.where(first | second, 1.0, 0.0)
        term = jnp.dot(weight.astype(BF16), tokens[...], preferred_element_type=F32)
        total = term if total is None else total + term
    out_ref[...] = total.astype(BF16)


def dispatch(target_rows, gate_rows, own, other, rows, gated):
    steps = 4
    return call(
        functools.partial(dispatch_kernel, gated),
        5,
        (steps,),
        [whole(target_rows.shape), whole(gate_rows.shape), whole(own.shape), whole(other.shape)],
        stepped((rows // steps, D)),
        pltpu.HBM((rows, D), BF16),
    )(target_rows, gate_rows, own, other)


def combined(target_ref, gate_ref, slots_ref):
    count, rows = target_ref.shape[1], slots_ref.shape[0]
    place = lax.broadcasted_iota(jnp.int32, (count, rows), 1)
    first = place == target_ref[0, :, 0:1]
    second = place == target_ref[0, :, 1:2]
    weight = jnp.where(first, gate_ref[0, :, 0:1], jnp.where(second, gate_ref[0, :, 1:2], 0.0))
    return jnp.dot(weight.astype(BF16), slots_ref[...], preferred_element_type=F32)


def selection_kernel(target_ref, out_ref):
    place = lax.broadcasted_iota(jnp.int32, out_ref.shape[1:], 1)
    first = place == target_ref[0, :, 0:1]
    second = place == target_ref[0, :, 1:2]
    out_ref[0] = jnp.where(first | second, 1.0, 0.0).astype(BF16)


def selection(target, rows):
    steps = 4
    count = 2 * target.shape[1] // steps
    return call(
        selection_kernel,
        8,
        (steps,),
        [pl.BlockSpec((1, count, TOP), lambda g: (g // 2, g % 2, 0))],
        pl.BlockSpec((1, count, rows), lambda g: (g // 2, g % 2, 0)),
        jax.ShapeDtypeStruct((2, target.shape[1], rows), BF16),
    )(target)


def select_kernel(chosen_ref, slots_ref, out_ref):
    out = jnp.dot(chosen_ref[0], slots_ref[...], preferred_element_type=F32)
    out_ref[...] = out.astype(out_ref.dtype)


def selected(selection, half, slots, dtype):
    steps = 2
    rows = selection.shape[1] // steps
    return call(
        select_kernel,
        3,
        (steps,),
        [
            pl.BlockSpec((1, rows, selection.shape[2]), lambda g: (half, g, 0)),
            whole(slots.shape),
        ],
        stepped((rows, D)),
        jax.ShapeDtypeStruct((selection.shape[1], D), dtype),
    )(selection, slots)


def combine_out_kernel(
    place_ref, target_ref, gate_ref, slots_ref, middle_ref, kept_ref, sent_ref
):
    out = combined(target_ref, gate_ref, slots_ref)
    out = jnp.where(place_ref[1] == 0, out + middle_ref[...], out)
    kept_ref[...], sent_ref[...] = feature_halves(place_ref, out.astype(BF16))


def feature_halves(place_ref, value):
    half = value.shape[-1] // 2
    low, high = value[..., :half], value[..., half:]
    first = place_ref[0] == 0
    return jnp.where(first, low, high), jnp.where(first, high, low)


def combine(place, half, target, gates, slots, middle):
    steps = 2
    count = target.shape[1]
    column = pl.BlockSpec((1, count // steps, TOP), lambda g, place: (place[1], g, 0))
    return call(
        combine_out_kernel,
        5,
        (steps,),
        [column, column, whole(slots.shape), stepped((count // steps, D))],
        [stepped((count // steps, D // 2))] * 2,
        [jax.ShapeDtypeStruct((count, D // 2), BF16)] * 2,
        scalars=1,
    )(jnp.stack([place[0], half]), target, gates, slots, middle)


def block_type(size):
    return BF16 if D // (2 * size) % 16 == 0 else F32


EXTRA = 16


def unpack_kernel(place_ref, own_ref, other_ref, wq_ref, wp_ref, bq_ref, bp_ref):
    size = own_ref.shape[0]
    depth, half = D // (2 * size), D // 2
    row = place_ref[0]
    bq_ref[:, D : 2 * D] = jnp.zeros((1, D), F32)
    for ref, r in ((own_ref, row), (other_ref, 1 - row)):
        at_r = pl.multiple_of(r * half, half)
        for c in range(2):
            at_c = c * half
            biases = jnp.sum(ref[:, c, 4 * depth : 4 * depth + EXTRA, :].astype(F32), axis=0)
            bq_ref[:, at_c : at_c + half] = biases[0:1]
            bq_ref[:, 2 * D + at_c : 2 * D + at_c + half] = biases[1:2]
            bp_ref[:, pl.ds(at_r, half)] = biases[2:3]
            for dp in range(size):
                rows = pl.ds(pl.multiple_of(r * half + dp * depth, depth), depth)
                for part in range(3):
                    at = part * D + at_c
                    wq_ref[rows, at : at + half] = ref[dp, c, part * depth : (part + 1) * depth, :]
                rows = slice(at_c + dp * depth, at_c + (dp + 1) * depth)
                wp_ref[rows, pl.ds(at_r, half)] = ref[dp, c, 3 * depth : 4 * depth, :]


def unpacked(place, parts):
    kind = block_type(parts[0].shape[0])
    shapes = [(D, 3 * D), (D, D), (1, 3 * D), (1, D)]
    wq, wp, bq, bp = call(
        unpack_kernel,
        2,
        (1,),
        [whole(part.shape) for part in parts],
        [whole(shape) for shape in shapes],
        [jax.ShapeDtypeStruct(shape, t) for shape, t in zip(shapes, (kind, kind, F32, F32))],
        scalars=1,
    )(place, *[part.astype(kind) for part in parts])
    return wq.astype(BF16), wp.astype(BF16), bq, bp


def normalized(value):
    center = jnp.mean(value, axis=-1, keepdims=True)
    spread = jnp.mean(value * value, axis=-1, keepdims=True) - center * center
    factor = lax.rsqrt(spread + EPS)
    return (value - center) * factor, factor


def norm_back(grad, scaled, factor, gain):
    upper = grad * gain
    return factor * (
        upper
        - jnp.mean(upper, axis=-1, keepdims=True)
        - scaled * jnp.mean(upper * scaled, axis=-1, keepdims=True)
    )


def forward_kernel(
    x_ref,
    wq_ref,
    bq_ref,
    wp_ref,
    bp_ref,
    norm_ref,
    low_ref,
    mid_ref,
    tri_ref,
    att_ref,
    lse_ref,
):
    x = x_ref[0].astype(F32)
    scaled, _ = normalized(x)
    low = (scaled * norm_ref[0:1, :] + norm_ref[1:2, :]).astype(BF16)
    tri = jnp.dot(low, wq_ref[...], preferred_element_type=F32) + bq_ref[...]
    tri_ref[0] = tri.astype(BF16)
    lane = lax.broadcasted_iota(jnp.int32, (PAD, PAIR), 1)
    shut = lax.broadcasted_iota(jnp.int32, (PAD, PAD), 1) >= SEQ
    logs = jnp.zeros((PAD, 128), F32)
    column = lax.broadcasted_iota(jnp.int32, (PAD, 128), 1)
    for pair in range(HEADS // 2):
        at = pair * PAIR
        query = tri_ref[0, :, at : at + PAIR]
        keys = tri_ref[0, :, D + at : D + at + PAIR]
        values = tri_ref[0, :, 2 * D + at : 2 * D + at + PAIR]
        outs = []
        for side in range(2):
            mine = (lane // HEAD_DIM) == side
            scores = contract(jnp.where(mine, query, jnp.zeros_like(query)), keys, 1, 1) * SCALE
            scores = jnp.where(shut, FAR, scores)
            peak = jnp.max(scores, axis=-1, keepdims=True)
            expo = jnp.exp(scores - peak)
            total = jnp.sum(expo, axis=-1, keepdims=True)
            prob = (expo / total).astype(BF16)
            outs.append(jnp.dot(prob, values, preferred_element_type=F32))
            logs = jnp.where(column == 2 * pair + side, peak + jnp.log(total), logs)
        att_ref[0, :, at : at + PAIR] = jnp.where(lane < HEAD_DIM, outs[0], outs[1]).astype(BF16)
    lse_ref[0] = logs
    branch = jnp.dot(att_ref[0], wp_ref[...], preferred_element_type=F32) + bp_ref[...]
    middle = x + branch
    mid_ref[0] = middle
    scaled2, _ = normalized(middle)
    low_ref[0] = (scaled2 * norm_ref[2:3, :] + norm_ref[3:4, :]).astype(BF16)


def attention_forward(x, wq, bq, wp, bp, norms):
    images = x.shape[0]
    return call(
        forward_kernel,
        9,
        (images,),
        [
            stepped((1, PAD, D)),
            whole(wq.shape),
            whole(bq.shape),
            whole(wp.shape),
            whole(bp.shape),
            whole(norms.shape),
        ],
        [
            stepped((1, PAD, D)),
            stepped((1, PAD, D)),
            stepped((1, PAD, 3 * D)),
            stepped((1, PAD, D)),
            stepped((1, PAD, 128)),
        ],
        [
            jax.ShapeDtypeStruct((images, PAD, D), BF16),
            jax.ShapeDtypeStruct((images, PAD, D), F32),
            jax.ShapeDtypeStruct((images, PAD, 3 * D), BF16),
            jax.ShapeDtypeStruct((images, PAD, D), BF16),
            jax.ShapeDtypeStruct((images, PAD, 128), F32),
        ],
    )(x, wq, bq, wp, bp, norms)


def backward_kernel(
    place_ref,
    x_ref,
    mid_ref,
    cot_ref,
    own_ref,
    got_ref,
    tri_ref,
    att_ref,
    lse_ref,
    wq_ref,
    wp_ref,
    norm_ref,
    extra_ref,
    kept_ref,
    sent_ref,
    blocks_ref,
    sums_ref,
    dwq_ref,
    dwp_ref,
    tg_ref,
):
    @pl.when(pl.program_id(0) == 0)
    def _():
        dwq_ref[...] = jnp.zeros_like(dwq_ref)
        dwp_ref[...] = jnp.zeros_like(dwp_ref)
        sums_ref[...] = jnp.zeros_like(sums_ref)

    low_grad = own_ref[0] + got_ref[0].astype(F32)
    scaled2, factor2 = normalized(mid_ref[0])
    sums_ref[2:3, :] += jnp.sum(low_grad * scaled2, axis=0, keepdims=True)
    sums_ref[3:4, :] += jnp.sum(low_grad, axis=0, keepdims=True)
    mid_grad = cot_ref[0].astype(F32) + norm_back(low_grad, scaled2, factor2, norm_ref[2:3, :])
    branch = mid_grad.astype(BF16)
    sums_ref[4:5, :] += jnp.sum(branch.astype(F32), axis=0, keepdims=True)
    dwp_ref[...] += contract(att_ref[0], branch, 0, 0)
    att_grad = contract(branch, wp_ref[...], 1, 1).astype(BF16)
    lane = lax.broadcasted_iota(jnp.int32, (PAD, PAIR), 1)
    shut = lax.broadcasted_iota(jnp.int32, (PAD, PAD), 1) >= SEQ
    for pair in range(HEADS // 2):
        at = pair * PAIR
        query = tri_ref[0, :, at : at + PAIR]
        keys = tri_ref[0, :, D + at : D + at + PAIR]
        values = tri_ref[0, :, 2 * D + at : 2 * D + at + PAIR]
        upstream = att_grad[:, at : at + PAIR]
        query_grads = []
        key_grad = jnp.zeros((PAD, PAIR), F32)
        value_grad = jnp.zeros((PAD, PAIR), F32)
        for side in range(2):
            mine = (lane // HEAD_DIM) == side
            query_one = jnp.where(mine, query, jnp.zeros_like(query))
            grad_one = jnp.where(mine, upstream, jnp.zeros_like(upstream))
            scores = contract(query_one, keys, 1, 1) * SCALE
            scores = jnp.where(shut, FAR, scores)
            head = 2 * pair + side
            prob = jnp.exp(scores - lse_ref[0, :, head : head + 1])
            prob_grad = contract(grad_one, values, 1, 1)
            value_grad += contract(prob.astype(BF16), grad_one, 0, 0)
            inside = jnp.sum(prob * prob_grad, axis=-1, keepdims=True)
            score_grad = (prob * (prob_grad - inside)).astype(BF16)
            query_grads.append(jnp.dot(score_grad, keys, preferred_element_type=F32))
            key_grad += contract(score_grad, query_one, 0, 0)
        query_grad = jnp.where(lane < HEAD_DIM, query_grads[0], query_grads[1])
        tg_ref[:, at : at + PAIR] = (query_grad * SCALE).astype(BF16)
        tg_ref[:, D + at : D + at + PAIR] = (key_grad * SCALE).astype(BF16)
        tg_ref[:, 2 * D + at : 2 * D + at + PAIR] = value_grad.astype(BF16)
    tri_grad = tg_ref[...]
    sums_ref[5:6, :] += jnp.sum(tri_grad[:, :D].astype(F32), axis=0, keepdims=True)
    sums_ref[6:7, :] += jnp.sum(tri_grad[:, 2 * D :].astype(F32), axis=0, keepdims=True)
    scaled, factor = normalized(x_ref[0].astype(F32))
    low = (scaled * norm_ref[0:1, :] + norm_ref[1:2, :]).astype(BF16)
    dwq_ref[...] += contract(low, tri_grad, 0, 0)
    normed_grad = contract(tri_grad, wq_ref[...], 1, 1)
    sums_ref[0:1, :] += jnp.sum(normed_grad * scaled, axis=0, keepdims=True)
    sums_ref[1:2, :] += jnp.sum(normed_grad, axis=0, keepdims=True)
    grad = mid_grad + norm_back(normed_grad, scaled, factor, norm_ref[0:1, :])
    kept_ref[0], sent_ref[0] = feature_halves(place_ref, grad.astype(BF16))

    @pl.when(pl.program_id(0) == pl.num_programs(0) - 1)
    def _():
        size = blocks_ref.shape[1]
        depth, half, kind = D // (2 * size), D // 2, blocks_ref.dtype
        sums = jnp.concatenate([sums_ref[:, :half], sums_ref[:, half:]], 0).astype(kind)
        blocks_ref[:, :, :, 4 * depth : 4 * depth + EXTRA, :] = extra_ref[...]
        for row in range(2):
            for dp in range(size):
                for col in range(2):
                    block = blocks_ref.at[row, dp, col]
                    rows = slice(row * half + dp * depth, row * half + (dp + 1) * depth)
                    for part in range(3):
                        at = part * D + col * half
                        block[part * depth : (part + 1) * depth, :] = dwq_ref[
                            rows, at : at + half
                        ].astype(kind)
                    rows = slice(col * half + dp * depth, col * half + (dp + 1) * depth)
                    block[3 * depth : 4 * depth, :] = dwp_ref[
                        rows, row * half : (row + 1) * half
                    ].astype(kind)
                    block[4 * depth + EXTRA :, :] = sums


def attention_backward(place, x, middle, cot, own, got, tri, att, lse, wq, wp, norms, extra):
    images = x.shape[0]
    size = extra.shape[1]
    blocks = (2, size, 2, 2 * D // size + EXTRA + 16, D // 2)
    return call(
        backward_kernel,
        21,
        (images,),
        [
            stepped((1, PAD, D)),
            stepped((1, PAD, D)),
            stepped((1, PAD, D)),
            stepped((1, PAD, D)),
            stepped((1, PAD, D)),
            stepped((1, PAD, 3 * D)),
            stepped((1, PAD, D)),
            stepped((1, PAD, 128)),
            whole(wq.shape),
            whole(wp.shape),
            whole(norms.shape),
            whole(extra.shape),
        ],
        [
            stepped((1, PAD, D // 2)),
            stepped((1, PAD, D // 2)),
            whole(blocks),
        ],
        [
            jax.ShapeDtypeStruct((images, PAD, D // 2), BF16),
            jax.ShapeDtypeStruct((images, PAD, D // 2), BF16),
            jax.ShapeDtypeStruct(blocks, block_type(size)),
        ],
        scratch=[
            pltpu.VMEM((8, D), F32),
            pltpu.VMEM((D, 3 * D), F32),
            pltpu.VMEM((D, D), F32),
            pltpu.VMEM((PAD, 3 * D), BF16),
        ],
        scalars=1,
    )(place, x, middle, cot, own, got, tri, att, lse, wq, wp, norms, extra)


STEPS = 4


def own_first(place_ref, value):
    half = value.shape[-1] // 2
    low, high = value[..., :half], value[..., half:]
    first = place_ref[2] == 0
    return jnp.concatenate([jnp.where(first, low, high), jnp.where(first, high, low)], -1)


def active_grad_kernel(place_ref, grad_ref, own_ref, other_ref, out_ref):
    weight = jnp.concatenate([own_ref[0], other_ref[0]], 1)
    out_ref[...] = contract(own_first(place_ref, grad_ref[...]), weight, 1, 1).astype(BF16)


def expert_kernel(place_ref, slots_ref, gact_ref, own_ref, other_ref, be_ref, *refs):
    *before, act_ref, inner_grad_ref, slot_grad_ref = refs
    weight = jnp.concatenate([own_ref[0], other_ref[0]], 0)
    tokens = own_first(place_ref, slots_ref[...])
    inner = jnp.dot(tokens, weight, preferred_element_type=F32) + be_ref[...]
    share = 0.5 * (1.0 + lax.erf(inner * ROOT_HALF))
    act_ref[...] = (inner * share).astype(BF16)
    slope = share + inner * (DENSITY * jnp.exp(-0.5 * inner * inner))
    grad = (gact_ref[...].astype(F32) * slope).astype(BF16)
    inner_grad_ref[...] = grad
    total = own_first(place_ref, contract(grad, weight, 1, 1))
    for ref in before:
        total += ref[...].astype(F32)
    slot_grad_ref[...] = total.astype(BF16)


def outer_kernel(place_ref, act0_ref, act1_ref, wc0_ref, wc1_ref, wc2_ref, wc3_ref, bc_ref, out_ref):
    total = jnp.dot(
        act0_ref[...], jnp.concatenate([wc0_ref[0], wc1_ref[0]], 1), preferred_element_type=F32
    )
    total += jnp.dot(
        act1_ref[...], jnp.concatenate([wc2_ref[0], wc3_ref[0]], 1), preferred_element_type=F32
    )
    out_ref[...] = (own_first(place_ref, total) + bc_ref[...]).astype(BF16)


def contract_grad_kernel(place_ref, act_ref, grad_ref, out_ref, bias_ref):
    product = contract(act_ref[...], grad_ref[...], 0, 0).astype(BF16)
    half = product.shape[1] // 2
    low, high = product[:, :half], product[:, half:]
    out_ref[0] = jnp.where(place_ref[2] == 0, low, high)
    out_ref[1] = jnp.where(place_ref[2] == 0, high, low)

    @pl.when(pl.program_id(0) == 0)
    def _():
        bias_ref[...] = jnp.sum(grad_ref[...].astype(F32), axis=0, keepdims=True)


def expand_grad_kernel(place_ref, slots_ref, grad_ref, out_ref, bias_ref):
    product = contract(slots_ref[...], grad_ref[...], 0, 0).astype(BF16)
    half = product.shape[0] // 2
    low, high = product[:half], product[half:]
    out_ref[0] = jnp.where(place_ref[2] == 0, low, high)
    out_ref[1] = jnp.where(place_ref[2] == 0, high, low)
    bias_ref[...] = jnp.sum(grad_ref[...].astype(F32), axis=0, keepdims=True)


def weight_specs(pieces, half):
    shape = (1,) + pieces[0].shape[1:]
    places = [lambda g, place: (place[0], 0, 0), lambda g, place: (place[1], 0, 0)]
    if half:
        places = [lambda g, place: (0, 0, 0)] * 2
    return [pl.BlockSpec(shape, place) for place in places]


def active_grad(place, grad_slots, wc, half):
    rows, hidden = grad_slots.shape[0], wc[0].shape[1]
    return call(
        active_grad_kernel,
        5,
        (STEPS,),
        [stepped((rows // STEPS, D))] + weight_specs(wc, half),
        stepped((rows // STEPS, hidden)),
        jax.ShapeDtypeStruct((rows, hidden), BF16),
        scalars=1,
    )(place, grad_slots, *wc[2 * half : 2 * half + 2])


def experts_middle(place, slots, gact, we, be, half, *before):
    rows, hidden = gact.shape
    return call(
        expert_kernel,
        11,
        (STEPS,),
        [stepped((rows // STEPS, D)), stepped((rows // STEPS, hidden))]
        + weight_specs(we, half)
        + [whole((1, hidden))]
        + [stepped((rows // STEPS, D))] * len(before),
        [
            stepped((rows // STEPS, hidden)),
            stepped((rows // STEPS, hidden)),
            stepped((rows // STEPS, D)),
        ],
        [
            jax.ShapeDtypeStruct((rows, hidden), BF16),
            jax.ShapeDtypeStruct((rows, hidden), BF16),
            pltpu.HBM((rows, D), BF16),
        ],
        scalars=1,
    )(place, slots, gact, *we[2 * half : 2 * half + 2], be[half : half + 1], *before)


def experts_outer(place, acts, wc, bc):
    rows, hidden = acts[0].shape
    return call(
        outer_kernel,
        9,
        (STEPS,),
        [stepped((rows // STEPS, hidden))] * 2
        + weight_specs(wc, 0)
        + weight_specs(wc, 1)
        + [whole(bc.shape)],
        stepped((rows // STEPS, D)),
        jax.ShapeDtypeStruct((rows, D), BF16),
        scalars=1,
    )(place, *acts, *wc, bc)


def contract_grad(place, act, grad_slots):
    rows, hidden = act.shape
    chunk = hidden // 2
    return call(
        contract_grad_kernel,
        5,
        (2,),
        [stepped((rows, chunk), 1), whole(grad_slots.shape)],
        [stepped((2, chunk, D // 2), 1), whole((1, D))],
        [
            jax.ShapeDtypeStruct((2, hidden, D // 2), BF16),
            jax.ShapeDtypeStruct((1, D), F32),
        ],
        scalars=1,
    )(place, act, grad_slots)


def expand_grad(place, slots, inner_grad):
    rows, hidden = inner_grad.shape
    chunk = hidden // 2
    return call(
        expand_grad_kernel,
        5,
        (2,),
        [whole(slots.shape), stepped((rows, chunk), 1)],
        [stepped((2, D // 2, chunk), 2), stepped((1, chunk), 1)],
        [
            jax.ShapeDtypeStruct((2, D // 2, hidden), BF16),
            jax.ShapeDtypeStruct((1, hidden), F32),
        ],
        scalars=1,
    )(place, slots, inner_grad)


def other_core(block, row):
    if block.shape[0] == 1:
        return swap(block, "row")
    return swap(lax.dynamic_slice_in_dim(block, 2 * (1 - row), 2, 0), "row")


def other_chip(block, got, row, col, earlier=()):
    own, other = block, got
    if block.shape[0] > 1:
        own = lax.dynamic_slice_in_dim(own, 2 * row + 1 - col, 1, 0)
        other = lax.dynamic_slice_in_dim(other, 1 - col, 1, 0)
    own = swap(own, "col")
    return block, got, own, swap(after(other, earlier), "col")


def assemble_kernel(place_ref, *refs):
    for step, ref in enumerate(refs[:4]):

        @pl.when(pl.program_id(0) == step)
        def _(ref=ref):
            refs[4][0] = ref[...].astype(F32)


def grad_block(pieces, row, col):
    shape = pieces[0].shape
    order = jnp.stack([2 * row + col, 2 * row + 1 - col, 2 * (1 - row) + col, 3 - 2 * row - col])
    return call(
        assemble_kernel,
        4,
        (4,),
        [whole(shape)] * 4,
        pl.BlockSpec((1,) + shape, lambda g, order: (order[g], 0, 0)),
        jax.ShapeDtypeStruct((4,) + shape, F32),
        scalars=1,
    )(order, *pieces)


def weight_grad(grad, far, row, col, experts):
    if experts == 1:
        own, near = (grad[side].astype(F32) + far[side].astype(F32) for side in range(2))
        return (own + swap(near.astype(BF16), "row").astype(F32))[None]
    return grad_block((grad[0], far[0], swap(grad[1], "row"), swap(far[1], "row")), row, col)


def as_rows(value, width):
    flat = value.reshape(-1)
    return jnp.pad(flat, (0, round_up(flat.shape[0], width) - flat.shape[0])).reshape(-1, width)


def on_device(
    tokens_in,
    out_cotangent,
    expert_ids,
    gate_values,
    first_gain,
    first_shift,
    second_gain,
    second_shift,
    qkv_weight,
    qkv_bias,
    proj_weight,
    proj_bias,
    expand_weight,
    expand_bias,
    contract_weight,
    contract_bias,
):
    size = lax.axis_size("dp")
    row, col, place = lax.axis_index("row"), lax.axis_index("col"), lax.axis_index("dp")
    local_rows, width = tokens_in.shape[1:]
    group = expert_ids.shape[1]
    images = local_rows // SEQ
    capacity = (group * TOP * 4 + 3 * EXPERTS - 1) // (3 * EXPERTS)
    local_experts = EXPERTS // size
    share = local_experts * capacity // 4
    held_rows = round_up(share, 8)
    peers = 2 * size
    rows = peers * held_rows

    def at_place(array):
        mine = (jnp.arange(size, dtype=jnp.int32) == place).astype(F32)
        return (mine[None, :, None] * array[:, None, :]).reshape(-1, width)

    biases = jnp.concatenate(
        [
            at_place(qkv_bias),
            at_place(proj_bias[None]),
            expand_bias.reshape(-1, width),
            contract_bias.reshape(-1, width),
        ],
        0,
    )
    biases = jnp.pad(biases, ((0, EXTRA - biases.shape[0]), (0, 0)))
    block = jnp.concatenate(
        [qkv_weight.transpose(1, 0, 2).reshape(-1, width), proj_weight, biases.astype(BF16)], 0
    )
    parts = jnp.broadcast_to(block[None], (peers,) + block.shape)
    parts = lax.all_to_all(parts, ("dp", "col"), 0, 0, tiled=True)
    parts = parts.reshape((size, 2) + block.shape)

    def by_image(array):
        shaped = array.reshape(2, images, SEQ, width)
        return jnp.pad(shaped, ((0, 0), (0, 0), (0, PAD - SEQ), (0, 0)))

    same = row == col

    routes = chosen(expert_ids, col)
    gates = chosen(gate_values, col)
    slot = destinations(routes, capacity)
    unit = routes % local_experts * capacity + slot
    home = unit // share
    target = (routes // local_experts * 2 + home % 2) * held_rows + unit % share
    target = jnp.where(home // 2 == row, target, -1)

    def own_first(array, fill):
        shaped = array.reshape(2, images, SEQ, TOP)
        shaped = jnp.pad(
            shaped, ((0, 0), (0, 0), (0, PAD - SEQ), (0, 0)), constant_values=fill
        ).reshape(2, images * PAD, TOP)
        return jnp.where(row == 0, shaped, shaped[::-1])

    target = own_first(target, -1)
    gates = own_first(gates, 0)
    target_rows = target.transpose(0, 2, 1).reshape(2 * TOP, images * PAD)
    gate_rows = gates.transpose(0, 2, 1).reshape(2 * TOP, images * PAD)

    def by_chip(array, earlier):
        own = chosen(array, col)
        got = swap(after(chosen(array, 1 - col), earlier), "col")
        return either(same, own, got), either(same, got, own)

    kept, sent = by_chip(by_image(out_cotangent), ())
    kept = after(kept, target_rows, gate_rows)
    cot = in_order(row, jnp.stack([kept, sent]), swap(jnp.stack([sent, kept]), "row"), 3)
    kept, sent = by_chip(by_image(tokens_in), kept)
    x = in_order(row, kept, swap(after(sent, parts), "row"), 2)

    def exchange(slots):
        shaped = slots.reshape(peers, held_rows, D)
        return lax.all_to_all(shaped, ("dp", "col"), 0, 0, tiled=True).reshape(rows, D)

    def flat(array):
        return array.reshape(images * PAD, D)

    if local_experts == 1:
        where = jnp.stack([jnp.zeros_like(row), jnp.zeros_like(row), row])
    else:
        where = jnp.stack([2 * row + col, col, row])
    norms = jnp.stack([first_gain, first_shift, second_gain, second_shift])
    norms = in_order(row, norms, swap(norms, "row"), 1)
    we_got = other_core(expand_weight, row)
    wc_got = other_core(contract_weight, row)
    wc = other_chip(contract_weight, wc_got, row, col)
    we = other_chip(expand_weight, we_got, row, col)
    cot = after(cot, norms)
    grad_slots = dispatch(target_rows, gate_rows, flat(cot[0]), flat(cot[1]), rows, True)
    grad_slots = exchange(grad_slots)

    parts = [parts, swap(parts, "row")]
    here = jnp.stack([row, col])
    wq, wp, bq, bp = unpacked(here, parts)
    bias_rows = [part[:, :, 2 * D // size + 3 :].astype(F32)[:, :, None] for part in parts]
    bias_rows = in_order(row, *bias_rows, 2)

    def taken(start, like):
        count = like.size // width
        found = bias_rows[:, :, :, start : start + count]
        return found.reshape(found.shape[:3] + like.shape), start + count

    expert = place * local_experts + (2 * row + col) * local_experts // 4
    be, at = taken(0, expand_bias)
    be = chosen(be, expert // (EXPERTS // 2), 2)
    be = chosen(be, expert % (EXPERTS // 2), 2).transpose(1, 0, 2).reshape(2, -1)
    be = either(col == 0, be, be[::-1])
    bc, at = taken(at, contract_bias)
    bc = chosen(bc[:, 0], expert, 2).transpose(1, 0, 2).reshape(1, D)

    x = after(x, wc_got, we_got)
    low, middle, tri, att, lse = attention_forward(x, wq, bq, wp, bp, norms)
    low = flat(low)
    slots = dispatch(target_rows, gate_rows, low, swap(low, "row"), rows, False)
    slots = exchange(slots)
    gact = active_grad(where, grad_slots, wc, 0)
    where_slots = selection(target, rows)
    slots = after(slots, gact, where_slots)
    act, inner_grad, slot_grad = experts_middle(where, slots, gact, we, be, 0)
    gact = active_grad(where, after(grad_slots, slot_grad), wc, 1)
    act_far, inner_grad_far, slot_grad = experts_middle(
        where, slots, gact, we, be, 1, slot_grad
    )
    slot_grad = exchange(slot_grad)
    wc_grad_far, bc_grad = contract_grad(where, act_far, grad_slots)
    we_grad_far, be_grad_far = expand_grad(where, slots, inner_grad_far)
    wc_far, we_far = swap(wc_grad_far, "col"), swap(we_grad_far, "col")
    wc_grad, _ = contract_grad(where, after(act, we_grad_far, wc_grad_far), grad_slots)
    we_grad, be_grad = expand_grad(where, after(slots, we_grad_far, wc_grad_far), inner_grad)
    outer = experts_outer(where, (act, act_far), wc, bc)
    slot_grad = after(slot_grad, wc_grad, we_grad, outer)
    outer = exchange(after(outer, slot_grad))

    mine = (jnp.arange(EXPERTS, dtype=jnp.int32) == expert).astype(F32)
    be_grad = jnp.stack([be_grad, be_grad_far]).reshape(2, size, -1)
    be_grad = either(col == 0, be_grad, be_grad[::-1]).transpose(1, 0, 2)
    be_grad = mine.reshape(2, 1, 1, -1, 1) * be_grad[None, :, :, None, :]
    bc_grad = mine.reshape(1, 1, 1, -1, 1) * bc_grad.reshape(2, size, 1, 1, -1)
    bc_grad = jnp.broadcast_to(bc_grad, (2, size, 2) + bc_grad.shape[3:])
    extra = jnp.concatenate(
        [
            be_grad.reshape(2, size, 2, -1, width),
            bc_grad.reshape(2, size, 2, -1, width),
        ],
        3,
    )
    short = EXTRA - extra.shape[3]
    extra = jnp.pad(extra, ((0, 0),) * 3 + ((0, short), (0, 0))).astype(block_type(size))

    def to_image(array):
        return array.reshape(images, PAD, -1)

    got = swap(selected(where_slots, 1, slot_grad, BF16), "row")
    own = selected(where_slots, 0, slot_grad, F32)
    grad_kept, grad_sent, blocks = attention_backward(
        here, x, middle, cot[0], to_image(own), to_image(got), tri, att, lse, wq, wp, norms, extra
    )
    blocks = after(blocks.astype(BF16), we_far, wc_far)
    kept = chosen(blocks, row).astype(F32)
    blocks = (kept + swap(chosen(blocks, 1 - row), "row").astype(F32)).astype(BF16)
    kept = chosen(blocks, col, 1).astype(F32)
    blocks = (kept + swap(chosen(blocks, 1 - col, 1), "col").astype(F32)).astype(BF16)
    reduced = lax.all_to_all(after(blocks, outer), "dp", 0, 0, tiled=True)
    reduced = jnp.sum(reduced.astype(F32), axis=0)
    wc_grad = weight_grad(wc_grad, wc_far, row, col, local_experts)
    we_grad = weight_grad(we_grad, we_far, row, col, local_experts)
    outer = after(outer, wc_grad, we_grad)

    def to_tokens(kept, sent):
        got = swap(sent, "row")
        own, other = either(same, kept, got), either(same, got, kept)
        return own, swap(other, "col")

    def placed(own, other, dtype):
        both = in_order(col, own[None].astype(F32), other[None].astype(F32), 0)[:, :, :SEQ]
        return both.reshape(2, local_rows, width).astype(dtype)

    own_grad, far_grad = to_tokens(grad_kept, grad_sent)

    def out_half(half):
        kept, sent = combine(here, half, target, gates, outer, flat(middle))
        return to_image(kept.astype(F32) + swap(sent, "row").astype(F32))

    leaves = either(same, 1, 0)
    leaving = out_half(leaves).astype(BF16)
    other = swap(leaving, "col")
    input_grad = placed(own_grad, after(far_grad, leaving), F32)
    staying = out_half(1 - leaves)

    depth = qkv_weight.shape[0]
    out_wq = reduced[: 3 * depth].reshape(3, depth, width).transpose(1, 0, 2)
    out_wp = reduced[3 * depth : 4 * depth]
    be_rows = expand_bias.size // width
    out_be = reduced[4 * depth : 4 * depth + be_rows].reshape(expand_bias.shape)
    bc_rows = contract_bias.size // width
    out_bc = reduced[4 * depth + be_rows : 4 * depth + be_rows + bc_rows]
    out_bc = out_bc.reshape(contract_bias.shape)
    sums = reduced[4 * depth + EXTRA :].reshape(2, 8, width)
    norm_total = chosen(sums, row)
    out_bp = chosen(norm_total[4].reshape(size, -1), place)
    out_bq = chosen(chosen(sums, col)[5:7].reshape(2, size, -1), place, 1)
    other = after(other, out_wq, out_wp, out_be, out_bc, out_bq, out_bp, norm_total)
    layer_out = placed(staying, other, BF16)
    return (
        layer_out,
        input_grad,
        norm_total[0],
        norm_total[1],
        norm_total[2],
        norm_total[3],
        out_wq,
        out_bq,
        out_wp,
        out_bp,
        we_grad,
        out_be,
        wc_grad,
        out_bc,
    )


def solution(mesh):
    return jax.shard_map(
        on_device,
        mesh=mesh,
        in_specs=(
            P(None, ("dp", "col"), "row"),
            P(None, ("dp", "col"), "row"),
            P(None, "dp", None),
            P(None, "dp", None),
            P("row"),
            P("row"),
            P("row"),
            P("row"),
            P(("row", "dp"), None, "col"),
            P(None, ("col", "dp")),
            P(("col", "dp"), "row"),
            P(("row", "dp")),
            P("dp", "row", "col"),
            P("row", ("col", "dp")),
            P("dp", "col", "row"),
            P(None, ("row", "dp")),
        ),
        out_specs=(
            P(None, ("dp", "col"), "row"),
            P(None, ("dp", "col"), "row"),
            P("row"),
            P("row"),
            P("row"),
            P("row"),
            P(("row", "dp"), None, "col"),
            P(None, ("col", "dp")),
            P(("col", "dp"), "row"),
            P(("row", "dp")),
            P("dp", "row", "col"),
            P("row", ("col", "dp")),
            P("dp", "col", "row"),
            P(None, ("row", "dp")),
        ),
        check_vma=False,
    )
```

```python
import functools

import jax
import jax.numpy as jnp
from jax import lax
from jax.experimental import pallas as pl
from jax.experimental.pallas import tpu as pltpu
from jax.sharding import PartitionSpec as P

D = 512
HEADS = 8
EXPERTS = 32
TOP = 2
SEQ = 197
HEAD_DIM = D // HEADS
PAIR = 2 * HEAD_DIM
PAD = 208

EPS = 1e-06
HIGH = lax.Precision.HIGHEST
ROOT_HALF = 0.7071067811865476
DENSITY = 0.3989422804014327
SCALE = HEAD_DIM ** (-0.5)
FAR = -1e30
MIB = 1 << 20

BF16 = jnp.bfloat16
F32 = jnp.float32


def round_up(value, unit):
    return (value + unit - 1) // unit * unit


def swap(value, axis, bit=1):
    size = lax.axis_size(axis)
    return lax.ppermute(value, axis, [(place, place ^ bit) for place in range(size)])


def either(first, when_true, when_false):
    return jnp.where(first, when_true, when_false)


def in_order(index, own, other, axis):
    return jnp.where(
        index == 0,
        jnp.concatenate([own, other], axis),
        jnp.concatenate([other, own], axis),
    )


def chosen(array, index, axis=0):
    return lax.dynamic_index_in_dim(array, index, axis, keepdims=False)


def contract(left, right, left_dim, right_dim):
    return lax.dot_general(
        left, right, (((left_dim,), (right_dim,)), ((), ())), preferred_element_type=F32
    )


def after(value, *others):
    return lax.optimization_barrier((value,) + others)[0]


def call(
    kernel, micros, grid, in_specs, out_specs, out_shape, scratch=(), limit=48, scalars=0
):
    return pl.pallas_call(
        kernel,
        grid_spec=pltpu.PrefetchScalarGridSpec(
            num_scalar_prefetch=scalars,
            grid=grid,
            in_specs=in_specs,
            out_specs=out_specs,
            scratch_shapes=list(scratch),
        ),
        out_shape=out_shape,
        cost_estimate=pl.CostEstimate(
            flops=int(micros * 1e9), bytes_accessed=int(micros * 2e6), transcendentals=0
        ),
        compiler_params=pltpu.CompilerParams(
            dimension_semantics=("arbitrary",) * len(grid), vmem_limit_bytes=limit * MIB
        ),
    )


def whole(shape):
    return pl.BlockSpec(shape, lambda *_: (0,) * len(shape))


def stepped(shape, axis=0):
    return pl.BlockSpec(
        shape, lambda g, *_: tuple(g if place == axis else 0 for place in range(len(shape)))
    )


def destinations(routes, capacity):
    labels = jnp.arange(EXPERTS, dtype=jnp.int32)
    named = (routes[:, :, None] == labels).astype(F32)
    count = routes.shape[0]
    place = jnp.arange(count, dtype=jnp.int32)
    earlier = (place[None, :] < place[:, None]).astype(BF16)
    before = jnp.dot(earlier, named.sum(axis=1).astype(BF16), preferred_element_type=F32)
    return jnp.sum(before[:, None, :] * named, axis=2).astype(jnp.int32)


def dispatch_kernel(gated, target_ref, gate_ref, own_ref, other_ref, out_ref):
    rows = out_ref.shape[0]
    count = own_ref.shape[0]
    place = lax.broadcasted_iota(jnp.int32, (rows, count), 0) + pl.program_id(0) * rows
    total = None
    for half, tokens in ((0, own_ref), (1, other_ref)):
        first = place == target_ref[2 * half : 2 * half + 1, :]
        second = place == target_ref[2 * half + 1 : 2 * half + 2, :]
        if gated:
            weight = jnp.where(
                first,
                gate_ref[2 * half : 2 * half + 1, :],
                jnp.where(second, gate_ref[2 * half + 1 : 2 * half + 2, :], 0.0),
            )
        else:
            weight = jnp.where(first | second, 1.0, 0.0)
        term = jnp.dot(weight.astype(BF16), tokens[...], preferred_element_type=F32)
        total = term if total is None else total + term
    out_ref[...] = total.astype(BF16)


def dispatch(target_rows, gate_rows, own, other, rows, gated):
    steps = 4
    return call(
        functools.partial(dispatch_kernel, gated),
        5,
        (steps,),
        [whole(target_rows.shape), whole(gate_rows.shape), whole(own.shape), whole(other.shape)],
        stepped((rows // steps, D)),
        pltpu.HBM((rows, D), BF16),
    )(target_rows, gate_rows, own, other)


def combined(target_ref, gate_ref, slots_ref):
    count, rows = target_ref.shape[1], slots_ref.shape[0]
    place = lax.broadcasted_iota(jnp.int32, (count, rows), 1)
    first = place == target_ref[0, :, 0:1]
    second = place == target_ref[0, :, 1:2]
    weight = jnp.where(first, gate_ref[0, :, 0:1], jnp.where(second, gate_ref[0, :, 1:2], 0.0))
    return jnp.dot(weight.astype(BF16), slots_ref[...], preferred_element_type=F32)


def selection_kernel(target_ref, out_ref):
    place = lax.broadcasted_iota(jnp.int32, out_ref.shape[1:], 1)
    first = place == target_ref[0, :, 0:1]
    second = place == target_ref[0, :, 1:2]
    out_ref[0] = jnp.where(first | second, 1.0, 0.0).astype(BF16)


def selection(target, rows):
    steps = 4
    count = 2 * target.shape[1] // steps
    return call(
        selection_kernel,
        8,
        (steps,),
        [pl.BlockSpec((1, count, TOP), lambda g: (g // 2, g % 2, 0))],
        pl.BlockSpec((1, count, rows), lambda g: (g // 2, g % 2, 0)),
        jax.ShapeDtypeStruct((2, target.shape[1], rows), BF16),
    )(target)


def select_kernel(chosen_ref, slots_ref, out_ref):
    out = jnp.dot(chosen_ref[0], slots_ref[...], preferred_element_type=F32)
    out_ref[...] = out.astype(out_ref.dtype)


def selected(selection, half, slots, dtype):
    steps = 2
    rows = selection.shape[1] // steps
    return call(
        select_kernel,
        3,
        (steps,),
        [
            pl.BlockSpec((1, rows, selection.shape[2]), lambda g: (half, g, 0)),
            whole(slots.shape),
        ],
        stepped((rows, D)),
        jax.ShapeDtypeStruct((selection.shape[1], D), dtype),
    )(selection, slots)


def combine_out_kernel(
    place_ref, target_ref, gate_ref, slots_ref, middle_ref, kept_ref, sent_ref
):
    out = combined(target_ref, gate_ref, slots_ref)
    out = jnp.where(place_ref[1] == 0, out + middle_ref[...], out)
    kept_ref[...], sent_ref[...] = feature_halves(place_ref, out.astype(BF16))


def feature_halves(place_ref, value):
    half = value.shape[-1] // 2
    low, high = value[..., :half], value[..., half:]
    first = place_ref[0] == 0
    return jnp.where(first, low, high), jnp.where(first, high, low)


def combine(place, half, target, gates, slots, middle):
    steps = 2
    count = target.shape[1]
    column = pl.BlockSpec((1, count // steps, TOP), lambda g, place: (place[1], g, 0))
    return call(
        combine_out_kernel,
        5,
        (steps,),
        [column, column, whole(slots.shape), stepped((count // steps, D))],
        [stepped((count // steps, D // 2))] * 2,
        [jax.ShapeDtypeStruct((count, D // 2), BF16)] * 2,
        scalars=1,
    )(jnp.stack([place[0], half]), target, gates, slots, middle)


def block_type(size):
    return BF16 if D // (2 * size) % 16 == 0 else F32


EXTRA = 16


def unpack_kernel(place_ref, own_ref, other_ref, wq_ref, wp_ref, bq_ref, bp_ref):
    size = own_ref.shape[0]
    depth, half = D // (2 * size), D // 2
    row = place_ref[0]
    bq_ref[:, D : 2 * D] = jnp.zeros((1, D), F32)
    for ref, r in ((own_ref, row), (other_ref, 1 - row)):
        at_r = pl.multiple_of(r * half, half)
        for c in range(2):
            at_c = c * half
            biases = jnp.sum(ref[:, c, 4 * depth : 4 * depth + EXTRA, :].astype(F32), axis=0)
            bq_ref[:, at_c : at_c + half] = biases[0:1]
            bq_ref[:, 2 * D + at_c : 2 * D + at_c + half] = biases[1:2]
            bp_ref[:, pl.ds(at_r, half)] = biases[2:3]
            for dp in range(size):
                rows = pl.ds(pl.multiple_of(r * half + dp * depth, depth), depth)
                for part in range(3):
                    at = part * D + at_c
                    wq_ref[rows, at : at + half] = ref[dp, c, part * depth : (part + 1) * depth, :]
                rows = slice(at_c + dp * depth, at_c + (dp + 1) * depth)
                wp_ref[rows, pl.ds(at_r, half)] = ref[dp, c, 3 * depth : 4 * depth, :]


def unpacked(place, parts):
    kind = block_type(parts[0].shape[0])
    shapes = [(D, 3 * D), (D, D), (1, 3 * D), (1, D)]
    wq, wp, bq, bp = call(
        unpack_kernel,
        2,
        (1,),
        [whole(part.shape) for part in parts],
        [whole(shape) for shape in shapes],
        [jax.ShapeDtypeStruct(shape, t) for shape, t in zip(shapes, (kind, kind, F32, F32))],
        scalars=1,
    )(place, *[part.astype(kind) for part in parts])
    return wq.astype(BF16), wp.astype(BF16), bq, bp


def normalized(value):
    center = jnp.mean(value, axis=-1, keepdims=True)
    spread = jnp.mean(value * value, axis=-1, keepdims=True) - center * center
    factor = lax.rsqrt(spread + EPS)
    return (value - center) * factor, factor


def norm_back(grad, scaled, factor, gain):
    upper = grad * gain
    return factor * (
        upper
        - jnp.mean(upper, axis=-1, keepdims=True)
        - scaled * jnp.mean(upper * scaled, axis=-1, keepdims=True)
    )


def forward_kernel(
    x_ref,
    wq_ref,
    bq_ref,
    wp_ref,
    bp_ref,
    norm_ref,
    low_ref,
    mid_ref,
    tri_ref,
    att_ref,
    lse_ref,
):
    x = x_ref[0].astype(F32)
    scaled, _ = normalized(x)
    low = (scaled * norm_ref[0:1, :] + norm_ref[1:2, :]).astype(BF16)
    tri = jnp.dot(low, wq_ref[...], preferred_element_type=F32) + bq_ref[...]
    tri_ref[0] = tri.astype(BF16)
    lane = lax.broadcasted_iota(jnp.int32, (PAD, PAIR), 1)
    shut = lax.broadcasted_iota(jnp.int32, (PAD, PAD), 1) >= SEQ
    logs = jnp.zeros((PAD, 128), F32)
    column = lax.broadcasted_iota(jnp.int32, (PAD, 128), 1)
    for pair in range(HEADS // 2):
        at = pair * PAIR
        query = tri_ref[0, :, at : at + PAIR]
        keys = tri_ref[0, :, D + at : D + at + PAIR]
        values = tri_ref[0, :, 2 * D + at : 2 * D + at + PAIR]
        outs = []
        for side in range(2):
            mine = (lane // HEAD_DIM) == side
            scores = contract(jnp.where(mine, query, jnp.zeros_like(query)), keys, 1, 1) * SCALE
            scores = jnp.where(shut, FAR, scores)
            peak = jnp.max(scores, axis=-1, keepdims=True)
            expo = jnp.exp(scores - peak)
            total = jnp.sum(expo, axis=-1, keepdims=True)
            prob = (expo / total).astype(BF16)
            outs.append(jnp.dot(prob, values, preferred_element_type=F32))
            logs = jnp.where(column == 2 * pair + side, peak + jnp.log(total), logs)
        att_ref[0, :, at : at + PAIR] = jnp.where(lane < HEAD_DIM, outs[0], outs[1]).astype(BF16)
    lse_ref[0] = logs
    branch = jnp.dot(att_ref[0], wp_ref[...], preferred_element_type=F32) + bp_ref[...]
    middle = x + branch
    mid_ref[0] = middle
    scaled2, _ = normalized(middle)
    low_ref[0] = (scaled2 * norm_ref[2:3, :] + norm_ref[3:4, :]).astype(BF16)


def attention_forward(x, wq, bq, wp, bp, norms):
    images = x.shape[0]
    return call(
        forward_kernel,
        9,
        (images,),
        [
            stepped((1, PAD, D)),
            whole(wq.shape),
            whole(bq.shape),
            whole(wp.shape),
            whole(bp.shape),
            whole(norms.shape),
        ],
        [
            stepped((1, PAD, D)),
            stepped((1, PAD, D)),
            stepped((1, PAD, 3 * D)),
            stepped((1, PAD, D)),
            stepped((1, PAD, 128)),
        ],
        [
            jax.ShapeDtypeStruct((images, PAD, D), BF16),
            jax.ShapeDtypeStruct((images, PAD, D), F32),
            jax.ShapeDtypeStruct((images, PAD, 3 * D), BF16),
            jax.ShapeDtypeStruct((images, PAD, D), BF16),
            jax.ShapeDtypeStruct((images, PAD, 128), F32),
        ],
    )(x, wq, bq, wp, bp, norms)


def backward_kernel(
    place_ref,
    x_ref,
    mid_ref,
    cot_ref,
    own_ref,
    got_ref,
    tri_ref,
    att_ref,
    lse_ref,
    wq_ref,
    wp_ref,
    norm_ref,
    extra_ref,
    kept_ref,
    sent_ref,
    blocks_ref,
    sums_ref,
    dwq_ref,
    dwp_ref,
    tg_ref,
):
    @pl.when(pl.program_id(0) == 0)
    def _():
        dwq_ref[...] = jnp.zeros_like(dwq_ref)
        dwp_ref[...] = jnp.zeros_like(dwp_ref)
        sums_ref[...] = jnp.zeros_like(sums_ref)

    low_grad = own_ref[0] + got_ref[0].astype(F32)
    scaled2, factor2 = normalized(mid_ref[0])
    sums_ref[2:3, :] += jnp.sum(low_grad * scaled2, axis=0, keepdims=True)
    sums_ref[3:4, :] += jnp.sum(low_grad, axis=0, keepdims=True)
    mid_grad = cot_ref[0].astype(F32) + norm_back(low_grad, scaled2, factor2, norm_ref[2:3, :])
    branch = mid_grad.astype(BF16)
    sums_ref[4:5, :] += jnp.sum(branch.astype(F32), axis=0, keepdims=True)
    dwp_ref[...] += contract(att_ref[0], branch, 0, 0)
    att_grad = contract(branch, wp_ref[...], 1, 1).astype(BF16)
    lane = lax.broadcasted_iota(jnp.int32, (PAD, PAIR), 1)
    shut = lax.broadcasted_iota(jnp.int32, (PAD, PAD), 1) >= SEQ
    for pair in range(HEADS // 2):
        at = pair * PAIR
        query = tri_ref[0, :, at : at + PAIR]
        keys = tri_ref[0, :, D + at : D + at + PAIR]
        values = tri_ref[0, :, 2 * D + at : 2 * D + at + PAIR]
        upstream = att_grad[:, at : at + PAIR]
        query_grads = []
        key_grad = jnp.zeros((PAD, PAIR), F32)
        value_grad = jnp.zeros((PAD, PAIR), F32)
        for side in range(2):
            mine = (lane // HEAD_DIM) == side
            query_one = jnp.where(mine, query, jnp.zeros_like(query))
            grad_one = jnp.where(mine, upstream, jnp.zeros_like(upstream))
            scores = contract(query_one, keys, 1, 1) * SCALE
            scores = jnp.where(shut, FAR, scores)
            head = 2 * pair + side
            prob = jnp.exp(scores - lse_ref[0, :, head : head + 1])
            prob_grad = contract(grad_one, values, 1, 1)
            value_grad += contract(prob.astype(BF16), grad_one, 0, 0)
            inside = jnp.sum(prob * prob_grad, axis=-1, keepdims=True)
            score_grad = (prob * (prob_grad - inside)).astype(BF16)
            query_grads.append(jnp.dot(score_grad, keys, preferred_element_type=F32))
            key_grad += contract(score_grad, query_one, 0, 0)
        query_grad = jnp.where(lane < HEAD_DIM, query_grads[0], query_grads[1])
        tg_ref[:, at : at + PAIR] = (query_grad * SCALE).astype(BF16)
        tg_ref[:, D + at : D + at + PAIR] = (key_grad * SCALE).astype(BF16)
        tg_ref[:, 2 * D + at : 2 * D + at + PAIR] = value_grad.astype(BF16)
    tri_grad = tg_ref[...]
    sums_ref[5:6, :] += jnp.sum(tri_grad[:, :D].astype(F32), axis=0, keepdims=True)
    sums_ref[6:7, :] += jnp.sum(tri_grad[:, 2 * D :].astype(F32), axis=0, keepdims=True)
    scaled, factor = normalized(x_ref[0].astype(F32))
    low = (scaled * norm_ref[0:1, :] + norm_ref[1:2, :]).astype(BF16)
    dwq_ref[...] += contract(low, tri_grad, 0, 0)
    normed_grad = contract(tri_grad, wq_ref[...], 1, 1)
    sums_ref[0:1, :] += jnp.sum(normed_grad * scaled, axis=0, keepdims=True)
    sums_ref[1:2, :] += jnp.sum(normed_grad, axis=0, keepdims=True)
    grad = mid_grad + norm_back(normed_grad, scaled, factor, norm_ref[0:1, :])
    kept_ref[0], sent_ref[0] = feature_halves(place_ref, grad.astype(BF16))

    @pl.when(pl.program_id(0) == pl.num_programs(0) - 1)
    def _():
        size = blocks_ref.shape[1]
        depth, half, kind = D // (2 * size), D // 2, blocks_ref.dtype
        sums = jnp.concatenate([sums_ref[:, :half], sums_ref[:, half:]], 0).astype(kind)
        blocks_ref[:, :, :, 4 * depth : 4 * depth + EXTRA, :] = extra_ref[...]
        for row in range(2):
            for dp in range(size):
                for col in range(2):
                    block = blocks_ref.at[row, dp, col]
                    rows = slice(row * half + dp * depth, row * half + (dp + 1) * depth)
                    for part in range(3):
                        at = part * D + col * half
                        block[part * depth : (part + 1) * depth, :] = dwq_ref[
                            rows, at : at + half
                        ].astype(kind)
                    rows = slice(col * half + dp * depth, col * half + (dp + 1) * depth)
                    block[3 * depth : 4 * depth, :] = dwp_ref[
                        rows, row * half : (row + 1) * half
                    ].astype(kind)
                    block[4 * depth + EXTRA :, :] = sums


def attention_backward(place, x, middle, cot, own, got, tri, att, lse, wq, wp, norms, extra):
    images = x.shape[0]
    size = extra.shape[1]
    blocks = (2, size, 2, 2 * D // size + EXTRA + 16, D // 2)
    return call(
        backward_kernel,
        21,
        (images,),
        [
            stepped((1, PAD, D)),
            stepped((1, PAD, D)),
            stepped((1, PAD, D)),
            stepped((1, PAD, D)),
            stepped((1, PAD, D)),
            stepped((1, PAD, 3 * D)),
            stepped((1, PAD, D)),
            stepped((1, PAD, 128)),
            whole(wq.shape),
            whole(wp.shape),
            whole(norms.shape),
            whole(extra.shape),
        ],
        [
            stepped((1, PAD, D // 2)),
            stepped((1, PAD, D // 2)),
            whole(blocks),
        ],
        [
            jax.ShapeDtypeStruct((images, PAD, D // 2), BF16),
            jax.ShapeDtypeStruct((images, PAD, D // 2), BF16),
            jax.ShapeDtypeStruct(blocks, block_type(size)),
        ],
        scratch=[
            pltpu.VMEM((8, D), F32),
            pltpu.VMEM((D, 3 * D), F32),
            pltpu.VMEM((D, D), F32),
            pltpu.VMEM((PAD, 3 * D), BF16),
        ],
        scalars=1,
    )(place, x, middle, cot, own, got, tri, att, lse, wq, wp, norms, extra)


STEPS = 4


def own_first(place_ref, value):
    half = value.shape[-1] // 2
    low, high = value[..., :half], value[..., half:]
    first = place_ref[2] == 0
    return jnp.concatenate([jnp.where(first, low, high), jnp.where(first, high, low)], -1)


def active_grad_kernel(place_ref, grad_ref, own_ref, other_ref, out_ref):
    weight = jnp.concatenate([own_ref[0], other_ref[0]], 1)
    out_ref[...] = contract(own_first(place_ref, grad_ref[...]), weight, 1, 1).astype(BF16)


def expert_kernel(place_ref, slots_ref, gact_ref, own_ref, other_ref, be_ref, *refs):
    *before, act_ref, inner_grad_ref, slot_grad_ref = refs
    weight = jnp.concatenate([own_ref[0], other_ref[0]], 0)
    tokens = own_first(place_ref, slots_ref[...])
    inner = jnp.dot(tokens, weight, preferred_element_type=F32) + be_ref[...]
    share = 0.5 * (1.0 + lax.erf(inner * ROOT_HALF))
    act_ref[...] = (inner * share).astype(BF16)
    slope = share + inner * (DENSITY * jnp.exp(-0.5 * inner * inner))
    grad = (gact_ref[...].astype(F32) * slope).astype(BF16)
    inner_grad_ref[...] = grad
    total = own_first(place_ref, contract(grad, weight, 1, 1))
    for ref in before:
        total += ref[...].astype(F32)
    slot_grad_ref[...] = total.astype(BF16)


def outer_kernel(place_ref, act0_ref, act1_ref, wc0_ref, wc1_ref, wc2_ref, wc3_ref, bc_ref, out_ref):
    total = jnp.dot(
        act0_ref[...], jnp.concatenate([wc0_ref[0], wc1_ref[0]], 1), preferred_element_type=F32
    )
    total += jnp.dot(
        act1_ref[...], jnp.concatenate([wc2_ref[0], wc3_ref[0]], 1), preferred_element_type=F32
    )
    out_ref[...] = (own_first(place_ref, total) + bc_ref[...]).astype(BF16)


def contract_grad_kernel(place_ref, act_ref, grad_ref, out_ref, bias_ref):
    product = contract(act_ref[...], grad_ref[...], 0, 0).astype(BF16)
    half = product.shape[1] // 2
    low, high = product[:, :half], product[:, half:]
    out_ref[0] = jnp.where(place_ref[2] == 0, low, high)
    out_ref[1] = jnp.where(place_ref[2] == 0, high, low)

    @pl.when(pl.program_id(0) == 0)
    def _():
        bias_ref[...] = jnp.sum(grad_ref[...].astype(F32), axis=0, keepdims=True)


def expand_grad_kernel(place_ref, slots_ref, grad_ref, out_ref, bias_ref):
    product = contract(slots_ref[...], grad_ref[...], 0, 0).astype(BF16)
    half = product.shape[0] // 2
    low, high = product[:half], product[half:]
    out_ref[0] = jnp.where(place_ref[2] == 0, low, high)
    out_ref[1] = jnp.where(place_ref[2] == 0, high, low)
    bias_ref[...] = jnp.sum(grad_ref[...].astype(F32), axis=0, keepdims=True)


def weight_specs(pieces, half):
    shape = (1,) + pieces[0].shape[1:]
    places = [lambda g, place: (place[0], 0, 0), lambda g, place: (place[1], 0, 0)]
    if half:
        places = [lambda g, place: (0, 0, 0)] * 2
    return [pl.BlockSpec(shape, place) for place in places]


def active_grad(place, grad_slots, wc, half):
    rows, hidden = grad_slots.shape[0], wc[0].shape[1]
    return call(
        active_grad_kernel,
        5,
        (STEPS,),
        [stepped((rows // STEPS, D))] + weight_specs(wc, half),
        stepped((rows // STEPS, hidden)),
        jax.ShapeDtypeStruct((rows, hidden), BF16),
        scalars=1,
    )(place, grad_slots, *wc[2 * half : 2 * half + 2])


def experts_middle(place, slots, gact, we, be, half, *before):
    rows, hidden = gact.shape
    return call(
        expert_kernel,
        11,
        (STEPS,),
        [stepped((rows // STEPS, D)), stepped((rows // STEPS, hidden))]
        + weight_specs(we, half)
        + [whole((1, hidden))]
        + [stepped((rows // STEPS, D))] * len(before),
        [
            stepped((rows // STEPS, hidden)),
            stepped((rows // STEPS, hidden)),
            stepped((rows // STEPS, D)),
        ],
        [
            jax.ShapeDtypeStruct((rows, hidden), BF16),
            jax.ShapeDtypeStruct((rows, hidden), BF16),
            pltpu.HBM((rows, D), BF16),
        ],
        scalars=1,
    )(place, slots, gact, *we[2 * half : 2 * half + 2], be[half : half + 1], *before)


def experts_outer(place, acts, wc, bc):
    rows, hidden = acts[0].shape
    return call(
        outer_kernel,
        9,
        (STEPS,),
        [stepped((rows // STEPS, hidden))] * 2
        + weight_specs(wc, 0)
        + weight_specs(wc, 1)
        + [whole(bc.shape)],
        stepped((rows // STEPS, D)),
        pltpu.HBM((rows, D), BF16),
        scalars=1,
    )(place, *acts, *wc, bc)


def contract_grad(place, act, grad_slots):
    rows, hidden = act.shape
    chunk = hidden // 2
    return call(
        contract_grad_kernel,
        5,
        (2,),
        [stepped((rows, chunk), 1), whole(grad_slots.shape)],
        [stepped((2, chunk, D // 2), 1), whole((1, D))],
        [
            jax.ShapeDtypeStruct((2, hidden, D // 2), BF16),
            jax.ShapeDtypeStruct((1, D), F32),
        ],
        scalars=1,
    )(place, act, grad_slots)


def expand_grad(place, slots, inner_grad):
    rows, hidden = inner_grad.shape
    chunk = hidden // 2
    return call(
        expand_grad_kernel,
        5,
        (2,),
        [whole(slots.shape), stepped((rows, chunk), 1)],
        [stepped((2, D // 2, chunk), 2), stepped((1, chunk), 1)],
        [
            jax.ShapeDtypeStruct((2, D // 2, hidden), BF16),
            jax.ShapeDtypeStruct((1, hidden), F32),
        ],
        scalars=1,
    )(place, slots, inner_grad)


def other_core(block, row):
    if block.shape[0] == 1:
        return swap(block, "row")
    return swap(lax.dynamic_slice_in_dim(block, 2 * (1 - row), 2, 0), "row")


def other_chip(block, got, row, col, earlier=()):
    own, other = block, got
    if block.shape[0] > 1:
        own = lax.dynamic_slice_in_dim(own, 2 * row + 1 - col, 1, 0)
        other = lax.dynamic_slice_in_dim(other, 1 - col, 1, 0)
    own = swap(own, "col")
    return block, got, own, swap(after(other, earlier), "col")


def assemble_kernel(place_ref, *refs):
    for step, ref in enumerate(refs[:4]):

        @pl.when(pl.program_id(0) == step)
        def _(ref=ref):
            refs[4][0] = ref[...].astype(F32)


def grad_block(pieces, row, col):
    shape = pieces[0].shape
    order = jnp.stack([2 * row + col, 2 * row + 1 - col, 2 * (1 - row) + col, 3 - 2 * row - col])
    return call(
        assemble_kernel,
        4,
        (4,),
        [whole(shape)] * 4,
        pl.BlockSpec((1,) + shape, lambda g, order: (order[g], 0, 0)),
        jax.ShapeDtypeStruct((4,) + shape, F32),
        scalars=1,
    )(order, *pieces)


def weight_grad(grad, far, row, col, experts):
    if experts == 1:
        own, near = (grad[side].astype(F32) + far[side].astype(F32) for side in range(2))
        return (own + swap(near.astype(BF16), "row").astype(F32))[None]
    return grad_block((grad[0], far[0], swap(grad[1], "row"), swap(far[1], "row")), row, col)


def as_rows(value, width):
    flat = value.reshape(-1)
    return jnp.pad(flat, (0, round_up(flat.shape[0], width) - flat.shape[0])).reshape(-1, width)


def on_device(
    tokens_in,
    out_cotangent,
    expert_ids,
    gate_values,
    first_gain,
    first_shift,
    second_gain,
    second_shift,
    qkv_weight,
    qkv_bias,
    proj_weight,
    proj_bias,
    expand_weight,
    expand_bias,
    contract_weight,
    contract_bias,
):
    size = lax.axis_size("dp")
    row, col, place = lax.axis_index("row"), lax.axis_index("col"), lax.axis_index("dp")
    local_rows, width = tokens_in.shape[1:]
    group = expert_ids.shape[1]
    images = local_rows // SEQ
    capacity = (group * TOP * 4 + 3 * EXPERTS - 1) // (3 * EXPERTS)
    local_experts = EXPERTS // size
    share = local_experts * capacity // 4
    held_rows = round_up(share, 8)
    peers = 2 * size
    rows = peers * held_rows

    def at_place(array):
        mine = (jnp.arange(size, dtype=jnp.int32) == place).astype(F32)
        return (mine[None, :, None] * array[:, None, :]).reshape(-1, width)

    biases = jnp.concatenate(
        [
            at_place(qkv_bias),
            at_place(proj_bias[None]),
            expand_bias.reshape(-1, width),
            contract_bias.reshape(-1, width),
        ],
        0,
    )
    biases = jnp.pad(biases, ((0, EXTRA - biases.shape[0]), (0, 0)))
    block = jnp.concatenate(
        [qkv_weight.transpose(1, 0, 2).reshape(-1, width), proj_weight, biases.astype(BF16)], 0
    )
    parts = jnp.broadcast_to(block[None], (peers,) + block.shape)
    parts = lax.all_to_all(parts, ("dp", "col"), 0, 0, tiled=True)
    parts = parts.reshape((size, 2) + block.shape)

    def by_image(array):
        shaped = array.reshape(2, images, SEQ, width)
        return jnp.pad(shaped, ((0, 0), (0, 0), (0, PAD - SEQ), (0, 0)))

    same = row == col

    routes = chosen(expert_ids, col)
    gates = chosen(gate_values, col)
    slot = destinations(routes, capacity)
    unit = routes % local_experts * capacity + slot
    home = unit // share
    target = (routes // local_experts * 2 + home % 2) * held_rows + unit % share
    target = jnp.where(home // 2 == row, target, -1)

    def own_first(array, fill):
        shaped = array.reshape(2, images, SEQ, TOP)
        shaped = jnp.pad(
            shaped, ((0, 0), (0, 0), (0, PAD - SEQ), (0, 0)), constant_values=fill
        ).reshape(2, images * PAD, TOP)
        return jnp.where(row == 0, shaped, shaped[::-1])

    target = own_first(target, -1)
    gates = own_first(gates, 0)
    target_rows = target.transpose(0, 2, 1).reshape(2 * TOP, images * PAD)
    gate_rows = gates.transpose(0, 2, 1).reshape(2 * TOP, images * PAD)

    def by_chip(array, earlier):
        own = chosen(array, col)
        got = swap(after(chosen(array, 1 - col), earlier), "col")
        return either(same, own, got), either(same, got, own)

    kept, sent = by_chip(by_image(out_cotangent), ())
    kept = after(kept, target_rows, gate_rows)
    cot = in_order(row, jnp.stack([kept, sent]), swap(jnp.stack([sent, kept]), "row"), 3)
    kept, sent = by_chip(by_image(tokens_in), kept)
    x = in_order(row, kept, swap(after(sent, parts), "row"), 2)

    def exchange(slots):
        shaped = slots.reshape(peers, held_rows, D)
        return lax.all_to_all(shaped, ("dp", "col"), 0, 0, tiled=True).reshape(rows, D)

    def flat(array):
        return array.reshape(images * PAD, D)

    if local_experts == 1:
        where = jnp.stack([jnp.zeros_like(row), jnp.zeros_like(row), row])
    else:
        where = jnp.stack([2 * row + col, col, row])
    norms = jnp.stack([first_gain, first_shift, second_gain, second_shift])
    norms = in_order(row, norms, swap(norms, "row"), 1)
    we_got = other_core(expand_weight, row)
    wc_got = other_core(contract_weight, row)
    wc = other_chip(contract_weight, wc_got, row, col)
    we = other_chip(expand_weight, we_got, row, col)
    cot = after(cot, norms)
    grad_slots = dispatch(target_rows, gate_rows, flat(cot[0]), flat(cot[1]), rows, True)
    grad_slots = exchange(grad_slots)

    parts = [parts, swap(parts, "row")]
    here = jnp.stack([row, col])
    wq, wp, bq, bp = unpacked(here, parts)
    bias_rows = [part[:, :, 2 * D // size + 3 :].astype(F32)[:, :, None] for part in parts]
    bias_rows = in_order(row, *bias_rows, 2)

    def taken(start, like):
        count = like.size // width
        found = bias_rows[:, :, :, start : start + count]
        return found.reshape(found.shape[:3] + like.shape), start + count

    expert = place * local_experts + (2 * row + col) * local_experts // 4
    be, at = taken(0, expand_bias)
    be = chosen(be, expert // (EXPERTS // 2), 2)
    be = chosen(be, expert % (EXPERTS // 2), 2).transpose(1, 0, 2).reshape(2, -1)
    be = either(col == 0, be, be[::-1])
    bc, at = taken(at, contract_bias)
    bc = chosen(bc[:, 0], expert, 2).transpose(1, 0, 2).reshape(1, D)

    x = after(x, wc_got, we_got)
    low, middle, tri, att, lse = attention_forward(x, wq, bq, wp, bp, norms)
    low = flat(low)
    slots = dispatch(target_rows, gate_rows, low, swap(low, "row"), rows, False)
    slots = exchange(slots)
    gact = active_grad(where, grad_slots, wc, 0)
    where_slots = selection(target, rows)
    slots = after(slots, gact, where_slots)
    act, inner_grad, slot_grad = experts_middle(where, slots, gact, we, be, 0)
    gact = active_grad(where, after(grad_slots, slot_grad), wc, 1)
    act_far, inner_grad_far, slot_grad = experts_middle(
        where, slots, gact, we, be, 1, slot_grad
    )
    slot_grad = exchange(slot_grad)
    wc_grad_far, bc_grad = contract_grad(where, act_far, grad_slots)
    we_grad_far, be_grad_far = expand_grad(where, slots, inner_grad_far)
    wc_far, we_far = swap(wc_grad_far, "col"), swap(we_grad_far, "col")
    wc_grad, _ = contract_grad(where, after(act, we_grad_far, wc_grad_far), grad_slots)
    we_grad, be_grad = expand_grad(where, after(slots, we_grad_far, wc_grad_far), inner_grad)
    outer = experts_outer(where, (act, act_far), wc, bc)
    slot_grad = after(slot_grad, wc_grad, we_grad, outer)
    outer = exchange(after(outer, slot_grad))

    mine = (jnp.arange(EXPERTS, dtype=jnp.int32) == expert).astype(F32)
    be_grad = jnp.stack([be_grad, be_grad_far]).reshape(2, size, -1)
    be_grad = either(col == 0, be_grad, be_grad[::-1]).transpose(1, 0, 2)
    be_grad = mine.reshape(2, 1, 1, -1, 1) * be_grad[None, :, :, None, :]
    bc_grad = mine.reshape(1, 1, 1, -1, 1) * bc_grad.reshape(2, size, 1, 1, -1)
    bc_grad = jnp.broadcast_to(bc_grad, (2, size, 2) + bc_grad.shape[3:])
    extra = jnp.concatenate(
        [
            be_grad.reshape(2, size, 2, -1, width),
            bc_grad.reshape(2, size, 2, -1, width),
        ],
        3,
    )
    short = EXTRA - extra.shape[3]
    extra = jnp.pad(extra, ((0, 0),) * 3 + ((0, short), (0, 0))).astype(block_type(size))

    def to_image(array):
        return array.reshape(images, PAD, -1)

    got = swap(selected(where_slots, 1, slot_grad, BF16), "row")
    own = selected(where_slots, 0, slot_grad, F32)
    grad_kept, grad_sent, blocks = attention_backward(
        here, x, middle, cot[0], to_image(own), to_image(got), tri, att, lse, wq, wp, norms, extra
    )
    blocks = after(blocks.astype(BF16), we_far, wc_far)
    kept = chosen(blocks, row).astype(F32)
    blocks = (kept + swap(chosen(blocks, 1 - row), "row").astype(F32)).astype(BF16)
    kept = chosen(blocks, col, 1).astype(F32)
    blocks = (kept + swap(chosen(blocks, 1 - col, 1), "col").astype(F32)).astype(BF16)
    reduced = lax.all_to_all(after(blocks, outer), "dp", 0, 0, tiled=True)
    reduced = jnp.sum(reduced.astype(F32), axis=0)
    wc_grad = weight_grad(wc_grad, wc_far, row, col, local_experts)
    we_grad = weight_grad(we_grad, we_far, row, col, local_experts)
    outer = after(outer, wc_grad, we_grad)

    def to_tokens(kept, sent):
        got = swap(sent, "row")
        own, other = either(same, kept, got), either(same, got, kept)
        return own, swap(other, "col")

    def placed(own, other, dtype):
        both = in_order(col, own[None].astype(F32), other[None].astype(F32), 0)[:, :, :SEQ]
        return both.reshape(2, local_rows, width).astype(dtype)

    own_grad, far_grad = to_tokens(grad_kept, grad_sent)

    def out_half(half):
        kept, sent = combine(here, half, target, gates, outer, flat(middle))
        return to_image(kept.astype(F32) + swap(sent, "row").astype(F32))

    leaves = either(same, 1, 0)
    leaving = out_half(leaves).astype(BF16)
    other = swap(leaving, "col")
    input_grad = placed(own_grad, after(far_grad, leaving), F32)
    staying = out_half(1 - leaves)

    depth = qkv_weight.shape[0]
    out_wq = reduced[: 3 * depth].reshape(3, depth, width).transpose(1, 0, 2)
    out_wp = reduced[3 * depth : 4 * depth]
    be_rows = expand_bias.size // width
    out_be = reduced[4 * depth : 4 * depth + be_rows].reshape(expand_bias.shape)
    bc_rows = contract_bias.size // width
    out_bc = reduced[4 * depth + be_rows : 4 * depth + be_rows + bc_rows]
    out_bc = out_bc.reshape(contract_bias.shape)
    sums = reduced[4 * depth + EXTRA :].reshape(2, 8, width)
    norm_total = chosen(sums, row)
    out_bp = chosen(norm_total[4].reshape(size, -1), place)
    out_bq = chosen(chosen(sums, col)[5:7].reshape(2, size, -1), place, 1)
    other = after(other, out_wq, out_wp, out_be, out_bc, out_bq, out_bp, norm_total)
    layer_out = placed(staying, other, BF16)
    return (
        layer_out,
        input_grad,
        norm_total[0],
        norm_total[1],
        norm_total[2],
        norm_total[3],
        out_wq,
        out_bq,
        out_wp,
        out_bp,
        we_grad,
        out_be,
        wc_grad,
        out_bc,
    )


def solution(mesh):
    return jax.shard_map(
        on_device,
        mesh=mesh,
        in_specs=(
            P(None, ("dp", "col"), "row"),
            P(None, ("dp", "col"), "row"),
            P(None, "dp", None),
            P(None, "dp", None),
            P("row"),
            P("row"),
            P("row"),
            P("row"),
            P(("row", "dp"), None, "col"),
            P(None, ("col", "dp")),
            P(("col", "dp"), "row"),
            P(("row", "dp")),
            P("dp", "row", "col"),
            P("row", ("col", "dp")),
            P("dp", "col", "row"),
            P(None, ("row", "dp")),
        ),
        out_specs=(
            P(None, ("dp", "col"), "row"),
            P(None, ("dp", "col"), "row"),
            P("row"),
            P("row"),
            P("row"),
            P("row"),
            P(("row", "dp"), None, "col"),
            P(None, ("col", "dp")),
            P(("col", "dp"), "row"),
            P(("row", "dp")),
            P("dp", "row", "col"),
            P("row", ("col", "dp")),
            P("dp", "col", "row"),
            P(None, ("row", "dp")),
        ),
        check_vma=False,
    )
```
